32 devices in a mesh: seq: 4 (over x, core), dp: 8 (over z, y).
Axes of the slice: x: 2, y: 2, z: 4, core: 2. Of those that a mesh axis runs over, the one named last changes fastest.
Arguments:
- tokens: bfloat16 [2048, 8, 1024], P('seq', 'dp'), may hold values from -6 to 6
- cotangent: bfloat16 [2048, 8, 1024], P('seq', 'dp'), may hold values from -6 to 6
- norm_attn: bfloat16 [1024], P('dp'), may hold values from 0.25 to 1.75
- w_qkv: bfloat16 [1024, 4096], P('dp'), may hold values from -0.1875 to 0.1875
- w_ba: bfloat16 [1024, 16], P('dp'), may hold values from -0.1875 to 0.1875
- conv_w: bfloat16 [4, 4096], P(None, 'dp'), may hold values from -3 to 3
- a_log: float32 [8], replicated, may hold values from 0 to 2.77
- dt_bias: float32 [8], replicated, may hold values from -6.9 to -2.3
- w_outgate: bfloat16 [1024, 2048], P('dp'), may hold values from -0.1875 to 0.1875
- head_gain: bfloat16 [256], replicated, may hold values from 0.25 to 1.75
- w_out: bfloat16 [2048, 1024], P('dp'), may hold values from -0.1875 to 0.1875
- norm_ffn: bfloat16 [1024], P('dp'), may hold values from 0.25 to 1.75
- w_gate: bfloat16 [1024, 2816], P('dp'), may hold values from -0.1875 to 0.1875
- w_up: bfloat16 [1024, 2816], P('dp'), may hold values from -0.1875 to 0.1875
- w_down: bfloat16 [2816, 1024], P('dp'), may hold values from -0.15625 to 0.15625
Outputs:
- block_out: bfloat16 [2048, 8, 1024], P('seq', 'dp')
- grad_tokens: bfloat16 [2048, 8, 1024], P('seq', 'dp')
- grad_norm_attn: float32 [1024], P('dp')
- grad_w_qkv: float32 [1024, 4096], P('dp')
- grad_w_ba: float32 [1024, 16], P('dp')
- grad_conv_w: float32 [4, 4096], P(None, 'dp')
- grad_a_log: float32 [8], replicated
- grad_dt_bias: float32 [8], replicated
- grad_w_outgate: float32 [1024, 2048], P('dp')
- grad_head_gain: float32 [256], replicated
- grad_w_out: float32 [2048, 1024], P('dp')
- grad_norm_ffn: float32 [1024], P('dp')
- grad_w_gate: float32 [1024, 2816], P('dp')
- grad_w_up: float32 [1024, 2816], P('dp')
- grad_w_down: float32 [2816, 1024], P('dp')
The draws below stay inside these ranges and needn't reach their ends.
All inputs are finite; a program needn't handle non-finite values.
Results may differ from the reference program's by a relative error of at most 0.019.
Values may be sent and summed in bfloat16 or wider, within the bound.
No kernel may reach another device: no remote copies, remote signals or barrier semaphores. Data moves between devices by JAX's collectives and lax.ppermute only.
A program may use at most 320 MiB of HBM per device.

```python
import jax
import jax.numpy as jnp
from jax import lax

D = 1024
H = 8
DK = 128
DV = 256
FF = 2816
CONV = 4
GROUP = 64
LEN = 2048
BATCH = 8


def levels(own_key, dims, cuts, low, top_value):
    level, own = 1.0, jax.random.fold_in(own_key, 6)
    for axis_at, blocks in cuts:
        heights = jnp.exp(jax.random.uniform(jax.random.fold_in(own, axis_at), (blocks,), jnp.float32, low / len(cuts), top_value / len(cuts)))
        level = level * jnp.repeat(heights, dims[axis_at] // blocks).reshape([-1 if axis == axis_at else 1 for axis in range(len(dims))])
    return level


def bell_draw(stream_key, extent, width, reach, split=(), kind=jnp.bfloat16):
    values = width * jax.random.normal(stream_key, extent, jnp.float32)
    if split:
        values = values * levels(stream_key, extent, split, -0.22, 0.18)
    return jnp.clip(values, -reach, reach).astype(kind)


def setup_inputs(seed: int = 0) -> dict:
    splits = jax.random.split(jax.random.key(seed), 16)
    tokens = bell_draw(splits[0], (LEN, BATCH, D), 1.0, 6.0, ((0, 4), (1, 8)))
    cotangent = bell_draw(splits[1], (LEN, BATCH, D), 1.0, 6.0, ((0, 4), (1, 8)))
    norm_attn = jnp.clip(1.0 + 0.15 * jax.random.normal(splits[2], (D,), jnp.float32), 0.25, 1.75).astype(jnp.bfloat16)
    w_qkv = bell_draw(splits[3], (D, H * (2 * DK + DV)), D ** -0.5, 0.1875, ((0, 8),))
    w_ba = bell_draw(splits[4], (D, 2 * H), D ** -0.5, 0.1875, ((0, 8),))
    conv_w = bell_draw(splits[5], (CONV, H * (2 * DK + DV)), CONV ** -0.5, 3.0, ((1, 8),))
    a_log = jnp.clip(jax.random.uniform(splits[6], (H,), jnp.float32, 0.0, 2.77), 0.0, 2.77)
    dt_bias = jnp.clip(jax.random.uniform(splits[7], (H,), jnp.float32, -6.9, -2.3), -6.9, -2.3)
    w_outgate = bell_draw(splits[8], (D, H * DV), D ** -0.5, 0.1875, ((0, 8),))
    head_gain = jnp.clip(1.0 + 0.15 * jax.random.normal(splits[9], (DV,), jnp.float32), 0.25, 1.75).astype(jnp.bfloat16)
    w_out = bell_draw(splits[10], (H * DV, D), (H * DV // 2) ** -0.5, 0.1875, ((0, 8),))
    norm_ffn = jnp.clip(1.0 + 0.15 * jax.random.normal(splits[11], (D,), jnp.float32), 0.25, 1.75).astype(jnp.bfloat16)
    w_gate = bell_draw(splits[12], (D, FF), D ** -0.5, 0.1875, ((0, 8),))
    w_up = bell_draw(splits[13], (D, FF), D ** -0.5, 0.1875, ((0, 8),))
    w_down = bell_draw(splits[14], (FF, D), (FF // 2) ** -0.5, 0.15625, ((0, 8),))
    return {"tokens": tokens, "cotangent": cotangent, "norm_attn": norm_attn, "w_qkv": w_qkv, "w_ba": w_ba, "conv_w": conv_w, "a_log": a_log, "dt_bias": dt_bias, "w_outgate": w_outgate, "head_gain": head_gain, "w_out": w_out, "norm_ffn": norm_ffn, "w_gate": w_gate, "w_up": w_up, "w_down": w_down}


@jax.custom_vjp
def low(v):
    return lax.optimization_barrier(v.astype(jnp.bfloat16)).astype(jnp.float32)

@jax.custom_vjp
def low_back(v):
    return v

def low_keep(v):
    return (low(v), None)

def low_pass(kept, grad):
    return (grad,)

def back_keep(v):
    return (v, None)

def back_low(kept, grad):
    return (low(grad),)
low.defvjp(low_keep, low_pass)
low_back.defvjp(back_keep, back_low)
epsilon = 1e-06
highest = lax.Precision.HIGHEST

def product(left, right):
    return jnp.dot(left, right, precision=highest, preferred_element_type=jnp.float32)

def rms_norm(values, gain):
    return values * lax.rsqrt(lax.optimization_barrier(jnp.mean(values * values, axis=-1, keepdims=True)) + epsilon) * gain

def delta_mixer(projected, rates, conv_part, decay_log, decay_bias):
    length, head_count, row_width = projected.shape
    kernel = conv_part.reshape(CONV, head_count, row_width)
    padded = jnp.pad(projected, ((CONV - 1, 0), (0, 0), (0, 0)))
    summed = padded[0:length] * kernel[0]
    for offset in range(1, CONV):
        summed = summed + padded[offset:offset + length] * kernel[offset]
    active = jax.nn.silu(summed)
    queries = active[..., :DK]
    key_rows = active[..., DK:2 * DK]
    values = active[..., 2 * DK:]
    queries = queries * lax.rsqrt(lax.optimization_barrier(jnp.sum(queries * queries, axis=-1, keepdims=True)) + epsilon) * DK ** (-0.5)
    key_rows = key_rows * lax.rsqrt(lax.optimization_barrier(jnp.sum(key_rows * key_rows, axis=-1, keepdims=True)) + epsilon)
    strength = jax.nn.sigmoid(rates[..., 0])
    decay = -jnp.exp(decay_log) * jax.nn.softplus(rates[..., 1] + decay_bias)
    blocks = length // GROUP

    def to_blocks(array):
        return jnp.swapaxes(array.reshape(blocks, GROUP, head_count, -1), 1, 2)
    query_blocks = to_blocks(queries)
    key_blocks = to_blocks(key_rows)
    value_blocks = to_blocks(values)
    strength_blocks = to_blocks(strength[..., None])[..., 0]
    cumulative = jnp.cumsum(to_blocks(decay[..., None])[..., 0], axis=-1)
    final_decay = cumulative[..., -1:]
    positions = jnp.arange(GROUP)
    strictly = positions[:, None] > positions[None, :]
    through = positions[:, None] >= positions[None, :]
    spread = cumulative[..., :, None] - cumulative[..., None, :]
    strict_fade = jnp.where(strictly, jnp.exp(jnp.where(strictly, spread, 0.0)), 0.0)
    full_fade = jnp.where(through, jnp.exp(jnp.where(through, spread, 0.0)), 0.0)
    key_dots = jnp.einsum('bhck,bhek->bhce', key_blocks, key_blocks, precision=highest)
    negated = -(strength_blocks[..., None] * strict_fade * key_dots)
    identity = jnp.eye(GROUP, dtype=jnp.float32)
    inverse = identity + negated
    power = negated
    for section in range(1, (GROUP - 1).bit_length()):
        power = jnp.einsum('bhce,bhef->bhcf', power, power, precision=highest)
        inverse = inverse + jnp.einsum('bhce,bhef->bhcf', inverse, power, precision=highest)
    right_side = jnp.concatenate([strength_blocks[..., None] * value_blocks, (strength_blocks * jnp.exp(cumulative))[..., None] * key_blocks], axis=-1)
    solved = jnp.einsum('bhce,bhef->bhcf', inverse, right_side, precision=highest)
    updates = solved[..., :DV]
    key_weights = solved[..., DV:]
    key_faded = key_blocks * jnp.exp(final_decay - cumulative)[..., None]

    def advance(state, block):
        block_updates, block_weights, block_faded, block_final = block
        corrected = block_updates - jnp.einsum('hck,hvk->hcv', block_weights, state, precision=highest)
        following = state * jnp.exp(block_final)[:, :, None] + jnp.einsum('hcv,hck->hvk', corrected, block_faded, precision=highest)
        return (following, (corrected, state))
    start_state = jnp.zeros((head_count, DV, DK), jnp.float32)
    unused, (corrected_all, states) = lax.scan(advance, start_state, (updates, key_weights, key_faded, final_decay))
    query_dots = jnp.einsum('bhck,bhek->bhce', query_blocks, key_blocks, precision=highest) * full_fade
    result = jnp.einsum('bhck,bhvk->bhcv', query_blocks * jnp.exp(cumulative)[..., None], states, precision=highest)
    result = result + jnp.einsum('bhce,bhev->bhcv', query_dots, corrected_all, precision=highest)
    return jnp.swapaxes(result, 1, 2).reshape(length, head_count, DV)

def block_forward(rows, params):
    norm_attn, w_qkv, w_ba, conv_w, a_log, dt_bias, w_outgate, head_gain, w_out, norm_ffn, w_gate, w_up, w_down = params
    length = rows.shape[0]
    head_count = a_log.shape[0]
    normed_one = low(rms_norm(rows, norm_attn))
    projected = low_back(low(product(normed_one, w_qkv))).reshape(length, head_count, -1)
    rates = low_back(low(product(normed_one, w_ba))).reshape(length, head_count, 2)
    out_gate = low_back(product(normed_one, w_outgate)).reshape(length, head_count, DV)
    mixed = low_back(low(delta_mixer(projected, rates, conv_w, a_log, dt_bias)))
    gated = low((rms_norm(mixed, head_gain) * jax.nn.silu(out_gate)).reshape(length, -1))
    after_mix = rows + low_back(product(gated, w_out))
    normed_two = low(rms_norm(after_mix, norm_ffn))
    gate_pre = low_back(product(normed_two, w_gate))
    up_pre = low_back(product(normed_two, w_up))
    hidden = low(jax.nn.silu(gate_pre) * up_pre)
    return after_mix + product(hidden, w_down)

def reference(tokens, cotangent, norm_attn, w_qkv, w_ba, conv_w, a_log, dt_bias, w_outgate, head_gain, w_out, norm_ffn, w_gate, w_up, w_down):
    params = tuple((item.astype(jnp.float32) for item in (norm_attn, w_qkv, w_ba, conv_w, a_log, dt_bias, w_outgate, head_gain, w_out, norm_ffn, w_gate, w_up, w_down)))

    def per_sequence(totals, pair):
        seq_rows, seq_cot = pair
        result, back_fn = jax.vjp(block_forward, seq_rows, params)
        grad_rows, grad_params = back_fn(seq_cot)
        totals = jax.tree.map(lambda first, second: first + second, totals, grad_params)
        return (totals, (result.astype(jnp.bfloat16), grad_rows.astype(jnp.bfloat16)))
    inputs = (jnp.swapaxes(tokens, 0, 1).astype(jnp.float32), jnp.swapaxes(cotangent, 0, 1).astype(jnp.float32))
    start_totals = jax.tree.map(jnp.zeros_like, params)
    totals, (results, grads) = lax.scan(per_sequence, start_totals, inputs)
    return (jnp.swapaxes(results, 0, 1), jnp.swapaxes(grads, 0, 1), totals[0], totals[1], totals[2], totals[3], totals[4], totals[5], totals[6], totals[7], totals[8], totals[9], totals[10], totals[11], totals[12])
```

```python
import jax
import jax.numpy as jnp
from jax import lax
from jax.experimental import pallas as pl
from jax.experimental.pallas import tpu as pltpu
from jax.sharding import PartitionSpec as P

DK = 128
DV = 256
CONV = 4
ROW = 2 * DK + DV
LANES = 128
CHUNK = 256
HALO = 8

epsilon = 1e-06
narrow = jnp.bfloat16
wide = jnp.float32


def by_weight(left, right):
    return jnp.dot(left, right, preferred_element_type=wide)


def by_transpose(left, right):
    return lax.dot_general(
        left, right, (((1,), (1,)), ((), ())), preferred_element_type=wide
    )


def over_rows(left, right):
    return lax.dot_general(
        left, right, (((0,), (0,)), ((), ())), preferred_element_type=wide
    )


def row_norm(values, gain):
    inverse = lax.rsqrt(jnp.mean(values * values, axis=-1, keepdims=True) + epsilon)
    return (values * inverse * gain, inverse)


def norm_back(values, inverse, gain, grad_out):
    scaled = grad_out * gain
    grad_in = inverse * scaled - values * inverse * inverse * inverse * jnp.mean(
        scaled * values, axis=-1, keepdims=True
    )
    grad_gain = jnp.sum(grad_out * values * inverse, axis=tuple(range(values.ndim - 1)))
    return (grad_in, grad_gain)


def lower(array):
    return array.astype(narrow)


def row_sum(array):
    return jnp.sum(array, axis=1, keepdims=True)


def grid_indices():
    rows = lax.broadcasted_iota(jnp.int32, (CHUNK, CHUNK), 0)
    columns = lax.broadcasted_iota(jnp.int32, (CHUNK, CHUNK), 1)
    return rows, columns


def exact_dot(left, right):
    return jnp.dot(
        left, right, precision=lax.Precision.HIGHEST, preferred_element_type=wide
    )


def convolved(rows, before, taps):
    extended = jnp.concatenate([before, rows], axis=0)
    start = HALO - CONV + 1
    summed = extended[start : start + CHUNK] * taps[0:1]
    for offset in range(1, CONV):
        summed = summed + extended[start + offset : start + offset + CHUNK] * taps[
            offset : offset + 1
        ]
    return extended, summed


def gates(rates, coefficients, rows, columns):
    strength = jax.nn.sigmoid(rates)
    shifted = rates + coefficients[0:1]
    decay = coefficients[1:2] * jax.nn.softplus(shifted)
    through = jnp.where(rows >= columns, 1.0, 0.0)
    cumulative = exact_dot(through, decay)
    return strength, shifted, decay, cumulative


def unit(values):
    return lax.rsqrt(row_sum(values * values) + epsilon)


def invert(lower_part, rows, columns):
    apart = jnp.bitwise_xor(rows, columns)
    inverse = jnp.where(rows == columns, 1.0, 0.0) - jnp.where(apart == 1, lower_part, 0.0)
    level = 1
    while (1 << level) < CHUNK:
        corner = lower(
            jnp.where(lax.shift_right_logical(apart, level) == 1, lower_part, 0.0)
        )
        held = lower(inverse)
        inverse = inverse - by_weight(held, lower(by_weight(corner, held)))
        level += 1
    return inverse


def forward_kernel(
    heads,
    proj_ref,
    rates_ref,
    gate_ref,
    taps_ref,
    coef_ref,
    gain_ref,
    gated_ref,
    mixed_ref,
    inverse_ref,
    state_ref,
    corrected_ref,
    update_ref,
    weight_ref,
    before,
    state,
):
    @pl.when(pl.program_id(0) == 0)
    def _():
        before[...] = jnp.zeros_like(before)
        state[...] = jnp.zeros_like(state)

    rows, columns = grid_indices()
    raw = proj_ref[...].astype(wide)
    unused, summed = convolved(raw, before[...], taps_ref[...])
    before[...] = raw[CHUNK - HALO :]
    active = summed * jax.nn.sigmoid(summed)
    strength_all, unused, unused, cumulative_all = gates(
        rates_ref[...].astype(wide), coef_ref[...], rows, columns
    )
    turned = cumulative_all.T
    gain = gain_ref[0:1]
    for head in range(heads):
        base = head * ROW
        query = active[:, base : base + DK]
        key = active[:, base + DK : base + 2 * DK]
        value = active[:, base + 2 * DK : base + ROW]
        query = query * (unit(query) * DK ** (-0.5))
        key = key * unit(key)
        strength = strength_all[:, 2 * head : 2 * head + 1]
        cumulative = cumulative_all[:, 2 * head + 1 : 2 * head + 2]
        across = turned[2 * head + 1 : 2 * head + 2]
        final = cumulative_all[CHUNK - 1 :, 2 * head + 1 : 2 * head + 2]
        fade = jnp.where(
            rows >= columns, jnp.exp(jnp.minimum(cumulative - across, 0.0)), 0.0
        )
        grown = jnp.exp(cumulative)
        key_low = lower(key)
        query_low = lower(query)
        dots = by_transpose(key_low, key_low)
        lower_part = jnp.where(rows > columns, strength * fade * dots, 0.0)
        inverse = lower(invert(lower_part, rows, columns))
        update = by_weight(inverse, lower(strength * value))
        weight = lower(by_weight(inverse, lower(strength * grown * key)))
        held = state[head]
        held_low = lower(held)
        corrected = lower(update - by_transpose(weight, held_low))
        faded = lower(key * jnp.exp(final - cumulative))
        state[head] = held * jnp.exp(final) + over_rows(corrected, faded)
        inner = lower(by_transpose(query_low, key_low) * fade)
        result = grown * by_transpose(query_low, held_low) + by_weight(inner, corrected)
        mixed = lower(result)
        span = slice(head * DV, head * DV + DV)
        mixed_ref[:, span] = mixed
        mixed = mixed.astype(wide)
        normed, unused = row_norm(mixed, gain)
        gate = gate_ref[:, span]
        gated_ref[:, span] = lower(normed * (gate * jax.nn.sigmoid(gate)))
        inverse_ref[0, head] = inverse
        state_ref[0, head] = held_low
        corrected_ref[:, span] = corrected
        update_ref[:, span] = lower(update)
        weight_ref[:, head * DK : head * DK + DK] = weight


def backward_kernel(
    heads,
    proj_ref,
    edge_ref,
    rates_ref,
    gate_ref,
    taps_ref,
    coef_ref,
    gain_ref,
    mixed_ref,
    inverse_ref,
    state_ref,
    corrected_ref,
    update_ref,
    weight_ref,
    grad_ref,
    out_ref,
    taps_grad_ref,
    gain_grad_ref,
    small_grad_ref,
    after,
    state_grad,
):
    step = pl.program_id(0)

    @pl.when(step == 0)
    def _():
        after[...] = jnp.zeros_like(after)
        state_grad[...] = jnp.zeros_like(state_grad)
        taps_grad_ref[...] = jnp.zeros_like(taps_grad_ref)
        gain_grad_ref[...] = jnp.zeros_like(gain_grad_ref)
        small_grad_ref[...] = jnp.zeros_like(small_grad_ref)

    rows, columns = grid_indices()
    lanes = lax.broadcasted_iota(jnp.int32, (CHUNK, LANES), 1)
    raw = proj_ref[...].astype(wide)
    edge = edge_ref[edge_ref.shape[0] - HALO :].astype(wide)
    edge = jnp.where(step == pl.num_programs(0) - 1, 0.0, edge)
    taps = taps_ref[...]
    extended, summed = convolved(raw, edge, taps)
    sig = jax.nn.sigmoid(summed)
    active = summed * sig
    coefficients = coef_ref[...]
    strength_all, shifted, decay, cumulative_all = gates(
        rates_ref[...].astype(wide), coefficients, rows, columns
    )
    turned = cumulative_all.T
    gain = gain_ref[0:1]
    proj_width = heads * ROW
    active_grads = []
    spread_grad = jnp.zeros((CHUNK, LANES), wide)
    extra_grad = jnp.zeros((CHUNK, LANES), wide)
    strength_grad = jnp.zeros((CHUNK, LANES), wide)
    gain_grad = jnp.zeros((1, DV), wide)
    for head in range(heads):
        span = slice(head * DV, head * DV + DV)
        grad_gated = grad_ref[:, span].astype(wide)
        mixed = mixed_ref[:, span].astype(wide)
        normed, head_inverse = row_norm(mixed, gain)
        gate = gate_ref[:, span]
        sig_gate = jax.nn.sigmoid(gate)
        gate_start = proj_width + LANES + head * DV
        out_ref[:, gate_start : gate_start + DV] = lower(
            grad_gated * normed * sig_gate * (1.0 + gate * (1.0 - sig_gate))
        )
        normed_grad = grad_gated * (gate * sig_gate)
        scaled = normed_grad * gain
        grad_mixed = lower(
            head_inverse * scaled
            - mixed
            * (head_inverse * head_inverse * head_inverse)
            * jnp.mean(scaled * mixed, axis=-1, keepdims=True)
        )
        gain_grad = gain_grad + jnp.sum(
            normed_grad * mixed * head_inverse, axis=0, keepdims=True
        )
        base = head * ROW
        query_raw = active[:, base : base + DK]
        key_raw = active[:, base + DK : base + 2 * DK]
        value = active[:, base + 2 * DK : base + ROW]
        query_unit = unit(query_raw)
        key_unit = unit(key_raw)
        query = query_raw * (query_unit * DK ** (-0.5))
        key = key_raw * key_unit
        strength = strength_all[:, 2 * head : 2 * head + 1]
        cumulative = cumulative_all[:, 2 * head + 1 : 2 * head + 2]
        across = turned[2 * head + 1 : 2 * head + 2]
        final = cumulative_all[CHUNK - 1 :, 2 * head + 1 : 2 * head + 2]
        fade = jnp.where(
            rows >= columns, jnp.exp(jnp.minimum(cumulative - across, 0.0)), 0.0
        )
        strict_fade = jnp.where(rows > columns, fade, 0.0)
        grown = jnp.exp(cumulative)
        remaining = jnp.exp(final - cumulative)
        kept = jnp.exp(final)
        key_low = lower(key)
        query_low = lower(query)
        dots = by_transpose(key_low, key_low)
        inner = by_transpose(query_low, key_low) * fade
        inverse = inverse_ref[0, head]
        held = state_ref[0, head]
        corrected = corrected_ref[:, span]
        update = update_ref[:, span]
        weight = weight_ref[:, head * DK : head * DK + DK]
        faded = key * remaining
        grown_query = query * grown
        later = state_grad[head]
        later_low = lower(later)
        corrected_grad = over_rows(lower(inner), grad_mixed) + by_transpose(
            lower(faded), later_low
        )
        corrected_grad_low = lower(corrected_grad)
        state_grad[head] = (
            later * kept
            + over_rows(grad_mixed, lower(grown_query))
            - over_rows(corrected_grad_low, weight)
        )
        dot_grad = by_transpose(grad_mixed, corrected) * fade
        dot_grad_low = lower(dot_grad)
        grown_grad = by_weight(grad_mixed, held)
        faded_grad = by_weight(corrected, later_low)
        weight_grad = -by_weight(corrected_grad_low, held)
        value_side = over_rows(inverse, corrected_grad_low)
        key_side = over_rows(inverse, lower(weight_grad))
        lower_grad = -(
            by_transpose(lower(value_side), update) + by_transpose(lower(key_side), weight)
        ) * strict_fade
        inner_query = by_weight(dot_grad_low, key_low)
        inner_key = over_rows(dot_grad_low, query_low)
        lower_grad_low = lower(lower_grad)
        first_key = by_weight(lower_grad_low, key_low)
        second_key = over_rows(lower_grad_low, lower(strength * key))
        pairs = lower_grad * dots
        both = pairs * strength + dot_grad * by_transpose(query_low, key_low)
        faded_sum = row_sum(faded_grad * faded)
        key_sum = row_sum(key_side * key)
        query_grad = grown * grown_grad + inner_query
        key_grad = (
            (strength * grown) * key_side
            + strength * first_key
            + second_key
            + inner_key
            + remaining * faded_grad
        )
        value_grad = strength * value_side
        head_strength_grad = row_sum(value_side * value) + grown * key_sum + row_sum(pairs)
        head_spread = (
            (strength * grown) * key_sum
            + row_sum(both)
            + row_sum(grown_grad * grown_query)
            - faded_sum
        )
        column_total = jnp.sum(both, axis=0, keepdims=True)
        late_total = row_sum(jnp.where(columns >= rows, column_total, 0.0))
        final_grad = kept * jnp.sum(held.astype(wide) * later, keepdims=True) + jnp.sum(
            faded_sum, axis=0, keepdims=True
        )
        spread_grad = jnp.where(lanes == 2 * head + 1, head_spread, spread_grad)
        extra_grad = jnp.where(lanes == 2 * head + 1, final_grad - late_total, extra_grad)
        strength_grad = jnp.where(lanes == 2 * head, head_strength_grad, strength_grad)
        active_grads.append(
            DK ** (-0.5)
            * query_unit
            * (
                query_grad
                - query_raw * (query_unit * query_unit) * row_sum(query_grad * query_raw)
            )
        )
        active_grads.append(
            key_unit
            * (key_grad - key_raw * (key_unit * key_unit) * row_sum(key_grad * key_raw))
        )
        active_grads.append(value_grad)
    onward = jnp.where(columns >= rows, 1.0, 0.0)
    decay_grad = exact_dot(onward, spread_grad) + extra_grad
    shift_grad = decay_grad * coefficients[1:2] * jax.nn.sigmoid(shifted)
    rates_grad = strength_grad * strength_all * (1.0 - strength_all) + shift_grad
    out_ref[:, proj_width : proj_width + LANES] = lower(rates_grad)
    small_grad_ref[0:1] += jnp.sum(shift_grad, axis=0, keepdims=True)
    small_grad_ref[1:2] += jnp.sum(decay_grad * decay, axis=0, keepdims=True)
    gain_grad_ref[0:1] += gain_grad
    summed_grad = jnp.concatenate(active_grads, axis=1) * (
        sig * (1.0 + summed * (1.0 - sig))
    )
    following = jnp.concatenate([summed_grad, after[...]], axis=0)
    after[...] = summed_grad[:HALO]
    proj_grad = following[CONV - 1 : CONV - 1 + CHUNK] * taps[0:1]
    start = HALO - CONV + 1
    for offset in range(CONV):
        if offset:
            shift = CONV - 1 - offset
            proj_grad = proj_grad + following[shift : shift + CHUNK] * taps[offset : offset + 1]
        taps_grad_ref[offset : offset + 1] += jnp.sum(
            summed_grad * extended[start + offset : start + offset + CHUNK],
            axis=0,
            keepdims=True,
        )
    out_ref[:, :proj_width] = lower(proj_grad)


def params():
    return pltpu.CompilerParams(
        dimension_semantics=("arbitrary",), vmem_limit_bytes=48 * 1024 * 1024
    )


def mixer_forward(heads, proj, gate, taps, coefficients, gain, interpret=False):
    length = proj.shape[0]
    steps = length // CHUNK
    width = heads * ROW
    values = heads * DV

    def tall(columns, place=0):
        return pl.BlockSpec((CHUNK, columns), lambda i: (i, place))

    def whole(array):
        return pl.BlockSpec(array.shape, lambda i: (0,) * array.ndim)

    def stacked(first, second):
        return pl.BlockSpec((1, heads, first, second), lambda i: (i, 0, 0, 0))

    return pl.pallas_call(
        lambda *refs: forward_kernel(heads, *refs),
        grid=(steps,),
        in_specs=[
            tall(width),
            tall(LANES, width // LANES),
            tall(values),
            whole(taps),
            whole(coefficients),
            whole(gain),
        ],
        out_specs=[
            tall(values),
            tall(values),
            stacked(CHUNK, CHUNK),
            stacked(DV, DK),
            tall(values),
            tall(values),
            tall(heads * DK),
        ],
        out_shape=[
            jax.ShapeDtypeStruct((length, values), narrow),
            jax.ShapeDtypeStruct((length, values), narrow),
            jax.ShapeDtypeStruct((steps, heads, CHUNK, CHUNK), narrow),
            jax.ShapeDtypeStruct((steps, heads, DV, DK), narrow),
            jax.ShapeDtypeStruct((length, values), narrow),
            jax.ShapeDtypeStruct((length, values), narrow),
            jax.ShapeDtypeStruct((length, heads * DK), narrow),
        ],
        scratch_shapes=[
            pltpu.VMEM((HALO, width), wide),
            pltpu.VMEM((heads, DV, DK), wide),
        ],
        compiler_params=params(),
        interpret=interpret,
    )(proj, proj, gate, taps, coefficients, gain)


def mixer_backward(
    heads, proj, gate, taps, coefficients, gain, kept, grad_gated, interpret=False
):
    length = proj.shape[0]
    steps = length // CHUNK
    width = heads * ROW
    values = heads * DV
    edge_rows = 2 * HALO
    ratio = CHUNK // edge_rows

    def tall(columns, place=0):
        return pl.BlockSpec((CHUNK, columns), lambda i: (steps - 1 - i, place))

    def whole(shape):
        return pl.BlockSpec(shape, lambda i: (0,) * len(shape))

    def stacked(first, second):
        return pl.BlockSpec((1, heads, first, second), lambda i: (steps - 1 - i, 0, 0, 0))

    total = width + LANES + values
    return pl.pallas_call(
        lambda *refs: backward_kernel(heads, *refs),
        grid=(steps,),
        in_specs=[
            tall(width),
            pl.BlockSpec(
                (edge_rows, width),
                lambda i: (jnp.maximum((steps - 1 - i) * ratio - 1, 0), 0),
            ),
            tall(LANES, width // LANES),
            tall(values),
            whole(taps.shape),
            whole(coefficients.shape),
            whole(gain.shape),
            tall(values),
            stacked(CHUNK, CHUNK),
            stacked(DV, DK),
            tall(values),
            tall(values),
            tall(heads * DK),
            tall(values),
        ],
        out_specs=[
            tall(total),
            whole((HALO, width)),
            whole((HALO, DV)),
            whole((HALO, LANES)),
        ],
        out_shape=[
            jax.ShapeDtypeStruct((length, total), narrow),
            jax.ShapeDtypeStruct((HALO, width), wide),
            jax.ShapeDtypeStruct((HALO, DV), wide),
            jax.ShapeDtypeStruct((HALO, LANES), wide),
        ],
        scratch_shapes=[
            pltpu.VMEM((HALO, width), wide),
            pltpu.VMEM((heads, DV, DK), wide),
        ],
        compiler_params=params(),
        interpret=interpret,
    )(proj, proj, proj, gate, taps, coefficients, gain, *kept, grad_gated)


def per_device(
    tokens,
    cotangent,
    norm_attn,
    w_qkv,
    w_ba,
    conv_w,
    a_log,
    dt_bias,
    w_outgate,
    head_gain,
    w_out,
    norm_ffn,
    w_gate,
    w_up,
    w_down,
    interpret=False,
):
    parts = lax.axis_size("seq")
    shards = lax.axis_size("dp")
    place = lax.axis_index("seq")
    shard = lax.axis_index("dp")
    head_count = a_log.shape[0]
    heads = head_count // parts
    width = heads * ROW
    values = heads * DV
    model = tokens.shape[2]
    count = tokens.shape[0]
    own = norm_attn.shape[0]

    def mine(array, size, axis):
        return lax.dynamic_slice_in_dim(array, place * size, size, axis)

    def over_dp(array):
        return lax.all_gather(array, "dp", axis=0, tiled=True)

    def over_seq(array):
        return lax.all_gather(array, "seq", axis=0, tiled=True)

    def sum_seq(array):
        return lax.psum_scatter(
            array.astype(narrow), "seq", scatter_dimension=0, tiled=True
        )

    def sum_dp(array):
        return lax.psum_scatter(array.astype(narrow), "dp", scatter_dimension=0, tiled=True)

    ffn = w_gate.shape[1]
    piece = ffn // (shards * parts)

    def ffn_columns(array):
        split = array.reshape(own, shards, parts, piece)
        return lax.dynamic_index_in_dim(split, place, 2, keepdims=False).reshape(own, -1)

    own_tokens = tokens[:, 0, :]
    own_cot = cotangent[:, 0, :]
    all_tokens = over_seq(own_tokens)
    small_flat = jnp.concatenate([norm_attn, norm_ffn, conv_w.reshape(-1)])
    small_all = over_dp(small_flat[None, :])
    first_gain = small_all[:, :own].reshape(-1).astype(wide)
    second_gain = small_all[:, own : 2 * own].reshape(-1).astype(wide)
    taps_all = jnp.swapaxes(small_all[:, 2 * own :].reshape(shards, CONV, -1), 0, 1)
    taps = mine(taps_all.reshape(CONV, -1), width, 1).astype(wide)
    taps = jnp.pad(taps, ((0, HALO - CONV), (0, 0)))
    w_in = over_dp(
        jnp.concatenate(
            [
                mine(w_qkv, width, 1),
                jnp.pad(mine(w_ba, 2 * heads, 1), ((0, 0), (0, LANES - 2 * heads))),
                mine(w_outgate, values, 1),
            ],
            axis=1,
        )
    )
    out_part = over_dp(mine(w_out, model // parts, 1))
    w_out_own = lax.all_to_all(out_part, "seq", split_axis=0, concat_axis=1, tiled=True)
    gate_own = over_dp(ffn_columns(w_gate))
    up_own = over_dp(ffn_columns(w_up))
    down_own = over_dp(mine(w_down, w_down.shape[0] // parts, 0))
    all_cot = over_seq(own_cot)

    decay_part = mine(a_log, heads, 0)
    bias_part = mine(dt_bias, heads, 0)

    def odd_lanes(vector):
        spaced = jnp.stack([jnp.zeros_like(vector), vector], axis=1).reshape(-1)
        return jnp.pad(spaced, (0, LANES - 2 * heads))[None, :]

    coefficients = jnp.pad(
        jnp.concatenate([odd_lanes(bias_part), odd_lanes(-jnp.exp(decay_part))], axis=0),
        ((0, HALO - 2), (0, 0)),
    )
    gain = jnp.broadcast_to(head_gain.astype(wide)[None, :], (HALO, DV))

    rows = own_tokens.astype(wide)
    inverse_one = row_norm(rows, first_gain)[1]
    normed_one = row_norm(all_tokens.astype(wide), first_gain)[0].astype(narrow)
    w_in_first = w_in[:, : width + LANES]
    w_in_gate = w_in[:, width + LANES :]
    proj = by_weight(normed_one, w_in_first).astype(narrow)
    out_gate = by_weight(normed_one, w_in_gate)
    gated, *kept = mixer_forward(
        heads, proj, out_gate, taps, coefficients, gain, interpret
    )
    after_mix = rows + sum_seq(by_weight(gated, w_out_own)).astype(wide)
    normed_two, inverse_two = row_norm(after_mix, second_gain)
    normed_two = over_seq(normed_two.astype(narrow))
    gate_pre = by_weight(normed_two, gate_own)
    up_pre = by_weight(normed_two, up_own)
    sig_ffn = jax.nn.sigmoid(gate_pre)
    hidden = (gate_pre * sig_ffn * up_pre).astype(narrow)
    grad_hidden = by_transpose(all_cot, down_own)
    grad_gate_pre = (grad_hidden * up_pre * sig_ffn * (1.0 + gate_pre * (1.0 - sig_ffn))).astype(
        narrow
    )
    grad_up_pre = (grad_hidden * gate_pre * sig_ffn).astype(narrow)
    grad_normed_two = sum_seq(
        by_transpose(grad_gate_pre, gate_own) + by_transpose(grad_up_pre, up_own)
    )
    back_two, grad_norm_ffn = norm_back(
        after_mix, inverse_two, second_gain, grad_normed_two.astype(wide)
    )
    grad_after = own_cot.astype(wide) + back_two
    grad_branch = over_seq(grad_after.astype(narrow))
    grad_gated = by_transpose(grad_branch, w_out_own)
    result = after_mix + sum_seq(by_weight(hidden, down_own)).astype(wide)
    grad_gate = sum_dp(over_rows(normed_two, grad_gate_pre))
    grad_up = sum_dp(over_rows(normed_two, grad_up_pre))
    grad_down = sum_dp(over_rows(hidden, all_cot))
    grad_out = sum_dp(
        lax.all_to_all(
            over_rows(gated, grad_branch).astype(narrow),
            "seq",
            split_axis=1,
            concat_axis=0,
            tiled=True,
        )
    )
    grad_in, grad_taps, grad_gain, grad_small = mixer_backward(
        heads, proj, out_gate, taps, coefficients, gain, kept, grad_gated, interpret
    )
    grad_normed_one = sum_seq(by_transpose(grad_in, w_in))
    grad_w_in = sum_dp(over_rows(normed_one, grad_in))
    back_one, grad_norm_attn = norm_back(
        rows, inverse_one, first_gain, grad_normed_one.astype(wide)
    )
    grad_rows = (grad_after + back_one).astype(narrow)[:, None, :]

    taps_full = lax.dynamic_update_slice_in_dim(
        jnp.zeros((CONV, head_count * ROW), wide), grad_taps[:CONV], place * width, 1
    )

    def to_heads(lane_row):
        return lax.dynamic_update_slice_in_dim(
            jnp.zeros((head_count,), wide), lane_row[1 : 2 * heads : 2], place * heads, 0
        )

    packed = lax.psum(
        jnp.concatenate(
            [
                grad_norm_attn,
                grad_norm_ffn,
                taps_full.reshape(-1),
                grad_gain[0],
                to_heads(grad_small[1]),
                to_heads(grad_small[0]),
            ]
        ),
        ("dp", "seq"),
    )
    taps_at = 2 * model
    gain_at = taps_at + CONV * head_count * ROW
    heads_at = gain_at + DV
    norm_attn_total = lax.dynamic_slice_in_dim(packed[:model], shard * own, own, 0)
    norm_ffn_total = lax.dynamic_slice_in_dim(packed[model:taps_at], shard * own, own, 0)
    own_taps = conv_w.shape[1]
    taps_total = lax.dynamic_slice_in_dim(
        packed[taps_at:gain_at].reshape(CONV, -1), shard * own_taps, own_taps, 1
    )

    def stack_seq(array):
        return lax.all_gather(array, "seq", axis=0)

    in_all = stack_seq(grad_w_in)

    def columns_of(array):
        return jnp.swapaxes(array, 0, 1).reshape(own, -1).astype(wide)

    def ffn_full(array):
        stacked = stack_seq(array).reshape(parts, own, shards, piece)
        return jnp.transpose(stacked, (1, 2, 0, 3)).reshape(own, -1).astype(wide)

    return (
        result.astype(narrow)[:, None, :],
        grad_rows,
        norm_attn_total,
        columns_of(in_all[:, :, :width]),
        columns_of(in_all[:, :, width : width + 2 * heads]),
        taps_total,
        packed[heads_at : heads_at + head_count],
        packed[heads_at + head_count : heads_at + 2 * head_count],
        columns_of(in_all[:, :, width + LANES :]),
        packed[gain_at:heads_at],
        lax.all_gather(grad_out, "seq", axis=1, tiled=True).astype(wide),
        norm_ffn_total,
        ffn_full(grad_gate),
        ffn_full(grad_up),
        lax.all_gather(grad_down, "seq", axis=0, tiled=True).astype(wide),
    )


def solution(mesh):
    return jax.shard_map(
        per_device,
        mesh=mesh,
        in_specs=(
            P("seq", "dp", None),
            P("seq", "dp", None),
            P("dp"),
            P("dp", None),
            P("dp", None),
            P(None, "dp"),
            P(),
            P(),
            P("dp", None),
            P(),
            P("dp", None),
            P("dp"),
            P("dp", None),
            P("dp", None),
            P("dp", None),
        ),
        out_specs=(
            P("seq", "dp", None),
            P("seq", "dp", None),
            P("dp"),
            P("dp", None),
            P("dp", None),
            P(None, "dp"),
            P(),
            P(),
            P("dp", None),
            P(),
            P("dp", None),
            P("dp"),
            P("dp", None),
            P("dp", None),
            P("dp", None),
        ),
        check_vma=False,
    )
```

```python
import jax
import jax.numpy as jnp
from jax import lax
from jax.experimental import pallas as pl
from jax.experimental.pallas import tpu as pltpu
from jax.sharding import PartitionSpec as P

DK = 128
DV = 256
CONV = 4
ROW = 2 * DK + DV
LANES = 128
CHUNK = 256
HALO = 8

epsilon = 1e-06
narrow = jnp.bfloat16
wide = jnp.float32


def by_weight(left, right):
    return jnp.dot(left, right, preferred_element_type=wide)


def by_transpose(left, right):
    return lax.dot_general(
        left, right, (((1,), (1,)), ((), ())), preferred_element_type=wide
    )


def over_rows(left, right):
    return lax.dot_general(
        left, right, (((0,), (0,)), ((), ())), preferred_element_type=wide
    )


def row_norm(values, gain):
    inverse = lax.rsqrt(jnp.mean(values * values, axis=-1, keepdims=True) + epsilon)
    return (values * inverse * gain, inverse)


def norm_back(values, inverse, gain, grad_out):
    scaled = grad_out * gain
    grad_in = inverse * scaled - values * inverse * inverse * inverse * jnp.mean(
        scaled * values, axis=-1, keepdims=True
    )
    grad_gain = jnp.sum(grad_out * values * inverse, axis=tuple(range(values.ndim - 1)))
    return (grad_in, grad_gain)


def lower(array):
    return array.astype(narrow)


def row_sum(array):
    return jnp.sum(array, axis=1, keepdims=True)


def grid_indices():
    rows = lax.broadcasted_iota(jnp.int32, (CHUNK, CHUNK), 0)
    columns = lax.broadcasted_iota(jnp.int32, (CHUNK, CHUNK), 1)
    return rows, columns


def exact_dot(left, right):
    return jnp.dot(
        left, right, precision=lax.Precision.HIGHEST, preferred_element_type=wide
    )


def shifted_rows(rows, before):
    return jnp.concatenate([before, rows], axis=0)


def convolved(extended, taps, count):
    start = HALO - CONV + 1
    summed = extended[start : start + count] * taps[0:1]
    for offset in range(1, CONV):
        summed = summed + extended[start + offset : start + offset + count] * taps[
            offset : offset + 1
        ]
    return summed


def gates(rates, coefficients):
    strength = jax.nn.sigmoid(rates)
    shifted = rates + coefficients[0:1]
    decay = coefficients[1:2] * jax.nn.softplus(shifted)
    return strength, shifted, decay


def unit(values):
    return lax.rsqrt(row_sum(values * values) + epsilon)


def in_turn(parts):
    waiting = list(parts)
    while waiting:
        still = []
        for part in waiting:
            try:
                next(part)
                still.append(part)
            except StopIteration:
                pass
        waiting = still


def invert(lower_part, rows, columns, store):
    apart = jnp.bitwise_xor(rows, columns)
    inverse = jnp.where(rows == columns, 1.0, 0.0) - jnp.where(apart == 1, lower_part, 0.0)
    level = 1
    while (1 << level) < CHUNK:
        corner = lower(
            jnp.where(lax.shift_right_logical(apart, level) == 1, lower_part, 0.0)
        )
        held = lower(inverse)
        yield
        side = lower(by_weight(corner, held))
        yield
        inverse = inverse - by_weight(held, side)
        level += 1
    store.append(lower(inverse))


def forward_kernel(
    heads,
    place_ref,
    proj_ref,
    rates_ref,
    gate_ref,
    taps_ref,
    coef_ref,
    gain_ref,
    gated_ref,
    mixed_ref,
    inverse_ref,
    state_ref,
    corrected_ref,
    update_ref,
    weight_ref,
    before,
    state,
):
    @pl.when(pl.program_id(0) == 0)
    def _():
        before[...] = jnp.zeros_like(before)
        state[...] = jnp.zeros_like(state)

    count = proj_ref.shape[0]
    rows, columns = grid_indices()
    raw = proj_ref[...].astype(wide)
    summed = convolved(shifted_rows(raw, before[...]), taps_ref[...], count)
    before[...] = raw[count - HALO :]
    active = summed * jax.nn.sigmoid(summed)
    strength_rows, unused, decay_rows = gates(rates_ref[...].astype(wide), coef_ref[...])
    through = jnp.where(rows >= columns, 1.0, 0.0)
    gain = gain_ref[0:1]
    states = {(0, head): state[head] for head in range(heads)}
    blocks = count // CHUNK
    cumulative_rows = [
        exact_dot(through, decay_rows[block * CHUNK : (block + 1) * CHUNK])
        for block in range(blocks)
    ]
    turned_rows = [item.T for item in cumulative_rows]

    def one(block, head):
        base = head * ROW
        here = slice(block * CHUNK, (block + 1) * CHUNK)
        query = active[here, base : base + DK]
        key = active[here, base + DK : base + 2 * DK]
        value = active[here, base + 2 * DK : base + ROW]
        query = query * (unit(query) * DK ** (-0.5))
        key = key * unit(key)
        strength = strength_rows[here, 2 * head : 2 * head + 1]
        cumulative = cumulative_rows[block][:, 2 * head + 1 : 2 * head + 2]
        across = turned_rows[block][2 * head + 1 : 2 * head + 2]
        final = cumulative[CHUNK - 1 :]
        fade = jnp.where(
            rows >= columns, jnp.exp(jnp.minimum(cumulative - across, 0.0)), 0.0
        )
        grown = jnp.exp(cumulative)
        key_low = lower(key)
        query_low = lower(query)
        dots = by_transpose(key_low, key_low)
        yield
        lower_part = jnp.where(rows > columns, strength * fade * dots, 0.0)
        store = []
        yield from invert(lower_part, rows, columns, store)
        inverse = store[0]
        yield
        update = by_weight(inverse, lower(strength * value))
        weight = lower(by_weight(inverse, lower(strength * grown * key)))
        inner = lower(by_transpose(query_low, key_low) * fade)
        faded = lower(key * jnp.exp(final - cumulative))
        inverse_ref[block, head] = inverse
        span = slice(head * DV, head * DV + DV)
        update_ref[here, span] = lower(update)
        weight_ref[here, head * DK : head * DK + DK] = weight
        yield
        while (block, head) not in states:
            yield
        held = states[block, head]
        held_low = lower(held)
        state_ref[block, head] = held_low
        corrected = lower(update - by_transpose(weight, held_low))
        yield
        states[block + 1, head] = held * jnp.exp(final) + over_rows(corrected, faded)
        corrected_ref[here, span] = corrected
        result = grown * by_transpose(query_low, held_low) + by_weight(inner, corrected)
        yield
        mixed = lower(result)
        mixed_ref[here, span] = mixed
        normed, unused = row_norm(mixed.astype(wide), gain)
        gate = gate_ref[here, span]
        gated_ref[here, span] = lower(normed * (gate * jax.nn.sigmoid(gate)))

    in_turn(one(block, head) for block in range(blocks) for head in range(heads))
    for head in range(heads):
        state[head] = states[blocks, head]


def backward_kernel(
    heads,
    place_ref,
    proj_ref,
    edge_ref,
    rates_ref,
    gate_ref,
    taps_ref,
    coef_ref,
    gain_ref,
    mixed_ref,
    inverse_ref,
    state_ref,
    corrected_ref,
    update_ref,
    weight_ref,
    grad_ref,
    out_ref,
    taps_grad_ref,
    gain_grad_ref,
    small_grad_ref,
    after,
    state_grad,
):
    step = pl.program_id(0)

    @pl.when(step == 0)
    def _():
        after[...] = jnp.zeros_like(after)
        state_grad[...] = jnp.zeros_like(state_grad)
        taps_grad_ref[...] = jnp.zeros_like(taps_grad_ref)
        gain_grad_ref[...] = jnp.zeros_like(gain_grad_ref)
        small_grad_ref[...] = jnp.zeros_like(small_grad_ref)

    count = proj_ref.shape[0]
    blocks = count // CHUNK
    rows, columns = grid_indices()
    lanes = lax.broadcasted_iota(jnp.int32, (CHUNK, LANES), 1)
    raw = proj_ref[...].astype(wide)
    edge = edge_ref[edge_ref.shape[0] - HALO :].astype(wide)
    edge = jnp.where(step == pl.num_programs(0) - 1, 0.0, edge)
    taps = taps_ref[...]
    extended = shifted_rows(raw, edge)
    summed = convolved(extended, taps, count)
    sig = jax.nn.sigmoid(summed)
    active = summed * sig
    coefficients = coef_ref[...]
    strength_rows, shifted_rates, decay_rows = gates(
        rates_ref[...].astype(wide), coefficients
    )
    through = jnp.where(rows >= columns, 1.0, 0.0)
    onward = jnp.where(columns >= rows, 1.0, 0.0)
    gain = gain_ref[0:1]
    proj_width = heads * ROW
    cumulative_rows = [
        exact_dot(through, decay_rows[block * CHUNK : (block + 1) * CHUNK])
        for block in range(blocks)
    ]
    turned_rows = [item.T for item in cumulative_rows]
    laters = {(blocks - 1, head): state_grad[head] for head in range(heads)}
    active_grads = {}
    column_grads = {}
    gain_grads = []

    def one(block, head):
        here = slice(block * CHUNK, (block + 1) * CHUNK)
        span = slice(head * DV, head * DV + DV)
        grad_gated = grad_ref[here, span].astype(wide)
        mixed = mixed_ref[here, span].astype(wide)
        normed, head_inverse = row_norm(mixed, gain)
        gate = gate_ref[here, span]
        sig_gate = jax.nn.sigmoid(gate)
        gate_start = proj_width + LANES + head * DV
        out_ref[here, gate_start : gate_start + DV] = lower(
            grad_gated * normed * sig_gate * (1.0 + gate * (1.0 - sig_gate))
        )
        normed_grad = grad_gated * (gate * sig_gate)
        scaled = normed_grad * gain
        grad_mixed = lower(
            head_inverse * scaled
            - mixed
            * (head_inverse * head_inverse * head_inverse)
            * jnp.mean(scaled * mixed, axis=-1, keepdims=True)
        )
        gain_grads.append(
            jnp.sum(normed_grad * mixed * head_inverse, axis=0, keepdims=True)
        )
        base = head * ROW
        query_raw = active[here, base : base + DK]
        key_raw = active[here, base + DK : base + 2 * DK]
        value = active[here, base + 2 * DK : base + ROW]
        query_unit = unit(query_raw)
        key_unit = unit(key_raw)
        query = query_raw * (query_unit * DK ** (-0.5))
        key = key_raw * key_unit
        strength = strength_rows[here, 2 * head : 2 * head + 1]
        cumulative = cumulative_rows[block][:, 2 * head + 1 : 2 * head + 2]
        across = turned_rows[block][2 * head + 1 : 2 * head + 2]
        final = cumulative[CHUNK - 1 :]
        fade = jnp.where(
            rows >= columns, jnp.exp(jnp.minimum(cumulative - across, 0.0)), 0.0
        )
        strict_fade = jnp.where(rows > columns, fade, 0.0)
        grown = jnp.exp(cumulative)
        remaining = jnp.exp(final - cumulative)
        kept = jnp.exp(final)
        key_low = lower(key)
        query_low = lower(query)
        yield
        dots = by_transpose(key_low, key_low)
        cross = by_transpose(query_low, key_low)
        held = state_ref[block, head]
        corrected = corrected_ref[here, span]
        weight = weight_ref[here, head * DK : head * DK + DK]
        faded = key * remaining
        faded_low = lower(faded)
        grown_query = query * grown
        yield
        inner_side = over_rows(lower(cross * fade), grad_mixed)
        state_side = over_rows(grad_mixed, lower(grown_query))
        dot_grad = by_transpose(grad_mixed, corrected) * fade
        dot_grad_low = lower(dot_grad)
        grown_grad = by_weight(grad_mixed, held)
        yield
        while (block, head) not in laters:
            yield
        later = laters[block, head]
        later_low = lower(later)
        corrected_grad_low = lower(inner_side + by_transpose(faded_low, later_low))
        yield
        laters[block - 1, head] = (
            later * kept + state_side - over_rows(corrected_grad_low, weight)
        )
        faded_grad = by_weight(corrected, later_low)
        weight_grad = lower(-by_weight(corrected_grad_low, held))
        inverse = inverse_ref[block, head]
        yield
        value_side = over_rows(inverse, corrected_grad_low)
        key_side = over_rows(inverse, weight_grad)
        yield
        lower_grad = -(
            by_transpose(lower(value_side), update_ref[here, span])
            + by_transpose(lower(key_side), weight)
        ) * strict_fade
        inner_query = by_weight(dot_grad_low, key_low)
        inner_key = over_rows(dot_grad_low, query_low)
        yield
        lower_grad_low = lower(lower_grad)
        first_key = by_weight(lower_grad_low, key_low)
        second_key = over_rows(lower_grad_low, lower(strength * key))
        pairs = lower_grad * dots
        both = pairs * strength + dot_grad * cross
        faded_sum = row_sum(faded_grad * faded)
        key_sum = row_sum(key_side * key)
        yield
        query_grad = grown * grown_grad + inner_query
        key_grad = (
            (strength * grown) * key_side
            + strength * first_key
            + second_key
            + inner_key
            + remaining * faded_grad
        )
        head_strength_grad = row_sum(value_side * value) + grown * key_sum + row_sum(pairs)
        head_spread = (
            (strength * grown) * key_sum
            + row_sum(both)
            + row_sum(grown_grad * grown_query)
            - faded_sum
        )
        column_total = jnp.sum(both, axis=0, keepdims=True)
        late_total = row_sum(jnp.where(columns >= rows, column_total, 0.0))
        final_grad = kept * jnp.sum(held.astype(wide) * later, keepdims=True) + jnp.sum(
            faded_sum, axis=0, keepdims=True
        )
        column_grads[block, head] = (
            head_strength_grad,
            head_spread,
            final_grad - late_total,
        )
        active_grads[block, head] = (
            DK ** (-0.5)
            * query_unit
            * (
                query_grad
                - query_raw * (query_unit * query_unit) * row_sum(query_grad * query_raw)
            ),
            key_unit
            * (key_grad - key_raw * (key_unit * key_unit) * row_sum(key_grad * key_raw)),
            strength * value_side,
        )

    in_turn(
        one(block, head) for block in reversed(range(blocks)) for head in range(heads)
    )
    for head in range(heads):
        state_grad[head] = laters[-1, head]
    for block in range(blocks):
        here = slice(block * CHUNK, (block + 1) * CHUNK)
        strength_grad = jnp.zeros((CHUNK, LANES), wide)
        spread_grad = jnp.zeros((CHUNK, LANES), wide)
        extra_grad = jnp.zeros((CHUNK, LANES), wide)
        for head in range(heads):
            first, second, third = column_grads[block, head]
            strength_grad = jnp.where(lanes == 2 * head, first, strength_grad)
            spread_grad = jnp.where(lanes == 2 * head + 1, second, spread_grad)
            extra_grad = jnp.where(lanes == 2 * head + 1, third, extra_grad)
        decay_grad = exact_dot(onward, spread_grad) + extra_grad
        shift_grad = decay_grad * coefficients[1:2] * jax.nn.sigmoid(shifted_rates[here])
        strength_here = strength_rows[here]
        rates_grad = strength_grad * strength_here * (1.0 - strength_here) + shift_grad
        out_ref[here, proj_width : proj_width + LANES] = lower(rates_grad)
        small_grad_ref[0:1] += jnp.sum(shift_grad, axis=0, keepdims=True)
        small_grad_ref[1:2] += jnp.sum(decay_grad * decay_rows[here], axis=0, keepdims=True)
    gain_grad_ref[0:1] += sum(gain_grads)
    joined = jnp.concatenate(
        [
            jnp.concatenate(
                [part for head in range(heads) for part in active_grads[block, head]], axis=1
            )
            for block in range(blocks)
        ],
        axis=0,
    )
    summed_grad = joined * (sig * (1.0 + summed * (1.0 - sig)))
    following = jnp.concatenate([summed_grad, after[...]], axis=0)
    after[...] = summed_grad[:HALO]
    proj_grad = following[CONV - 1 : CONV - 1 + count] * taps[0:1]
    start = HALO - CONV + 1
    for offset in range(CONV):
        if offset:
            shift = CONV - 1 - offset
            proj_grad = proj_grad + following[shift : shift + count] * taps[offset : offset + 1]
        taps_grad_ref[offset : offset + 1] += jnp.sum(
            summed_grad * extended[start + offset : start + offset + count],
            axis=0,
            keepdims=True,
        )
    out_ref[:, :proj_width] = lower(proj_grad)


def params():
    return pltpu.CompilerParams(
        dimension_semantics=("arbitrary",), vmem_limit_bytes=52 * 1024 * 1024
    )


def effort(length, heads):
    return pl.CostEstimate(
        flops=length * heads * 10000000,
        bytes_accessed=length * heads * 8192,
        transcendentals=length * heads * 2048,
    )


def mixer_forward(heads, parts, place, proj, gate, taps, coefficients, gain, interpret=False):
    length = proj.shape[0]
    count = length // parts
    blocks = count // CHUNK
    width = heads * ROW
    values = heads * DV

    def tall(columns, at=0):
        return pl.BlockSpec((count, columns), lambda i, me: (jnp.bitwise_xor(i, me[0]), at))

    def whole(array):
        return pl.BlockSpec(array.shape, lambda i, me: (0,) * array.ndim)

    def stacked(first, second):
        return pl.BlockSpec((blocks, heads, first, second), lambda i, me: (i, 0, 0, 0))

    chunks = parts * blocks
    return pl.pallas_call(
        lambda *refs: forward_kernel(heads, *refs),
        grid_spec=pltpu.PrefetchScalarGridSpec(
            num_scalar_prefetch=1,
            grid=(parts,),
            in_specs=[
                tall(width),
                tall(LANES, width // LANES),
                tall(values),
                whole(taps),
                whole(coefficients),
                whole(gain),
            ],
            out_specs=[
                tall(values),
                tall(values),
                stacked(CHUNK, CHUNK),
                stacked(DV, DK),
                tall(values),
                tall(values),
                tall(heads * DK),
            ],
            scratch_shapes=[
                pltpu.VMEM((HALO, width), wide),
                pltpu.VMEM((heads, DV, DK), wide),
            ],
        ),
        out_shape=[
            jax.ShapeDtypeStruct((length, values), narrow),
            jax.ShapeDtypeStruct((length, values), narrow),
            jax.ShapeDtypeStruct((chunks, heads, CHUNK, CHUNK), narrow),
            jax.ShapeDtypeStruct((chunks, heads, DV, DK), narrow),
            jax.ShapeDtypeStruct((length, values), narrow),
            jax.ShapeDtypeStruct((length, values), narrow),
            jax.ShapeDtypeStruct((length, heads * DK), narrow),
        ],
        compiler_params=params(),
        cost_estimate=effort(length, heads),
        interpret=interpret,
    )(place, proj, proj, gate, taps, coefficients, gain)


def mixer_backward(
    heads, parts, place, proj, gate, taps, coefficients, gain, kept, grad_gated, interpret=False
):
    length = proj.shape[0]
    count = length // parts
    blocks = count // CHUNK
    width = heads * ROW
    values = heads * DV
    edge_rows = 2 * HALO
    ratio = count // edge_rows

    def tall(columns, at=0):
        return pl.BlockSpec(
            (count, columns), lambda i, me: (jnp.bitwise_xor(parts - 1 - i, me[0]), at)
        )

    def edge_at(i, me):
        previous = jnp.bitwise_xor(jnp.maximum(parts - 2 - i, 0), me[0])
        return (previous * ratio + ratio - 1, 0)

    def whole(shape):
        return pl.BlockSpec(shape, lambda i, me: (0,) * len(shape))

    def stacked(first, second):
        return pl.BlockSpec(
            (blocks, heads, first, second), lambda i, me: (parts - 1 - i, 0, 0, 0)
        )

    total = width + LANES + values
    return pl.pallas_call(
        lambda *refs: backward_kernel(heads, *refs),
        grid_spec=pltpu.PrefetchScalarGridSpec(
            num_scalar_prefetch=1,
            grid=(parts,),
            in_specs=[
                tall(width),
                pl.BlockSpec((edge_rows, width), edge_at),
                tall(LANES, width // LANES),
                tall(values),
                whole(taps.shape),
                whole(coefficients.shape),
                whole(gain.shape),
                tall(values),
                stacked(CHUNK, CHUNK),
                stacked(DV, DK),
                tall(values),
                tall(values),
                tall(heads * DK),
                tall(values),
            ],
            out_specs=[
                tall(total),
                whole((HALO, width)),
                whole((HALO, DV)),
                whole((HALO, LANES)),
            ],
            scratch_shapes=[
                pltpu.VMEM((HALO, width), wide),
                pltpu.VMEM((heads, DV, DK), wide),
            ],
        ),
        out_shape=[
            jax.ShapeDtypeStruct((length, total), narrow),
            jax.ShapeDtypeStruct((HALO, width), wide),
            jax.ShapeDtypeStruct((HALO, DV), wide),
            jax.ShapeDtypeStruct((HALO, LANES), wide),
        ],
        compiler_params=params(),
        cost_estimate=effort(length, heads),
        interpret=interpret,
    )(place, proj, proj, proj, gate, taps, coefficients, gain, *kept, grad_gated)


def to_lanes(array):
    groups, rows, columns = array.shape
    split = array.reshape(groups, rows, columns // LANES, LANES)
    return jnp.swapaxes(split, 1, 2).reshape(groups, -1, LANES)


def from_lanes(array, rows):
    groups = array.shape[0]
    split = array.reshape(groups, -1, rows, LANES)
    return jnp.swapaxes(split, 1, 2).reshape(groups, rows, -1)


def per_device(
    tokens,
    cotangent,
    norm_attn,
    w_qkv,
    w_ba,
    conv_w,
    a_log,
    dt_bias,
    w_outgate,
    head_gain,
    w_out,
    norm_ffn,
    w_gate,
    w_up,
    w_down,
    interpret=False,
):
    parts = lax.axis_size("seq")
    shards = lax.axis_size("dp")
    place = lax.axis_index("seq")
    head_count = a_log.shape[0]
    heads = head_count // parts
    width = heads * ROW
    values = heads * DV
    model = tokens.shape[2]
    own = norm_attn.shape[0]
    out_rows = w_out.shape[0]
    quarter = model // parts

    def mine(array, size, axis):
        return lax.dynamic_slice_in_dim(array, place * size, size, axis)

    def flip(array, bit):
        return lax.ppermute(array, "seq", [(i, i ^ bit) for i in range(parts)])

    def over_dp(array):
        return lax.all_gather(array, "dp", axis=0, tiled=True)

    def sum_dp(array):
        return lax.psum_scatter(array, "dp", scatter_dimension=0, tiled=True)

    def gather_seq(array):
        across = flip(array, 2)
        near = jnp.concatenate([array, flip(array, 1)], axis=0)
        far = jnp.concatenate([across, flip(across, 1)], axis=0)
        return near, far

    def scatter_seq(near, far):
        half = near.shape[0] // 2
        across = far[:half] + flip(lower(far[half:]), 1).astype(wide)
        across = flip(lower(across), 2)
        beside = flip(lower(near[half:]), 1)
        return near[:half] + beside.astype(wide) + across.astype(wide)

    def absolute(stack):
        return jnp.concatenate(
            [
                lax.dynamic_index_in_dim(stack, jnp.bitwise_xor(place, at), 0)
                for at in range(parts)
            ],
            axis=0,
        )

    def stack_seq(array):
        near, far = gather_seq(array[None])
        return jnp.concatenate([near, far], axis=0)

    def exchange(stack):
        pieces = [
            lax.dynamic_index_in_dim(stack, jnp.bitwise_xor(place, at), 0)
            for at in range(parts)
        ]
        return absolute(
            jnp.concatenate(
                [pieces[0]] + [flip(pieces[at], at) for at in range(1, parts)], axis=0
            )
        )

    ffn = w_gate.shape[1]
    piece = ffn // (shards * parts)
    ffn_own = -(-(piece * shards) // LANES) * LANES
    padded = ffn_own // shards

    def ffn_columns(array):
        split = array.reshape(own, shards, parts, piece)
        split = lax.dynamic_index_in_dim(split, place, 2, keepdims=False)
        split = jnp.pad(split, ((0, 0), (0, 0), (0, padded - piece)))
        return to_lanes(split.reshape(1, own, ffn_own))[0]

    own_tokens = tokens[:, 0, :]
    own_cot = cotangent[:, 0, :]
    all_tokens = jnp.concatenate(gather_seq(own_tokens), axis=0)
    small_flat = jnp.concatenate([norm_attn, norm_ffn, conv_w.reshape(-1)])
    small_all = over_dp(small_flat[None, :])
    first_gain = small_all[:, :own].reshape(-1).astype(wide)
    second_gain = small_all[:, own : 2 * own].reshape(-1).astype(wide)
    taps_all = jnp.swapaxes(small_all[:, 2 * own :].reshape(shards, CONV, -1), 0, 1)
    taps = mine(taps_all.reshape(CONV, -1), width, 1).astype(wide)
    taps = jnp.pad(taps, ((0, HALO - CONV), (0, 0)))
    w_in = over_dp(
        jnp.concatenate(
            [
                mine(w_qkv, width, 1),
                jnp.pad(mine(w_ba, 2 * heads, 1), ((0, 0), (0, LANES - 2 * heads))),
                mine(w_outgate, values, 1),
            ],
            axis=1,
        )
    )
    ffn_part = jnp.concatenate(
        [
            ffn_columns(w_gate),
            ffn_columns(w_up),
            to_lanes(
                jnp.pad(
                    mine(w_down, piece, 0), ((0, padded - piece), (0, 0))
                )[None]
            )[0],
            to_lanes(mine(w_out, quarter, 1)[None])[0],
        ],
        axis=0,
    )
    ffn_part, w_in = lax.optimization_barrier((ffn_part, w_in))
    ffn_all = over_dp(ffn_part).reshape(shards, -1, LANES)
    decay_part = mine(a_log, heads, 0)
    bias_part = mine(dt_bias, heads, 0)

    def odd_lanes(vector):
        spaced = jnp.stack([jnp.zeros_like(vector), vector], axis=1).reshape(-1)
        return jnp.pad(spaced, (0, LANES - 2 * heads))[None, :]

    coefficients = jnp.pad(
        jnp.concatenate([odd_lanes(bias_part), odd_lanes(-jnp.exp(decay_part))], axis=0),
        ((0, HALO - 2), (0, 0)),
    )
    gain = jnp.broadcast_to(head_gain.astype(wide)[None, :], (HALO, DV))
    place_row = place.astype(jnp.int32)[None]

    rows = own_tokens.astype(wide)
    inverse_one = row_norm(rows, first_gain)[1]
    all_rows = all_tokens.astype(wide)
    normed_one, all_inverse = row_norm(all_rows, first_gain)
    normed_one = lower(normed_one)
    proj = lower(by_weight(normed_one, w_in[:, : width + LANES]))
    out_gate = by_weight(normed_one, w_in[:, width + LANES :])
    proj, cot_halves = lax.optimization_barrier((proj, gather_seq(own_cot)))
    gated, *kept = mixer_forward(
        heads, parts, place_row, proj, out_gate, taps, coefficients, gain, interpret
    )
    ffn_all, gated = lax.optimization_barrier((ffn_all, gated))
    out_part = from_lanes(ffn_all[:, -out_rows * (quarter // LANES) :], out_rows)
    w_out_own = jnp.swapaxes(
        exchange(out_part.reshape(parts, values, quarter)), 0, 1
    ).reshape(values, model)
    wide_rows = own * (ffn_own // LANES)
    gate_own = from_lanes(ffn_all[:, :wide_rows], own).reshape(model, ffn_own)
    up_own = from_lanes(ffn_all[:, wide_rows : 2 * wide_rows], own).reshape(model, ffn_own)
    down_own = from_lanes(ffn_all[:, 2 * wide_rows : 2 * wide_rows + padded * (model // LANES)], padded).reshape(ffn_own, model)
    half = gated.shape[0] // 2
    mixed_far = by_weight(gated[half:], w_out_own)
    mixed_near = by_weight(gated[:half], w_out_own)
    after_mix = rows + scatter_seq(mixed_near, mixed_far)
    normed_two, inverse_two = row_norm(after_mix, second_gain)
    sides = []
    for normed_half, cot_half in zip(gather_seq(lower(normed_two)), cot_halves):
        gate_pre = by_weight(normed_half, gate_own)
        up_pre = by_weight(normed_half, up_own)
        sig_ffn = jax.nn.sigmoid(gate_pre)
        hidden = lower(gate_pre * sig_ffn * up_pre)
        grad_hidden = by_transpose(cot_half, down_own)
        grad_gate_pre = lower(
            grad_hidden * up_pre * sig_ffn * (1.0 + gate_pre * (1.0 - sig_ffn))
        )
        grad_up_pre = lower(grad_hidden * gate_pre * sig_ffn)
        back = by_transpose(grad_gate_pre, gate_own) + by_transpose(grad_up_pre, up_own)
        sides.append(
            (
                back,
                by_weight(hidden, down_own),
                over_rows(normed_half, grad_gate_pre),
                over_rows(normed_half, grad_up_pre),
                over_rows(hidden, cot_half),
            )
        )
    near_side, far_side = sides
    back_two, grad_norm_ffn = norm_back(
        after_mix, inverse_two, second_gain, scatter_seq(near_side[0], far_side[0])
    )
    grad_after = own_cot.astype(wide) + back_two
    result = after_mix + scatter_seq(near_side[1], far_side[1])
    grad_ffn = sum_dp(
        jnp.concatenate(
            [
                to_lanes(lower(near_side[2] + far_side[2]).reshape(shards, own, ffn_own)),
                to_lanes(lower(near_side[3] + far_side[3]).reshape(shards, own, ffn_own)),
                to_lanes(lower(near_side[4] + far_side[4]).reshape(shards, padded, model)),
            ],
            axis=1,
        ).reshape(-1, LANES)
    )
    grad_branch = jnp.concatenate(gather_seq(lower(grad_after)), axis=0)
    grad_gated = by_transpose(grad_branch, w_out_own)
    grad_out = jnp.swapaxes(
        lower(over_rows(gated, grad_branch)).reshape(values, parts, quarter), 0, 1
    )
    grad_out = exchange(grad_out).reshape(shards, out_rows, quarter)
    grad_in, grad_taps, grad_gain, grad_small = mixer_backward(
        heads, parts, place_row, proj, out_gate, taps, coefficients, gain, kept, grad_gated, interpret
    )
    one_far = by_transpose(grad_in[half:], w_in)
    one_near = by_transpose(grad_in[:half], w_in)
    hat = all_rows * all_inverse
    grad_norm_attn = jnp.sum(one_far * hat[half:], axis=0) + jnp.sum(
        one_near * hat[:half], axis=0
    )
    grad_w_in = lower(over_rows(normed_one, grad_in)).reshape(shards, own, -1)

    taps_full = lax.dynamic_update_slice_in_dim(
        jnp.zeros((CONV, head_count * ROW), wide), grad_taps[:CONV], place * width, 1
    )

    def to_heads(lane_row):
        return lax.dynamic_update_slice_in_dim(
            jnp.zeros((head_count,), wide), lane_row[1 : 2 * heads : 2], place * heads, 0
        )

    common = jnp.concatenate([grad_gain[0], to_heads(grad_small[1]), to_heads(grad_small[0])])
    own_taps = conv_w.shape[1]
    packed = jnp.concatenate(
        [
            grad_norm_attn.reshape(shards, own),
            grad_norm_ffn.reshape(shards, own),
            jnp.swapaxes(taps_full.reshape(CONV, shards, own_taps), 0, 1).reshape(shards, -1),
            jnp.broadcast_to(common[None], (shards, common.shape[0])),
        ],
        axis=1,
    )
    tile = 2 * HALO * LANES
    packed = jnp.pad(packed, ((0, 0), (0, -packed.shape[1] % tile)))
    in_rows = own * (grad_w_in.shape[2] // LANES)
    lane_rows = out_rows * (quarter // LANES)
    last = sum_dp(
        jnp.concatenate(
            [
                to_lanes(grad_w_in),
                to_lanes(grad_out),
                lower(packed).reshape(shards, -1, LANES),
            ],
            axis=1,
        ).reshape(-1, LANES)
    )
    back_one = norm_back(rows, inverse_one, first_gain, scatter_seq(one_near, one_far))[0]
    grad_rows = lower(grad_after + back_one)[:, None, :]

    last_all = stack_seq(last)
    small_total = jnp.sum(
        last_all[:, in_rows + lane_rows :].astype(wide), axis=0
    ).reshape(-1)
    last_all = absolute(last_all)
    ffn_grads = absolute(stack_seq(grad_ffn))

    def side_by_side(array):
        return jnp.swapaxes(array, 0, 1).reshape(array.shape[1], -1).astype(wide)

    in_all = from_lanes(last_all[:, :in_rows], own)
    out_all = from_lanes(last_all[:, in_rows : in_rows + lane_rows], out_rows)

    def ffn_full(array):
        split = from_lanes(array, own).reshape(parts, own, shards, padded)[..., :piece]
        return jnp.transpose(split, (1, 2, 0, 3)).reshape(own, -1).astype(wide)

    down_all = from_lanes(ffn_grads[:, 2 * wide_rows :], padded)[:, :piece]
    taps_at = 2 * own
    gain_at = taps_at + CONV * own_taps
    heads_at = gain_at + DV

    return (
        lower(result)[:, None, :],
        grad_rows,
        small_total[:own],
        side_by_side(in_all[:, :, :width]),
        side_by_side(in_all[:, :, width : width + 2 * heads]),
        small_total[taps_at:gain_at].reshape(CONV, own_taps),
        small_total[heads_at : heads_at + head_count],
        small_total[heads_at + head_count : heads_at + 2 * head_count],
        side_by_side(in_all[:, :, width + LANES :]),
        small_total[gain_at:heads_at],
        side_by_side(out_all),
        small_total[own:taps_at],
        ffn_full(ffn_grads[:, :wide_rows]),
        ffn_full(ffn_grads[:, wide_rows : 2 * wide_rows]),
        down_all.reshape(parts * piece, model).astype(wide),
    )


def solution(mesh):
    return jax.shard_map(
        per_device,
        mesh=mesh,
        in_specs=(
            P("seq", "dp", None),
            P("seq", "dp", None),
            P("dp"),
            P("dp", None),
            P("dp", None),
            P(None, "dp"),
            P(),
            P(),
            P("dp", None),
            P(),
            P("dp", None),
            P("dp"),
            P("dp", None),
            P("dp", None),
            P("dp", None),
        ),
        out_specs=(
            P("seq", "dp", None),
            P("seq", "dp", None),
            P("dp"),
            P("dp", None),
            P("dp", None),
            P(None, "dp"),
            P(),
            P(),
            P("dp", None),
            P(),
            P("dp", None),
            P("dp"),
            P("dp", None),
            P("dp", None),
            P("dp", None),
        ),
        check_vma=False,
    )
```

```python
import jax
import jax.numpy as jnp
from jax import lax
from jax.experimental import pallas as pl
from jax.experimental.pallas import tpu as pltpu
from jax.sharding import PartitionSpec as P

DK = 128
DV = 256
CONV = 4
ROW = 2 * DK + DV
LANES = 128
CHUNK = 256
HALO = 8

epsilon = 1e-06
narrow = jnp.bfloat16
wide = jnp.float32


def by_weight(left, right):
    return jnp.dot(left, right, preferred_element_type=wide)


def by_transpose(left, right):
    return lax.dot_general(
        left, right, (((1,), (1,)), ((), ())), preferred_element_type=wide
    )


def over_rows(left, right):
    return lax.dot_general(
        left, right, (((0,), (0,)), ((), ())), preferred_element_type=wide
    )


def row_norm(values, gain):
    inverse = lax.rsqrt(jnp.mean(values * values, axis=-1, keepdims=True) + epsilon)
    return (values * inverse * gain, inverse)


def norm_back(values, inverse, gain, grad_out):
    scaled = grad_out * gain
    grad_in = inverse * scaled - values * inverse * inverse * inverse * jnp.mean(
        scaled * values, axis=-1, keepdims=True
    )
    grad_gain = jnp.sum(grad_out * values * inverse, axis=tuple(range(values.ndim - 1)))
    return (grad_in, grad_gain)


def lower(array):
    return array.astype(narrow)


def row_sum(array):
    return jnp.sum(array, axis=1, keepdims=True)


def grid_indices():
    rows = lax.broadcasted_iota(jnp.int32, (CHUNK, CHUNK), 0)
    columns = lax.broadcasted_iota(jnp.int32, (CHUNK, CHUNK), 1)
    return rows, columns


def exact_dot(left, right):
    return jnp.dot(
        left, right, precision=lax.Precision.HIGHEST, preferred_element_type=wide
    )


def shifted_rows(rows, before):
    return jnp.concatenate([before, rows], axis=0)


def convolved(extended, taps, count):
    start = HALO - CONV + 1
    summed = extended[start : start + count] * taps[0:1]
    for offset in range(1, CONV):
        summed = summed + extended[start + offset : start + offset + count] * taps[
            offset : offset + 1
        ]
    return summed


def gates(rates, coefficients):
    strength = jax.nn.sigmoid(rates)
    shifted = rates + coefficients[0:1]
    decay = coefficients[1:2] * jax.nn.softplus(shifted)
    return strength, shifted, decay


def unit(values):
    return lax.rsqrt(row_sum(values * values) + epsilon)


def in_turn(parts):
    waiting = list(parts)
    while waiting:
        still = []
        for part in waiting:
            try:
                next(part)
                still.append(part)
            except StopIteration:
                pass
        waiting = still


def invert(lower_part, rows, columns, store):
    apart = jnp.bitwise_xor(rows, columns)
    inverse = jnp.where(rows == columns, 1.0, 0.0) - jnp.where(apart == 1, lower_part, 0.0)
    level = 1
    while (1 << level) < CHUNK:
        corner = lower(
            jnp.where(lax.shift_right_logical(apart, level) == 1, lower_part, 0.0)
        )
        held = lower(inverse)
        yield
        side = lower(by_weight(corner, held))
        yield
        inverse = inverse - by_weight(held, side)
        level += 1
    store.append(lower(inverse))


def forward_kernel(
    heads,
    place_ref,
    proj_ref,
    rates_ref,
    taps_ref,
    coef_ref,
    mixed_ref,
    inverse_ref,
    state_ref,
    corrected_ref,
    update_ref,
    weight_ref,
    before,
    state,
):
    @pl.when(pl.program_id(0) == 0)
    def _():
        before[...] = jnp.zeros_like(before)
        state[...] = jnp.zeros_like(state)

    count = proj_ref.shape[0]
    rows, columns = grid_indices()
    raw = proj_ref[...].astype(wide)
    summed = convolved(shifted_rows(raw, before[...]), taps_ref[...], count)
    before[...] = raw[count - HALO :]
    active = summed * jax.nn.sigmoid(summed)
    strength_rows, unused, decay_rows = gates(rates_ref[...].astype(wide), coef_ref[...])
    through = jnp.where(rows >= columns, 1.0, 0.0)
    states = {(0, head): state[head] for head in range(heads)}
    blocks = count // CHUNK
    cumulative_rows = [
        exact_dot(through, decay_rows[block * CHUNK : (block + 1) * CHUNK])
        for block in range(blocks)
    ]
    turned_rows = [item.T for item in cumulative_rows]

    def one(block, head):
        base = head * ROW
        here = slice(block * CHUNK, (block + 1) * CHUNK)
        query = active[here, base : base + DK]
        key = active[here, base + DK : base + 2 * DK]
        value = active[here, base + 2 * DK : base + ROW]
        query = query * (unit(query) * DK ** (-0.5))
        key = key * unit(key)
        strength = strength_rows[here, 2 * head : 2 * head + 1]
        cumulative = cumulative_rows[block][:, 2 * head + 1 : 2 * head + 2]
        across = turned_rows[block][2 * head + 1 : 2 * head + 2]
        final = cumulative[CHUNK - 1 :]
        fade = jnp.where(
            rows >= columns, jnp.exp(jnp.minimum(cumulative - across, 0.0)), 0.0
        )
        grown = jnp.exp(cumulative)
        key_low = lower(key)
        query_low = lower(query)
        dots = by_transpose(key_low, key_low)
        yield
        lower_part = jnp.where(rows > columns, strength * fade * dots, 0.0)
        store = []
        yield from invert(lower_part, rows, columns, store)
        inverse = store[0]
        yield
        update = by_weight(inverse, lower(strength * value))
        weight = lower(by_weight(inverse, lower(strength * grown * key)))
        inner = lower(by_transpose(query_low, key_low) * fade)
        faded = lower(key * jnp.exp(final - cumulative))
        inverse_ref[block, head] = inverse
        span = slice(head * DV, head * DV + DV)
        update_ref[here, span] = lower(update)
        weight_ref[here, head * DK : head * DK + DK] = weight
        yield
        while (block, head) not in states:
            yield
        held = states[block, head]
        held_low = lower(held)
        state_ref[block, head] = held_low
        corrected = lower(update - by_transpose(weight, held_low))
        yield
        states[block + 1, head] = held * jnp.exp(final) + over_rows(corrected, faded)
        corrected_ref[here, span] = corrected
        result = grown * by_transpose(query_low, held_low) + by_weight(inner, corrected)
        yield
        mixed_ref[here, span] = lower(result)

    in_turn(one(block, head) for block in range(blocks) for head in range(heads))
    for head in range(heads):
        state[head] = states[blocks, head]


def gate_kernel(heads, mixed_ref, normed_ref, weight_ref, gain_ref, gated_ref, gate_ref):
    gate = by_weight(normed_ref[...], weight_ref[...])
    gate_ref[...] = gate
    gain = gain_ref[0:1]
    for head in range(heads):
        span = slice(head * DV, head * DV + DV)
        normed, unused = row_norm(mixed_ref[:, span].astype(wide), gain)
        here = gate[:, span]
        gated_ref[:, span] = lower(normed * (here * jax.nn.sigmoid(here)))


def backward_kernel(
    heads,
    place_ref,
    proj_ref,
    edge_ref,
    rates_ref,
    gate_ref,
    taps_ref,
    coef_ref,
    gain_ref,
    mixed_ref,
    inverse_ref,
    state_ref,
    corrected_ref,
    update_ref,
    weight_ref,
    grad_ref,
    out_ref,
    taps_grad_ref,
    gain_grad_ref,
    small_grad_ref,
    after,
    state_grad,
):
    step = pl.program_id(0)

    @pl.when(step == 0)
    def _():
        after[...] = jnp.zeros_like(after)
        state_grad[...] = jnp.zeros_like(state_grad)
        taps_grad_ref[...] = jnp.zeros_like(taps_grad_ref)
        gain_grad_ref[...] = jnp.zeros_like(gain_grad_ref)
        small_grad_ref[...] = jnp.zeros_like(small_grad_ref)

    count = proj_ref.shape[0]
    blocks = count // CHUNK
    rows, columns = grid_indices()
    lanes = lax.broadcasted_iota(jnp.int32, (CHUNK, LANES), 1)
    raw = proj_ref[...].astype(wide)
    edge = edge_ref[edge_ref.shape[0] - HALO :].astype(wide)
    edge = jnp.where(step == pl.num_programs(0) - 1, 0.0, edge)
    taps = taps_ref[...]
    extended = shifted_rows(raw, edge)
    summed = convolved(extended, taps, count)
    sig = jax.nn.sigmoid(summed)
    active = summed * sig
    coefficients = coef_ref[...]
    strength_rows, shifted_rates, decay_rows = gates(
        rates_ref[...].astype(wide), coefficients
    )
    through = jnp.where(rows >= columns, 1.0, 0.0)
    onward = jnp.where(columns >= rows, 1.0, 0.0)
    gain = gain_ref[0:1]
    proj_width = heads * ROW
    cumulative_rows = [
        exact_dot(through, decay_rows[block * CHUNK : (block + 1) * CHUNK])
        for block in range(blocks)
    ]
    turned_rows = [item.T for item in cumulative_rows]
    laters = {(blocks - 1, head): state_grad[head] for head in range(heads)}
    active_grads = {}
    column_grads = {}
    gain_grads = []

    def one(block, head):
        here = slice(block * CHUNK, (block + 1) * CHUNK)
        span = slice(head * DV, head * DV + DV)
        grad_gated = grad_ref[here, span].astype(wide)
        mixed = mixed_ref[here, span].astype(wide)
        normed, head_inverse = row_norm(mixed, gain)
        gate = gate_ref[here, span]
        sig_gate = jax.nn.sigmoid(gate)
        gate_start = proj_width + LANES + head * DV
        out_ref[here, gate_start : gate_start + DV] = lower(
            grad_gated * normed * sig_gate * (1.0 + gate * (1.0 - sig_gate))
        )
        normed_grad = grad_gated * (gate * sig_gate)
        scaled = normed_grad * gain
        grad_mixed = lower(
            head_inverse * scaled
            - mixed
            * (head_inverse * head_inverse * head_inverse)
            * jnp.mean(scaled * mixed, axis=-1, keepdims=True)
        )
        gain_grads.append(
            jnp.sum(normed_grad * mixed * head_inverse, axis=0, keepdims=True)
        )
        base = head * ROW
        query_raw = active[here, base : base + DK]
        key_raw = active[here, base + DK : base + 2 * DK]
        value = active[here, base + 2 * DK : base + ROW]
        query_unit = unit(query_raw)
        key_unit = unit(key_raw)
        query = query_raw * (query_unit * DK ** (-0.5))
        key = key_raw * key_unit
        strength = strength_rows[here, 2 * head : 2 * head + 1]
        cumulative = cumulative_rows[block][:, 2 * head + 1 : 2 * head + 2]
        across = turned_rows[block][2 * head + 1 : 2 * head + 2]
        final = cumulative[CHUNK - 1 :]
        fade = jnp.where(
            rows >= columns, jnp.exp(jnp.minimum(cumulative - across, 0.0)), 0.0
        )
        strict_fade = jnp.where(rows > columns, fade, 0.0)
        grown = jnp.exp(cumulative)
        remaining = jnp.exp(final - cumulative)
        kept = jnp.exp(final)
        key_low = lower(key)
        query_low = lower(query)
        yield
        dots = by_transpose(key_low, key_low)
        cross = by_transpose(query_low, key_low)
        held = state_ref[block, head]
        corrected = corrected_ref[here, span]
        weight = weight_ref[here, head * DK : head * DK + DK]
        faded = key * remaining
        faded_low = lower(faded)
        grown_query = query * grown
        yield
        inner_side = over_rows(lower(cross * fade), grad_mixed)
        state_side = over_rows(grad_mixed, lower(grown_query))
        dot_grad = by_transpose(grad_mixed, corrected) * fade
        dot_grad_low = lower(dot_grad)
        grown_grad = by_weight(grad_mixed, held)
        yield
        while (block, head) not in laters:
            yield
        later = laters[block, head]
        later_low = lower(later)
        corrected_grad_low = lower(inner_side + by_transpose(faded_low, later_low))
        yield
        laters[block - 1, head] = (
            later * kept + state_side - over_rows(corrected_grad_low, weight)
        )
        faded_grad = by_weight(corrected, later_low)
        weight_grad = lower(-by_weight(corrected_grad_low, held))
        inverse = inverse_ref[block, head]
        yield
        value_side = over_rows(inverse, corrected_grad_low)
        key_side = over_rows(inverse, weight_grad)
        yield
        lower_grad = -(
            by_transpose(lower(value_side), update_ref[here, span])
            + by_transpose(lower(key_side), weight)
        ) * strict_fade
        inner_query = by_weight(dot_grad_low, key_low)
        inner_key = over_rows(dot_grad_low, query_low)
        yield
        lower_grad_low = lower(lower_grad)
        first_key = by_weight(lower_grad_low, key_low)
        second_key = over_rows(lower_grad_low, lower(strength * key))
        pairs = lower_grad * dots
        both = pairs * strength + dot_grad * cross
        faded_sum = row_sum(faded_grad * faded)
        key_sum = row_sum(key_side * key)
        yield
        query_grad = grown * grown_grad + inner_query
        key_grad = (
            (strength * grown) * key_side
            + strength * first_key
            + second_key
            + inner_key
            + remaining * faded_grad
        )
        head_strength_grad = row_sum(value_side * value) + grown * key_sum + row_sum(pairs)
        head_spread = (
            (strength * grown) * key_sum
            + row_sum(both)
            + row_sum(grown_grad * grown_query)
            - faded_sum
        )
        column_total = jnp.sum(both, axis=0, keepdims=True)
        late_total = row_sum(jnp.where(columns >= rows, column_total, 0.0))
        final_grad = kept * jnp.sum(held.astype(wide) * later, keepdims=True) + jnp.sum(
            faded_sum, axis=0, keepdims=True
        )
        column_grads[block, head] = (
            head_strength_grad,
            head_spread,
            final_grad - late_total,
        )
        active_grads[block, head] = (
            DK ** (-0.5)
            * query_unit
            * (
                query_grad
                - query_raw * (query_unit * query_unit) * row_sum(query_grad * query_raw)
            ),
            key_unit
            * (key_grad - key_raw * (key_unit * key_unit) * row_sum(key_grad * key_raw)),
            strength * value_side,
        )

    in_turn(
        one(block, head) for block in reversed(range(blocks)) for head in range(heads)
    )
    for head in range(heads):
        state_grad[head] = laters[-1, head]
    for block in range(blocks):
        here = slice(block * CHUNK, (block + 1) * CHUNK)
        strength_grad = jnp.zeros((CHUNK, LANES), wide)
        spread_grad = jnp.zeros((CHUNK, LANES), wide)
        extra_grad = jnp.zeros((CHUNK, LANES), wide)
        for head in range(heads):
            first, second, third = column_grads[block, head]
            strength_grad = jnp.where(lanes == 2 * head, first, strength_grad)
            spread_grad = jnp.where(lanes == 2 * head + 1, second, spread_grad)
            extra_grad = jnp.where(lanes == 2 * head + 1, third, extra_grad)
        decay_grad = exact_dot(onward, spread_grad) + extra_grad
        shift_grad = decay_grad * coefficients[1:2] * jax.nn.sigmoid(shifted_rates[here])
        strength_here = strength_rows[here]
        rates_grad = strength_grad * strength_here * (1.0 - strength_here) + shift_grad
        out_ref[here, proj_width : proj_width + LANES] = lower(rates_grad)
        small_grad_ref[0:1] += jnp.sum(shift_grad, axis=0, keepdims=True)
        small_grad_ref[1:2] += jnp.sum(decay_grad * decay_rows[here], axis=0, keepdims=True)
    gain_grad_ref[0:1] += sum(gain_grads)
    joined = jnp.concatenate(
        [
            jnp.concatenate(
                [part for head in range(heads) for part in active_grads[block, head]], axis=1
            )
            for block in range(blocks)
        ],
        axis=0,
    )
    summed_grad = joined * (sig * (1.0 + summed * (1.0 - sig)))
    following = jnp.concatenate([summed_grad, after[...]], axis=0)
    after[...] = summed_grad[:HALO]
    proj_grad = following[CONV - 1 : CONV - 1 + count] * taps[0:1]
    start = HALO - CONV + 1
    for offset in range(CONV):
        if offset:
            shift = CONV - 1 - offset
            proj_grad = proj_grad + following[shift : shift + count] * taps[offset : offset + 1]
        taps_grad_ref[offset : offset + 1] += jnp.sum(
            summed_grad * extended[start + offset : start + offset + count],
            axis=0,
            keepdims=True,
        )
    out_ref[:, :proj_width] = lower(proj_grad)


def params():
    return pltpu.CompilerParams(
        dimension_semantics=("arbitrary",), vmem_limit_bytes=52 * 1024 * 1024
    )


def effort(length, heads, each=10000000):
    return pl.CostEstimate(
        flops=length * heads * each,
        bytes_accessed=length * heads * 1024,
        transcendentals=length * heads,
    )


def mixer_forward(heads, parts, place, proj, taps, coefficients, interpret=False):
    length = proj.shape[0]
    count = length // parts
    blocks = count // CHUNK
    width = heads * ROW
    values = heads * DV

    def tall(columns, at=0):
        return pl.BlockSpec((count, columns), lambda i, me: (jnp.bitwise_xor(i, me[0]), at))

    def whole(array):
        return pl.BlockSpec(array.shape, lambda i, me: (0,) * array.ndim)

    def stacked(first, second):
        return pl.BlockSpec((blocks, heads, first, second), lambda i, me: (i, 0, 0, 0))

    chunks = parts * blocks
    return pl.pallas_call(
        lambda *refs: forward_kernel(heads, *refs),
        grid_spec=pltpu.PrefetchScalarGridSpec(
            num_scalar_prefetch=1,
            grid=(parts,),
            in_specs=[
                tall(width),
                tall(LANES, width // LANES),
                whole(taps),
                whole(coefficients),
            ],
            out_specs=[
                tall(values),
                stacked(CHUNK, CHUNK),
                stacked(DV, DK),
                tall(values),
                tall(values),
                tall(heads * DK),
            ],
            scratch_shapes=[
                pltpu.VMEM((HALO, width), wide),
                pltpu.VMEM((heads, DV, DK), wide),
            ],
        ),
        out_shape=[
            jax.ShapeDtypeStruct((length, values), narrow),
            jax.ShapeDtypeStruct((chunks, heads, CHUNK, CHUNK), narrow),
            jax.ShapeDtypeStruct((chunks, heads, DV, DK), narrow),
            jax.ShapeDtypeStruct((length, values), narrow),
            jax.ShapeDtypeStruct((length, values), narrow),
            jax.ShapeDtypeStruct((length, heads * DK), narrow),
        ],
        compiler_params=params(),
        cost_estimate=effort(length, heads),
        interpret=interpret,
    )(place, proj, proj, taps, coefficients)


def gate_rows(heads, mixed, normed, weight, gain, interpret=False):
    length, values = mixed.shape
    model = normed.shape[1]
    block = 2 * CHUNK

    def tall(columns):
        return pl.BlockSpec((block, columns), lambda i: (i, 0))

    def whole(shape):
        return pl.BlockSpec(shape, lambda i: (0, 0))

    return pl.pallas_call(
        lambda *refs: gate_kernel(heads, *refs),
        grid=(length // block,),
        in_specs=[tall(values), tall(model), whole(weight.shape), whole(gain.shape)],
        out_specs=[tall(values), tall(values)],
        out_shape=[
            jax.ShapeDtypeStruct((length, values), narrow),
            jax.ShapeDtypeStruct((length, values), wide),
        ],
        compiler_params=params(),
        cost_estimate=pl.CostEstimate(
            flops=4 * length * model * values, bytes_accessed=length * values * 8,
            transcendentals=length * values,
        ),
        interpret=interpret,
    )(mixed, normed, weight, gain)


def mixer_backward(
    heads, parts, place, proj, gate, taps, coefficients, gain, kept, grad_gated, interpret=False
):
    length = proj.shape[0]
    count = length // parts
    blocks = count // CHUNK
    width = heads * ROW
    values = heads * DV
    edge_rows = 2 * HALO
    ratio = count // edge_rows

    def tall(columns, at=0):
        return pl.BlockSpec(
            (count, columns), lambda i, me: (jnp.bitwise_xor(parts - 1 - i, me[0]), at)
        )

    def edge_at(i, me):
        previous = jnp.bitwise_xor(jnp.maximum(parts - 2 - i, 0), me[0])
        return (previous * ratio + ratio - 1, 0)

    def whole(shape):
        return pl.BlockSpec(shape, lambda i, me: (0,) * len(shape))

    def stacked(first, second):
        return pl.BlockSpec(
            (blocks, heads, first, second), lambda i, me: (parts - 1 - i, 0, 0, 0)
        )

    total = width + LANES + values
    return pl.pallas_call(
        lambda *refs: backward_kernel(heads, *refs),
        grid_spec=pltpu.PrefetchScalarGridSpec(
            num_scalar_prefetch=1,
            grid=(parts,),
            in_specs=[
                tall(width),
                pl.BlockSpec((edge_rows, width), edge_at),
                tall(LANES, width // LANES),
                tall(values),
                whole(taps.shape),
                whole(coefficients.shape),
                whole(gain.shape),
                tall(values),
                stacked(CHUNK, CHUNK),
                stacked(DV, DK),
                tall(values),
                tall(values),
                tall(heads * DK),
                tall(values),
            ],
            out_specs=[
                tall(total),
                whole((HALO, width)),
                whole((HALO, DV)),
                whole((HALO, LANES)),
            ],
            scratch_shapes=[
                pltpu.VMEM((HALO, width), wide),
                pltpu.VMEM((heads, DV, DK), wide),
            ],
        ),
        out_shape=[
            jax.ShapeDtypeStruct((length, total), narrow),
            jax.ShapeDtypeStruct((HALO, width), wide),
            jax.ShapeDtypeStruct((HALO, DV), wide),
            jax.ShapeDtypeStruct((HALO, LANES), wide),
        ],
        compiler_params=params(),
        cost_estimate=effort(length, heads, 100000),
        interpret=interpret,
    )(place, proj, proj, proj, gate, taps, coefficients, gain, *kept, grad_gated)


def to_lanes(array):
    groups, rows, columns = array.shape
    split = array.reshape(groups, rows, columns // LANES, LANES)
    return jnp.swapaxes(split, 1, 2).reshape(groups, -1, LANES)


def from_lanes(array, rows):
    groups = array.shape[0]
    split = array.reshape(groups, -1, rows, LANES)
    return jnp.swapaxes(split, 1, 2).reshape(groups, rows, -1)


def per_device(
    tokens,
    cotangent,
    norm_attn,
    w_qkv,
    w_ba,
    conv_w,
    a_log,
    dt_bias,
    w_outgate,
    head_gain,
    w_out,
    norm_ffn,
    w_gate,
    w_up,
    w_down,
    interpret=False,
):
    parts = lax.axis_size("seq")
    shards = lax.axis_size("dp")
    place = lax.axis_index("seq")
    head_count = a_log.shape[0]
    heads = head_count // parts
    width = heads * ROW
    values = heads * DV
    model = tokens.shape[2]
    own = norm_attn.shape[0]
    out_rows = w_out.shape[0]
    quarter = model // parts

    def mine(array, size, axis):
        return lax.dynamic_slice_in_dim(array, place * size, size, axis)

    def flip(array, bit):
        return lax.ppermute(array, "seq", [(i, i ^ bit) for i in range(parts)])

    def over_dp(array):
        return lax.all_gather(array, "dp", axis=0, tiled=True)

    def sum_dp(array):
        return lax.psum_scatter(array, "dp", scatter_dimension=0, tiled=True)

    def gather_seq(array):
        across = flip(array, 2)
        near = jnp.concatenate([array, flip(array, 1)], axis=0)
        far = jnp.concatenate([across, flip(across, 1)], axis=0)
        return near, far

    def scatter_seq(near, far, beside=None):
        half = near.shape[0] // 2
        across = far[:half] + flip(lower(far[half:]), 1).astype(wide)
        across = flip(lower(across), 2)
        sibling = flip(lower(near[half:]), 1)
        if beside is not None:
            across, beside = lax.optimization_barrier((across, beside))
        total = near[:half] + sibling.astype(wide) + across.astype(wide)
        return (total, beside)

    def sum_all(array):
        for bit in range(1, parts):
            if bit & (bit - 1) == 0:
                array = array + flip(array, bit)
        bit = 1
        while bit < shards:
            array = array + lax.ppermute(array, "dp", [(i, i ^ bit) for i in range(shards)])
            bit *= 2
        return array

    def absolute(stack):
        return jnp.concatenate(
            [
                lax.dynamic_index_in_dim(stack, jnp.bitwise_xor(place, at), 0)
                for at in range(parts)
            ],
            axis=0,
        )

    def stack_seq(array):
        near, far = gather_seq(array[None])
        return jnp.concatenate([near, far], axis=0)

    def exchange(stack):
        pieces = [
            lax.dynamic_index_in_dim(stack, jnp.bitwise_xor(place, at), 0)
            for at in range(parts)
        ]
        return absolute(
            jnp.concatenate(
                [pieces[0]] + [flip(pieces[at], at) for at in range(1, parts)], axis=0
            )
        )

    ffn = w_gate.shape[1]
    piece = ffn // (shards * parts)
    ffn_own = -(-(piece * shards) // LANES) * LANES
    padded = ffn_own // shards

    def ffn_columns(array):
        split = array.reshape(own, shards, parts, piece)
        split = lax.dynamic_index_in_dim(split, place, 2, keepdims=False)
        split = jnp.pad(split, ((0, 0), (0, 0), (0, padded - piece)))
        return split.reshape(own, ffn_own)

    tie = lax.optimization_barrier
    own_tokens = tokens[:, 0, :]
    own_cot = cotangent[:, 0, :]
    half_lanes = LANES // 2
    small_flat = jnp.concatenate([norm_attn, norm_ffn, conv_w.reshape(-1)])
    small_count = small_flat.shape[0]
    small_flat = jnp.pad(small_flat, (0, own * half_lanes - small_count))
    w_in = over_dp(
        jnp.concatenate(
            [
                mine(w_qkv, width, 1),
                jnp.pad(
                    mine(w_ba, 2 * heads, 1), ((0, 0), (0, half_lanes - 2 * heads))
                ),
                small_flat.reshape(own, half_lanes),
            ],
            axis=1,
        )
    )
    all_tokens = jnp.concatenate(gather_seq(own_tokens), axis=0)
    small_all = w_in[:, width + half_lanes :].reshape(shards, -1)[:, :small_count]
    first_gain = small_all[:, :own].reshape(-1).astype(wide)
    second_gain = small_all[:, own : 2 * own].reshape(-1).astype(wide)
    taps_all = jnp.swapaxes(small_all[:, 2 * own :].reshape(shards, CONV, -1), 0, 1)
    taps = mine(taps_all.reshape(CONV, -1), width, 1).astype(wide)
    taps = jnp.pad(taps, ((0, HALO - CONV), (0, 0)))

    out_ratio = out_rows // own
    second = jnp.concatenate(
        [
            mine(w_outgate, values, 1),
            jnp.swapaxes(
                mine(w_out, quarter, 1).reshape(out_ratio, own, quarter), 0, 1
            ).reshape(own, -1),
        ],
        axis=1,
    )
    cot_near, cot_far = gather_seq(own_cot)
    second, w_in, all_tokens, cot_near, cot_far = tie(
        (second, w_in, all_tokens, cot_near, cot_far)
    )
    second_all = over_dp(second)
    down_part = jnp.pad(mine(w_down, piece, 0), ((0, padded - piece), (0, 0)))
    ffn_part = jnp.concatenate(
        [
            ffn_columns(w_gate),
            ffn_columns(w_up),
            from_lanes(to_lanes(down_part[None]), own)[0],
        ],
        axis=1,
    )
    ffn_part, w_in = tie((ffn_part, w_in))
    ffn_all = over_dp(ffn_part)
    both_own = ffn_all[:, : 2 * ffn_own]
    down_own = from_lanes(
        to_lanes(ffn_all[:, 2 * ffn_own :].reshape(shards, own, -1)), padded
    ).reshape(ffn_own, model)

    decay_part = mine(a_log, heads, 0)
    bias_part = mine(dt_bias, heads, 0)

    def odd_lanes(vector):
        spaced = jnp.stack([jnp.zeros_like(vector), vector], axis=1).reshape(-1)
        return jnp.pad(spaced, (0, LANES - 2 * heads))[None, :]

    coefficients = jnp.pad(
        jnp.concatenate([odd_lanes(bias_part), odd_lanes(-jnp.exp(decay_part))], axis=0),
        ((0, HALO - 2), (0, 0)),
    )
    gain = jnp.broadcast_to(head_gain.astype(wide)[None, :], (HALO, DV))
    place_row = place.astype(jnp.int32)[None]

    rows = own_tokens.astype(wide)
    inverse_one = row_norm(rows, first_gain)[1]
    normed_one = lower(row_norm(all_tokens.astype(wide), first_gain)[0])
    proj = lower(by_weight(normed_one, w_in))
    mixed, *kept = mixer_forward(
        heads, parts, place_row, proj, taps, coefficients, interpret
    )
    second_all, mixed = tie((second_all, mixed))
    w_gate_in = second_all[:, :values]
    out_part = jnp.swapaxes(
        second_all[:, values:].reshape(shards, own, out_ratio, quarter), 1, 2
    )
    w_out_own = jnp.swapaxes(
        exchange(out_part.reshape(parts, values, quarter)), 0, 1
    ).reshape(values, model)
    gated, out_gate = gate_rows(heads, mixed, normed_one, w_gate_in, gain, interpret)
    half = gated.shape[0] // 2
    mixed_far = by_weight(gated[half:], w_out_own)
    mixed_near = by_weight(gated[:half], w_out_own)
    after_mix = rows + scatter_seq(mixed_near, mixed_far)[0]
    normed_two, inverse_two = row_norm(after_mix, second_gain)
    normed_two = lower(normed_two)
    across = flip(normed_two, 2)
    normed_near = jnp.concatenate([normed_two, flip(normed_two, 1)], axis=0)
    pre_near = by_weight(normed_near, both_own)
    across, pre_near = tie((across, pre_near))
    normed_far = jnp.concatenate([across, flip(across, 1)], axis=0)

    def ffn_side(pre, cot_half):
        gate_pre = pre[:, :ffn_own]
        up_pre = pre[:, ffn_own:]
        sig_ffn = jax.nn.sigmoid(gate_pre)
        hidden = lower(gate_pre * sig_ffn * up_pre)
        grad_hidden = by_transpose(cot_half, down_own)
        grad_gate_pre = lower(
            grad_hidden * up_pre * sig_ffn * (1.0 + gate_pre * (1.0 - sig_ffn))
        )
        grad_up_pre = lower(grad_hidden * gate_pre * sig_ffn)
        grad_both = jnp.concatenate([grad_gate_pre, grad_up_pre], axis=1)
        return hidden, grad_both, by_transpose(grad_both, both_own)

    hidden_near, grad_near, back_near = ffn_side(pre_near, cot_near)
    hidden_far, grad_far, back_far = ffn_side(by_weight(normed_far, both_own), cot_far)
    grad_both = over_rows(normed_near, grad_near) + over_rows(normed_far, grad_far)
    grad_down = over_rows(hidden_near, cot_near) + over_rows(hidden_far, cot_far)
    grad_down = from_lanes(
        to_lanes(lower(grad_down).reshape(shards, padded, model)), own
    ).reshape(model, -1)
    grad_ffn = jnp.concatenate([lower(grad_both), grad_down], axis=1)
    grad_normed_two, grad_ffn = scatter_seq(back_near, back_far, grad_ffn)
    grad_ffn = sum_dp(grad_ffn)
    back_two, grad_norm_ffn = norm_back(after_mix, inverse_two, second_gain, grad_normed_two)
    grad_after = own_cot.astype(wide) + back_two
    grad_branch = jnp.concatenate(gather_seq(lower(grad_after)), axis=0)
    grad_branch, hidden_near, hidden_far = tie((grad_branch, hidden_near, hidden_far))
    grad_gated = by_transpose(grad_branch, w_out_own)
    grad_out = jnp.swapaxes(
        lower(over_rows(gated, grad_branch)).reshape(values, parts, quarter), 0, 1
    )
    grad_out = jnp.swapaxes(
        exchange(grad_out).reshape(shards, out_ratio, own, quarter), 1, 2
    ).reshape(model, -1)
    result = after_mix + scatter_seq(
        by_weight(hidden_near, down_own), by_weight(hidden_far, down_own)
    )[0]
    grad_in, grad_taps, grad_gain, grad_small = mixer_backward(
        heads, parts, place_row, proj, out_gate, taps, coefficients, gain, [mixed, *kept],
        grad_gated, interpret
    )
    grad_w_in = lower(over_rows(normed_one, grad_in))
    grad_in, grad_w_in = tie((grad_in, grad_w_in))
    grad_w_in = sum_dp(jnp.concatenate([grad_w_in, grad_out], axis=1))
    grad_first = grad_in[:, : width + LANES]
    grad_gate = grad_in[:, width + LANES :]
    one_far = by_transpose(grad_first[half:], w_in) + by_transpose(grad_gate[half:], w_gate_in)
    one_near = by_transpose(grad_first[:half], w_in) + by_transpose(
        grad_gate[:half], w_gate_in
    )
    back_one, grad_norm_attn = norm_back(
        rows, inverse_one, first_gain, scatter_seq(one_near, one_far)[0]
    )
    grad_rows = lower(grad_after + back_one)[:, None, :]

    taps_full = lax.dynamic_update_slice_in_dim(
        jnp.zeros((CONV, head_count * ROW), wide), grad_taps[:CONV], place * width, 1
    )

    def to_heads(lane_row):
        return lax.dynamic_update_slice_in_dim(
            jnp.zeros((head_count,), wide), lane_row[1 : 2 * heads : 2], place * heads, 0
        )

    common = jnp.concatenate([grad_gain[0], to_heads(grad_small[1]), to_heads(grad_small[0])])
    packed = jnp.concatenate(
        [grad_norm_attn, grad_norm_ffn, taps_full.reshape(-1), common]
    )
    packed_count = packed.shape[0]
    packed = jnp.pad(packed, (0, -packed_count % (HALO * LANES)))
    packed = sum_all(packed.reshape(-1, LANES)).reshape(-1)
    def pieces_of(array):
        stack = stack_seq(array)
        return [
            lax.dynamic_index_in_dim(stack, jnp.bitwise_xor(place, at), 0, keepdims=False)
            for at in range(parts)
        ]

    def side_by_side(pieces):
        return jnp.concatenate(pieces, axis=1).astype(wide)

    def ffn_full(pieces):
        split = jnp.stack(
            [item.reshape(own, shards, padded)[..., :piece] for item in pieces], axis=2
        )
        return split.reshape(own, -1).astype(wide)

    ffn_pieces = pieces_of(grad_ffn)
    grad_w_gate = ffn_full([item[:, :ffn_own] for item in ffn_pieces])
    grad_w_up = ffn_full([item[:, ffn_own : 2 * ffn_own] for item in ffn_pieces])
    grad_w_down = jnp.concatenate(
        [
            from_lanes(to_lanes(item[None, :, 2 * ffn_own :]), padded)[0][:piece]
            for item in ffn_pieces
        ],
        axis=0,
    ).astype(wide)
    early = (
        lower(result)[:, None, :],
        grad_rows,
        grad_w_gate,
        grad_w_up,
        grad_w_down,
        packed,
    )
    grad_w_in, early = tie((grad_w_in, early))
    block_out, grad_rows, grad_w_gate, grad_w_up, grad_w_down, packed = early
    taps_at = 2 * model
    gain_at = taps_at + CONV * head_count * ROW
    heads_at = gain_at + DV
    shard = lax.axis_index("dp")
    norm_attn_total = lax.dynamic_slice_in_dim(packed[:model], shard * own, own, 0)
    norm_ffn_total = lax.dynamic_slice_in_dim(packed[model:taps_at], shard * own, own, 0)
    own_taps = conv_w.shape[1]
    taps_total = lax.dynamic_slice_in_dim(
        packed[taps_at:gain_at].reshape(CONV, -1), shard * own_taps, own_taps, 1
    )

    in_pieces = pieces_of(grad_w_in)
    total = width + LANES + values
    return (
        block_out,
        grad_rows,
        norm_attn_total,
        side_by_side([item[:, :width] for item in in_pieces]),
        side_by_side([item[:, width : width + 2 * heads] for item in in_pieces]),
        taps_total,
        packed[heads_at : heads_at + head_count],
        packed[heads_at + head_count : heads_at + 2 * head_count],
        side_by_side([item[:, width + LANES : total] for item in in_pieces]),
        packed[gain_at:heads_at],
        side_by_side(
            [
                jnp.swapaxes(item[:, total:].reshape(own, out_ratio, quarter), 0, 1).reshape(
                    out_rows, quarter
                )
                for item in in_pieces
            ]
        ),
        norm_ffn_total,
        grad_w_gate,
        grad_w_up,
        grad_w_down,
    )


def solution(mesh):
    return jax.shard_map(
        per_device,
        mesh=mesh,
        in_specs=(
            P("seq", "dp", None),
            P("seq", "dp", None),
            P("dp"),
            P("dp", None),
            P("dp", None),
            P(None, "dp"),
            P(),
            P(),
            P("dp", None),
            P(),
            P("dp", None),
            P("dp"),
            P("dp", None),
            P("dp", None),
            P("dp", None),
        ),
        out_specs=(
            P("seq", "dp", None),
            P("seq", "dp", None),
            P("dp"),
            P("dp", None),
            P("dp", None),
            P(None, "dp"),
            P(),
            P(),
            P("dp", None),
            P(),
            P("dp", None),
            P("dp"),
            P("dp", None),
            P("dp", None),
            P("dp", None),
        ),
        check_vma=False,
    )
```

```python
import jax
import jax.numpy as jnp
from jax import lax
from jax.experimental import pallas as pl
from jax.experimental.pallas import tpu as pltpu
from jax.sharding import PartitionSpec as P

DK = 128
DV = 256
CONV = 4
ROW = 2 * DK + DV
LANES = 128
CHUNK = 256
HALO = 8

epsilon = 1e-06
narrow = jnp.bfloat16
wide = jnp.float32


def by_weight(left, right):
    return jnp.dot(left, right, preferred_element_type=wide)


def by_transpose(left, right):
    return lax.dot_general(
        left, right, (((1,), (1,)), ((), ())), preferred_element_type=wide
    )


def over_rows(left, right):
    return lax.dot_general(
        left, right, (((0,), (0,)), ((), ())), preferred_element_type=wide
    )


def row_norm(values, gain):
    inverse = lax.rsqrt(jnp.mean(values * values, axis=-1, keepdims=True) + epsilon)
    return (values * inverse * gain, inverse)


def norm_back(values, inverse, gain, grad_out):
    scaled = grad_out * gain
    grad_in = inverse * scaled - values * inverse * inverse * inverse * jnp.mean(
        scaled * values, axis=-1, keepdims=True
    )
    grad_gain = jnp.sum(grad_out * values * inverse, axis=tuple(range(values.ndim - 1)))
    return (grad_in, grad_gain)


def lower(array):
    return array.astype(narrow)


def row_sum(array):
    return jnp.sum(array, axis=1, keepdims=True)


def grid_indices():
    rows = lax.broadcasted_iota(jnp.int32, (CHUNK, CHUNK), 0)
    columns = lax.broadcasted_iota(jnp.int32, (CHUNK, CHUNK), 1)
    return rows, columns


def exact_dot(left, right):
    return jnp.dot(
        left, right, precision=lax.Precision.HIGHEST, preferred_element_type=wide
    )


def shifted_rows(rows, before):
    return jnp.concatenate([before, rows], axis=0)


def convolved(extended, taps, count):
    start = HALO - CONV + 1
    summed = extended[start : start + count] * taps[0:1]
    for offset in range(1, CONV):
        summed = summed + extended[start + offset : start + offset + count] * taps[
            offset : offset + 1
        ]
    return summed


def gates(rates, coefficients):
    strength = jax.nn.sigmoid(rates)
    shifted = rates + coefficients[0:1]
    decay = coefficients[1:2] * jax.nn.softplus(shifted)
    return strength, shifted, decay


def unit(values):
    return lax.rsqrt(row_sum(values * values) + epsilon)


def in_turn(parts):
    waiting = list(parts)
    while waiting:
        still = []
        for part in waiting:
            try:
                next(part)
                still.append(part)
            except StopIteration:
                pass
        waiting = still


def invert(lower_part, rows, columns, store):
    apart = jnp.bitwise_xor(rows, columns)
    inverse = jnp.where(rows == columns, 1.0, 0.0) - jnp.where(apart == 1, lower_part, 0.0)
    level = 1
    while (1 << level) < CHUNK:
        corner = lower(
            jnp.where(lax.shift_right_logical(apart, level) == 1, lower_part, 0.0)
        )
        held = lower(inverse)
        yield
        side = lower(by_weight(corner, held))
        yield
        inverse = inverse - by_weight(held, side)
        level += 1
    store.append(lower(inverse))


def forward_kernel(
    heads,
    place_ref,
    proj_ref,
    rates_ref,
    taps_ref,
    coef_ref,
    mixed_ref,
    inverse_ref,
    state_ref,
    corrected_ref,
    update_ref,
    weight_ref,
    before,
    state,
):
    @pl.when(pl.program_id(0) == 0)
    def _():
        before[...] = jnp.zeros_like(before)
        state[...] = jnp.zeros_like(state)

    count = proj_ref.shape[0]
    rows, columns = grid_indices()
    raw = proj_ref[...].astype(wide)
    summed = convolved(shifted_rows(raw, before[...]), taps_ref[...], count)
    before[...] = raw[count - HALO :]
    active = summed * jax.nn.sigmoid(summed)
    strength_rows, unused, decay_rows = gates(rates_ref[...].astype(wide), coef_ref[...])
    through = jnp.where(rows >= columns, 1.0, 0.0)
    states = {(0, head): state[head] for head in range(heads)}
    blocks = count // CHUNK
    cumulative_rows = [
        exact_dot(through, decay_rows[block * CHUNK : (block + 1) * CHUNK])
        for block in range(blocks)
    ]
    turned_rows = [item.T for item in cumulative_rows]

    def one(block, head):
        base = head * ROW
        here = slice(block * CHUNK, (block + 1) * CHUNK)
        query = active[here, base : base + DK]
        key = active[here, base + DK : base + 2 * DK]
        value = active[here, base + 2 * DK : base + ROW]
        query = query * (unit(query) * DK ** (-0.5))
        key = key * unit(key)
        strength = strength_rows[here, 2 * head : 2 * head + 1]
        cumulative = cumulative_rows[block][:, 2 * head + 1 : 2 * head + 2]
        across = turned_rows[block][2 * head + 1 : 2 * head + 2]
        final = cumulative[CHUNK - 1 :]
        fade = jnp.where(
            rows >= columns, jnp.exp(jnp.minimum(cumulative - across, 0.0)), 0.0
        )
        grown = jnp.exp(cumulative)
        key_low = lower(key)
        query_low = lower(query)
        dots = by_transpose(key_low, key_low)
        yield
        lower_part = jnp.where(rows > columns, strength * fade * dots, 0.0)
        store = []
        yield from invert(lower_part, rows, columns, store)
        inverse = store[0]
        yield
        update = by_weight(inverse, lower(strength * value))
        weight = lower(by_weight(inverse, lower(strength * grown * key)))
        inner = lower(by_transpose(query_low, key_low) * fade)
        faded = lower(key * jnp.exp(final - cumulative))
        inverse_ref[block, head] = inverse
        span = slice(head * DV, head * DV + DV)
        update_ref[here, span] = lower(update)
        weight_ref[here, head * DK : head * DK + DK] = weight
        yield
        while (block, head) not in states:
            yield
        held = states[block, head]
        held_low = lower(held)
        state_ref[block, head] = held_low
        corrected = lower(update - by_transpose(weight, held_low))
        yield
        states[block + 1, head] = held * jnp.exp(final) + over_rows(corrected, faded)
        corrected_ref[here, span] = corrected
        result = grown * by_transpose(query_low, held_low) + by_weight(inner, corrected)
        yield
        mixed_ref[here, span] = lower(result)

    in_turn(one(block, head) for block in range(blocks) for head in range(heads))
    for head in range(heads):
        state[head] = states[blocks, head]


def on_piece(pieces, body):
    for at, piece in enumerate(pieces):

        @pl.when(pl.program_id(0) == at)
        def _(at=at, piece=piece):
            body(at, piece)


def entry_kernel(count, *refs):
    weight_ref, gain_ref, normed_ref, proj_ref = refs[count:]

    def body(at, piece):
        normed = lower(row_norm(piece[...].astype(wide), gain_ref[0:1])[0])
        normed_ref[...] = normed
        proj_ref[...] = lower(by_weight(normed, weight_ref[...]))

    on_piece(refs[:count], body)


def gate_kernel(
    heads, mixed_ref, normed_ref, weight_ref, gain_ref, out_ref, gated_ref, gate_ref, *partials
):
    gate = by_weight(normed_ref[...], weight_ref[...])
    gate_ref[...] = gate
    gain = gain_ref[0:1]
    for head in range(heads):
        span = slice(head * DV, head * DV + DV)
        normed = row_norm(mixed_ref[:, span].astype(wide), gain)[0]
        here = gate[:, span]
        gated_ref[:, span] = lower(normed * (here * jax.nn.sigmoid(here)))
    partial = lower(by_weight(gated_ref[...], out_ref[...]))

    def body(at, piece):
        piece[...] = partial

    on_piece(partials, body)


def ffn_kernel(count, *refs):
    normed_pieces, cot_pieces = refs[:count], refs[count : 2 * count]
    both_ref, down_ref, normed_ref, cot_ref, hidden_ref, grad_ref = refs[
        2 * count : 2 * count + 6
    ]
    backs = refs[2 * count + 6 :]
    units = down_ref.shape[0]

    def body(at, piece):
        normed = piece[...]
        cot = cot_pieces[at][...]
        normed_ref[...] = normed
        cot_ref[...] = cot
        gate_pre = by_weight(normed, both_ref[:, :units])
        up_pre = by_weight(normed, both_ref[:, units:])
        sig = jax.nn.sigmoid(gate_pre)
        silu = gate_pre * sig
        hidden_ref[...] = lower(silu * up_pre)
        grad_hidden = by_transpose(cot, down_ref[...])
        grad_ref[:, :units] = lower(
            grad_hidden * up_pre * sig * (1.0 + gate_pre * (1.0 - sig))
        )
        grad_ref[:, units:] = lower(grad_hidden * silu)
        backs[at][...] = lower(by_transpose(grad_ref[...], both_ref[...]))

    on_piece(normed_pieces, body)


def branch_kernel(count, *refs):
    weight_ref, branch_ref, grad_ref = refs[count:]

    def body(at, piece):
        branch_ref[...] = piece[...]
        grad_ref[...] = by_transpose(piece[...], weight_ref[...])

    on_piece(refs[:count], body)


def backward_kernel(
    heads,
    place_ref,
    proj_ref,
    edge_ref,
    rates_ref,
    gate_ref,
    taps_ref,
    coef_ref,
    gain_ref,
    mixed_ref,
    inverse_ref,
    state_ref,
    corrected_ref,
    update_ref,
    weight_ref,
    grad_ref,
    out_ref,
    taps_grad_ref,
    gain_grad_ref,
    small_grad_ref,
    after,
    state_grad,
):
    step = pl.program_id(0)

    @pl.when(step == 0)
    def _():
        after[...] = jnp.zeros_like(after)
        state_grad[...] = jnp.zeros_like(state_grad)
        taps_grad_ref[...] = jnp.zeros_like(taps_grad_ref)
        gain_grad_ref[...] = jnp.zeros_like(gain_grad_ref)
        small_grad_ref[...] = jnp.zeros_like(small_grad_ref)

    count = proj_ref.shape[0]
    blocks = count // CHUNK
    rows, columns = grid_indices()
    lanes = lax.broadcasted_iota(jnp.int32, (CHUNK, LANES), 1)
    raw = proj_ref[...].astype(wide)
    edge = edge_ref[edge_ref.shape[0] - HALO :].astype(wide)
    edge = jnp.where(step == pl.num_programs(0) - 1, 0.0, edge)
    taps = taps_ref[...]
    extended = shifted_rows(raw, edge)
    summed = convolved(extended, taps, count)
    sig = jax.nn.sigmoid(summed)
    active = summed * sig
    coefficients = coef_ref[...]
    strength_rows, shifted_rates, decay_rows = gates(
        rates_ref[...].astype(wide), coefficients
    )
    through = jnp.where(rows >= columns, 1.0, 0.0)
    onward = jnp.where(columns >= rows, 1.0, 0.0)
    gain = gain_ref[0:1]
    proj_width = heads * ROW
    cumulative_rows = [
        exact_dot(through, decay_rows[block * CHUNK : (block + 1) * CHUNK])
        for block in range(blocks)
    ]
    turned_rows = [item.T for item in cumulative_rows]
    laters = {(blocks - 1, head): state_grad[head] for head in range(heads)}
    active_grads = {}
    column_grads = {}
    gain_grads = []

    def one(block, head):
        here = slice(block * CHUNK, (block + 1) * CHUNK)
        span = slice(head * DV, head * DV + DV)
        grad_gated = grad_ref[here, span].astype(wide)
        mixed = mixed_ref[here, span].astype(wide)
        normed, head_inverse = row_norm(mixed, gain)
        gate = gate_ref[here, span]
        sig_gate = jax.nn.sigmoid(gate)
        gate_start = proj_width + LANES + head * DV
        out_ref[here, gate_start : gate_start + DV] = lower(
            grad_gated * normed * sig_gate * (1.0 + gate * (1.0 - sig_gate))
        )
        normed_grad = grad_gated * (gate * sig_gate)
        scaled = normed_grad * gain
        grad_mixed = lower(
            head_inverse * scaled
            - mixed
            * (head_inverse * head_inverse * head_inverse)
            * jnp.mean(scaled * mixed, axis=-1, keepdims=True)
        )
        gain_grads.append(
            jnp.sum(normed_grad * mixed * head_inverse, axis=0, keepdims=True)
        )
        base = head * ROW
        query_raw = active[here, base : base + DK]
        key_raw = active[here, base + DK : base + 2 * DK]
        value = active[here, base + 2 * DK : base + ROW]
        query_unit = unit(query_raw)
        key_unit = unit(key_raw)
        query = query_raw * (query_unit * DK ** (-0.5))
        key = key_raw * key_unit
        strength = strength_rows[here, 2 * head : 2 * head + 1]
        cumulative = cumulative_rows[block][:, 2 * head + 1 : 2 * head + 2]
        across = turned_rows[block][2 * head + 1 : 2 * head + 2]
        final = cumulative[CHUNK - 1 :]
        fade = jnp.where(
            rows >= columns, jnp.exp(jnp.minimum(cumulative - across, 0.0)), 0.0
        )
        strict_fade = jnp.where(rows > columns, fade, 0.0)
        grown = jnp.exp(cumulative)
        remaining = jnp.exp(final - cumulative)
        kept = jnp.exp(final)
        key_low = lower(key)
        query_low = lower(query)
        yield
        dots = by_transpose(key_low, key_low)
        cross = by_transpose(query_low, key_low)
        held = state_ref[block, head]
        corrected = corrected_ref[here, span]
        weight = weight_ref[here, head * DK : head * DK + DK]
        faded = key * remaining
        faded_low = lower(faded)
        grown_query = query * grown
        yield
        inner_side = over_rows(lower(cross * fade), grad_mixed)
        state_side = over_rows(grad_mixed, lower(grown_query))
        dot_grad = by_transpose(grad_mixed, corrected) * fade
        dot_grad_low = lower(dot_grad)
        grown_grad = by_weight(grad_mixed, held)
        yield
        while (block, head) not in laters:
            yield
        later = laters[block, head]
        later_low = lower(later)
        corrected_grad_low = lower(inner_side + by_transpose(faded_low, later_low))
        yield
        laters[block - 1, head] = (
            later * kept + state_side - over_rows(corrected_grad_low, weight)
        )
        faded_grad = by_weight(corrected, later_low)
        weight_grad = lower(-by_weight(corrected_grad_low, held))
        inverse = inverse_ref[block, head]
        yield
        value_side = over_rows(inverse, corrected_grad_low)
        key_side = over_rows(inverse, weight_grad)
        yield
        lower_grad = -(
            by_transpose(lower(value_side), update_ref[here, span])
            + by_transpose(lower(key_side), weight)
        ) * strict_fade
        inner_query = by_weight(dot_grad_low, key_low)
        inner_key = over_rows(dot_grad_low, query_low)
        yield
        lower_grad_low = lower(lower_grad)
        first_key = by_weight(lower_grad_low, key_low)
        second_key = over_rows(lower_grad_low, lower(strength * key))
        pairs = lower_grad * dots
        both = pairs * strength + dot_grad * cross
        faded_sum = row_sum(faded_grad * faded)
        key_sum = row_sum(key_side * key)
        yield
        query_grad = grown * grown_grad + inner_query
        key_grad = (
            (strength * grown) * key_side
            + strength * first_key
            + second_key
            + inner_key
            + remaining * faded_grad
        )
        head_strength_grad = row_sum(value_side * value) + grown * key_sum + row_sum(pairs)
        head_spread = (
            (strength * grown) * key_sum
            + row_sum(both)
            + row_sum(grown_grad * grown_query)
            - faded_sum
        )
        column_total = jnp.sum(both, axis=0, keepdims=True)
        late_total = row_sum(jnp.where(columns >= rows, column_total, 0.0))
        final_grad = kept * jnp.sum(held.astype(wide) * later, keepdims=True) + jnp.sum(
            faded_sum, axis=0, keepdims=True
        )
        column_grads[block, head] = (
            head_strength_grad,
            head_spread,
            final_grad - late_total,
        )
        active_grads[block, head] = (
            DK ** (-0.5)
            * query_unit
            * (
                query_grad
                - query_raw * (query_unit * query_unit) * row_sum(query_grad * query_raw)
            ),
            key_unit
            * (key_grad - key_raw * (key_unit * key_unit) * row_sum(key_grad * key_raw)),
            strength * value_side,
        )

    in_turn(
        one(block, head) for block in reversed(range(blocks)) for head in range(heads)
    )
    for head in range(heads):
        state_grad[head] = laters[-1, head]
    for block in range(blocks):
        here = slice(block * CHUNK, (block + 1) * CHUNK)
        strength_grad = jnp.zeros((CHUNK, LANES), wide)
        spread_grad = jnp.zeros((CHUNK, LANES), wide)
        extra_grad = jnp.zeros((CHUNK, LANES), wide)
        for head in range(heads):
            first, second, third = column_grads[block, head]
            strength_grad = jnp.where(lanes == 2 * head, first, strength_grad)
            spread_grad = jnp.where(lanes == 2 * head + 1, second, spread_grad)
            extra_grad = jnp.where(lanes == 2 * head + 1, third, extra_grad)
        decay_grad = exact_dot(onward, spread_grad) + extra_grad
        shift_grad = decay_grad * coefficients[1:2] * jax.nn.sigmoid(shifted_rates[here])
        strength_here = strength_rows[here]
        rates_grad = strength_grad * strength_here * (1.0 - strength_here) + shift_grad
        out_ref[here, proj_width : proj_width + LANES] = lower(rates_grad)
        small_grad_ref[0:1] += jnp.sum(shift_grad, axis=0, keepdims=True)
        small_grad_ref[1:2] += jnp.sum(decay_grad * decay_rows[here], axis=0, keepdims=True)
    gain_grad_ref[0:1] += sum(gain_grads)
    joined = jnp.concatenate(
        [
            jnp.concatenate(
                [part for head in range(heads) for part in active_grads[block, head]], axis=1
            )
            for block in range(blocks)
        ],
        axis=0,
    )
    summed_grad = joined * (sig * (1.0 + summed * (1.0 - sig)))
    following = jnp.concatenate([summed_grad, after[...]], axis=0)
    after[...] = summed_grad[:HALO]
    proj_grad = following[CONV - 1 : CONV - 1 + count] * taps[0:1]
    start = HALO - CONV + 1
    for offset in range(CONV):
        if offset:
            shift = CONV - 1 - offset
            proj_grad = proj_grad + following[shift : shift + count] * taps[offset : offset + 1]
        taps_grad_ref[offset : offset + 1] += jnp.sum(
            summed_grad * extended[start + offset : start + offset + count],
            axis=0,
            keepdims=True,
        )
    out_ref[:, :proj_width] = lower(proj_grad)


def params():
    return pltpu.CompilerParams(
        dimension_semantics=("arbitrary",), vmem_limit_bytes=52 * 1024 * 1024
    )


def effort(length, heads, each=10000000):
    return pl.CostEstimate(
        flops=length * heads * each,
        bytes_accessed=length * heads * 1024,
        transcendentals=length * heads,
    )


def mixer_forward(heads, parts, place, proj, taps, coefficients, interpret=False):
    length = proj.shape[0]
    count = length // parts
    blocks = count // CHUNK
    width = heads * ROW
    values = heads * DV

    def tall(columns, at=0):
        return pl.BlockSpec((count, columns), lambda i, me: (jnp.bitwise_xor(i, me[0]), at))

    def whole(array):
        return pl.BlockSpec(array.shape, lambda i, me: (0,) * array.ndim)

    def stacked(first, second):
        return pl.BlockSpec((blocks, heads, first, second), lambda i, me: (i, 0, 0, 0))

    chunks = parts * blocks
    return pl.pallas_call(
        lambda *refs: forward_kernel(heads, *refs),
        grid_spec=pltpu.PrefetchScalarGridSpec(
            num_scalar_prefetch=1,
            grid=(parts,),
            in_specs=[
                tall(width),
                tall(LANES, width // LANES),
                whole(taps),
                whole(coefficients),
            ],
            out_specs=[
                tall(values),
                stacked(CHUNK, CHUNK),
                stacked(DV, DK),
                tall(values),
                tall(values),
                tall(heads * DK),
            ],
            scratch_shapes=[
                pltpu.VMEM((HALO, width), wide),
                pltpu.VMEM((heads, DV, DK), wide),
            ],
        ),
        out_shape=[
            jax.ShapeDtypeStruct((length, values), narrow),
            jax.ShapeDtypeStruct((chunks, heads, CHUNK, CHUNK), narrow),
            jax.ShapeDtypeStruct((chunks, heads, DV, DK), narrow),
            jax.ShapeDtypeStruct((length, values), narrow),
            jax.ShapeDtypeStruct((length, values), narrow),
            jax.ShapeDtypeStruct((length, heads * DK), narrow),
        ],
        compiler_params=params(),
        cost_estimate=effort(length, heads),
        interpret=interpret,
    )(place, proj, proj, taps, coefficients)


def fixed(shape):
    return pl.BlockSpec(shape, lambda i: (0,) * len(shape))


def rows_of(rows, columns):
    return pl.BlockSpec((rows, columns), lambda i: (i, 0))


def shape_of(rows, columns, kind=narrow):
    return jax.ShapeDtypeStruct((rows, columns), kind)


def row_call(kernel, steps, in_specs, out_specs, out_shape, flops, interpret):
    return pl.pallas_call(
        kernel,
        grid=(steps,),
        in_specs=in_specs,
        out_specs=out_specs,
        out_shape=out_shape,
        compiler_params=params(),
        cost_estimate=pl.CostEstimate(
            flops=flops, bytes_accessed=flops // 1024, transcendentals=0
        ),
        interpret=interpret,
    )


def enter(pieces, weight, gain, interpret):
    steps = len(pieces)
    rows, model = pieces[0].shape
    width = weight.shape[1]
    return row_call(
        lambda *refs: entry_kernel(steps, *refs),
        steps,
        [fixed(item.shape) for item in (*pieces, weight, gain)],
        [rows_of(rows, model), rows_of(rows, width)],
        [shape_of(steps * rows, model), shape_of(steps * rows, width)],
        2 * steps * rows * model * width,
        interpret,
    )(*pieces, weight, gain)


def gate_rows(heads, steps, mixed, normed, weight, gain, w_out, interpret):
    length, values = mixed.shape
    model = normed.shape[1]
    rows = length // steps
    return row_call(
        lambda *refs: gate_kernel(heads, *refs),
        steps,
        [
            rows_of(rows, values),
            rows_of(rows, model),
            fixed(weight.shape),
            fixed(gain.shape),
            fixed(w_out.shape),
        ],
        [rows_of(rows, values), rows_of(rows, values)] + [fixed((rows, model))] * steps,
        [shape_of(length, values), shape_of(length, values, wide)]
        + [shape_of(rows, model)] * steps,
        4 * length * model * values,
        interpret,
    )(mixed, normed, weight, gain, w_out)


def ffn_rows(normed_pieces, cot_pieces, both, down, interpret):
    steps = len(normed_pieces)
    rows, model = normed_pieces[0].shape
    units = down.shape[0]
    length = steps * rows
    return row_call(
        lambda *refs: ffn_kernel(steps, *refs),
        steps,
        [fixed(item.shape) for item in (*normed_pieces, *cot_pieces, both, down)],
        [
            rows_of(rows, model),
            rows_of(rows, model),
            rows_of(rows, units),
            rows_of(rows, 2 * units),
        ]
        + [fixed((rows, model))] * steps,
        [
            shape_of(length, model),
            shape_of(length, model),
            shape_of(length, units),
            shape_of(length, 2 * units),
        ]
        + [shape_of(rows, model)] * steps,
        10 * length * model * units,
        interpret,
    )(*normed_pieces, *cot_pieces, both, down)


def branch_rows(pieces, weight, interpret):
    steps = len(pieces)
    rows, model = pieces[0].shape
    values = weight.shape[0]
    return row_call(
        lambda *refs: branch_kernel(steps, *refs),
        steps,
        [fixed(item.shape) for item in (*pieces, weight)],
        [rows_of(rows, model), rows_of(rows, values)],
        [shape_of(steps * rows, model), shape_of(steps * rows, values, wide)],
        2 * steps * rows * model * values,
        interpret,
    )(*pieces, weight)


def mixer_backward(
    heads, parts, place, proj, gate, taps, coefficients, gain, kept, grad_gated, interpret=False
):
    length = proj.shape[0]
    count = length // parts
    blocks = count // CHUNK
    width = heads * ROW
    values = heads * DV
    edge_rows = 2 * HALO
    ratio = count // edge_rows

    def tall(columns, at=0):
        return pl.BlockSpec(
            (count, columns), lambda i, me: (jnp.bitwise_xor(parts - 1 - i, me[0]), at)
        )

    def edge_at(i, me):
        previous = jnp.bitwise_xor(jnp.maximum(parts - 2 - i, 0), me[0])
        return (previous * ratio + ratio - 1, 0)

    def whole(shape):
        return pl.BlockSpec(shape, lambda i, me: (0,) * len(shape))

    def stacked(first, second):
        return pl.BlockSpec(
            (blocks, heads, first, second), lambda i, me: (parts - 1 - i, 0, 0, 0)
        )

    total = width + LANES + values
    return pl.pallas_call(
        lambda *refs: backward_kernel(heads, *refs),
        grid_spec=pltpu.PrefetchScalarGridSpec(
            num_scalar_prefetch=1,
            grid=(parts,),
            in_specs=[
                tall(width),
                pl.BlockSpec((edge_rows, width), edge_at),
                tall(LANES, width // LANES),
                tall(values),
                whole(taps.shape),
                whole(coefficients.shape),
                whole(gain.shape),
                tall(values),
                stacked(CHUNK, CHUNK),
                stacked(DV, DK),
                tall(values),
                tall(values),
                tall(heads * DK),
                tall(values),
            ],
            out_specs=[
                tall(total),
                whole((HALO, width)),
                whole((HALO, DV)),
                whole((HALO, LANES)),
            ],
            scratch_shapes=[
                pltpu.VMEM((HALO, width), wide),
                pltpu.VMEM((heads, DV, DK), wide),
            ],
        ),
        out_shape=[
            jax.ShapeDtypeStruct((length, total), narrow),
            jax.ShapeDtypeStruct((HALO, width), wide),
            jax.ShapeDtypeStruct((HALO, DV), wide),
            jax.ShapeDtypeStruct((HALO, LANES), wide),
        ],
        compiler_params=params(),
        cost_estimate=effort(length, heads, 100000),
        interpret=interpret,
    )(place, proj, proj, proj, gate, taps, coefficients, gain, *kept, grad_gated)


def to_lanes(array):
    groups, rows, columns = array.shape
    split = array.reshape(groups, rows, columns // LANES, LANES)
    return jnp.swapaxes(split, 1, 2).reshape(groups, -1, LANES)


def from_lanes(array, rows):
    groups = array.shape[0]
    split = array.reshape(groups, -1, rows, LANES)
    return jnp.swapaxes(split, 1, 2).reshape(groups, rows, -1)


def per_device(
    tokens,
    cotangent,
    norm_attn,
    w_qkv,
    w_ba,
    conv_w,
    a_log,
    dt_bias,
    w_outgate,
    head_gain,
    w_out,
    norm_ffn,
    w_gate,
    w_up,
    w_down,
    interpret=False,
):
    parts = lax.axis_size("seq")
    shards = lax.axis_size("dp")
    place = lax.axis_index("seq")
    head_count = a_log.shape[0]
    heads = head_count // parts
    width = heads * ROW
    values = heads * DV
    model = tokens.shape[2]
    own = norm_attn.shape[0]
    out_rows = w_out.shape[0]
    quarter = model // parts

    def mine(array, size, axis):
        return lax.dynamic_slice_in_dim(array, place * size, size, axis)

    tie = lax.optimization_barrier

    def flip(array, bit):
        return lax.ppermute(array, "seq", [(i, i ^ bit) for i in range(parts)])

    def over_dp(array):
        return lax.all_gather(array, "dp", axis=0, tiled=True)

    def sum_dp(array):
        return lax.psum_scatter(array, "dp", scatter_dimension=0, tiled=True)

    def gather_seq(array):
        across = flip(array, 2)
        return [array, flip(array, 1), across, flip(across, 1)]

    def scatter_seq(pieces, beside=None):
        own_piece, sibling, across, corner = pieces
        across = across.astype(wide) + flip(lower(corner), 1).astype(wide)
        across = flip(lower(across), 2)
        sibling = flip(lower(sibling), 1)
        if beside is not None:
            across, beside = tie((across, beside))
        total = own_piece.astype(wide) + sibling.astype(wide) + across.astype(wide)
        return (total, beside)

    def gather_dp(array):
        shard = lax.axis_index("dp")
        stack = array[None]
        bits = shards.bit_length() - 1
        done = bits // 2
        for low, high in ((done, bits), (0, done)):
            size = 1 << (high - low)
            pieces = [stack] + [
                lax.ppermute(stack, "dp", [(i, i ^ (at << low)) for i in range(shards)])
                for at in range(1, size)
            ]
            for bit in range(high - low):
                upper = jnp.bitwise_and(shard, 1 << (low + bit)) != 0
                pieces = [
                    jnp.where(upper, pieces[at ^ (1 << bit)], pieces[at])
                    for at in range(size)
                ]
            stack = jnp.stack(pieces, axis=1).reshape((-1,) + array.shape)
        return stack

    def scatter_direct(pieces):
        total = pieces[0].astype(wide)
        for bit in range(1, parts):
            total = total + flip(lower(pieces[bit]), bit).astype(wide)
        return total

    def sum_all(array):
        for bit in range(1, parts):
            if bit & (bit - 1) == 0:
                array = array + flip(array, bit)
        bit = 1
        while bit < shards:
            array = array + lax.ppermute(array, "dp", [(i, i ^ bit) for i in range(shards)])
            bit *= 2
        return array

    def absolute(stack):
        return jnp.concatenate(
            [
                lax.dynamic_index_in_dim(stack, jnp.bitwise_xor(place, at), 0)
                for at in range(parts)
            ],
            axis=0,
        )

    def exchange(stack):
        pieces = [
            lax.dynamic_index_in_dim(stack, jnp.bitwise_xor(place, at), 0)
            for at in range(parts)
        ]
        return absolute(
            jnp.concatenate(
                [pieces[0]] + [flip(pieces[at], at) for at in range(1, parts)], axis=0
            )
        )

    ffn = w_gate.shape[1]
    piece = ffn // (shards * parts)
    ffn_own = -(-(piece * shards) // LANES) * LANES
    padded = ffn_own // shards

    def ffn_columns(array):
        split = array.reshape(own, shards, parts, piece)
        split = lax.dynamic_index_in_dim(split, place, 2, keepdims=False)
        split = jnp.pad(split, ((0, 0), (0, 0), (0, padded - piece)))
        return split.reshape(own, ffn_own)

    own_tokens = tokens[:, 0, :]
    own_cot = cotangent[:, 0, :]
    small_flat = jnp.concatenate([norm_attn, norm_ffn, conv_w.reshape(-1)])
    small_count = small_flat.shape[0]
    half_lanes = LANES // 2
    small_flat = jnp.pad(small_flat, (0, own * half_lanes - small_count))
    w_in = over_dp(
        jnp.concatenate(
            [
                mine(w_qkv, width, 1),
                jnp.pad(mine(w_ba, 2 * heads, 1), ((0, 0), (0, half_lanes - 2 * heads))),
                small_flat.reshape(own, half_lanes),
            ],
            axis=1,
        )
    )
    token_pieces = gather_seq(own_tokens)
    out_ratio = out_rows // own
    second_all = gather_dp(
        jnp.concatenate(
            [
                mine(w_outgate, values, 1),
                jnp.swapaxes(
                    mine(w_out, quarter, 1).reshape(out_ratio, own, quarter), 0, 1
                ).reshape(own, -1),
            ],
            axis=1,
        )
    )
    w_gate_in = second_all[:, :, :values].reshape(model, values)
    out_part = jnp.swapaxes(
        second_all[:, :, values:].reshape(shards, own, out_ratio, quarter), 1, 2
    )
    small_all = w_in[:, width + half_lanes :].reshape(shards, -1)[:, :small_count]
    first_gain = small_all[:, :own].reshape(-1).astype(wide)
    second_gain = small_all[:, own : 2 * own].reshape(-1).astype(wide)
    taps_all = jnp.swapaxes(small_all[:, 2 * own :].reshape(shards, CONV, -1), 0, 1)
    taps = mine(taps_all.reshape(CONV, -1), width, 1).astype(wide)
    taps = jnp.pad(taps, ((0, HALO - CONV), (0, 0)))

    down_part = jnp.pad(mine(w_down, piece, 0), ((0, padded - piece), (0, 0)))
    ffn_part = jnp.concatenate(
        [
            ffn_columns(w_gate),
            ffn_columns(w_up),
            from_lanes(to_lanes(down_part[None]), own)[0],
        ],
        axis=1,
    )
    ffn_part, w_in = tie((ffn_part, w_in))
    ffn_all = over_dp(ffn_part)
    both_own = ffn_all[:, : 2 * ffn_own]
    down_own = from_lanes(
        to_lanes(ffn_all[:, 2 * ffn_own :].reshape(shards, own, -1)), padded
    ).reshape(ffn_own, model)

    decay_part = mine(a_log, heads, 0)
    bias_part = mine(dt_bias, heads, 0)

    def odd_lanes(vector):
        spaced = jnp.stack([jnp.zeros_like(vector), vector], axis=1).reshape(-1)
        return jnp.pad(spaced, (0, LANES - 2 * heads))[None, :]

    coefficients = jnp.pad(
        jnp.concatenate([odd_lanes(bias_part), odd_lanes(-jnp.exp(decay_part))], axis=0),
        ((0, HALO - 2), (0, 0)),
    )
    gain = jnp.broadcast_to(head_gain.astype(wide)[None, :], (HALO, DV))
    place_row = place.astype(jnp.int32)[None]

    first_rows = jnp.broadcast_to(first_gain[None, :], (HALO, model))
    w_in, first_rows, *token_pieces = tie((w_in, first_rows, *token_pieces))
    normed_one, proj = enter(token_pieces, w_in, first_rows, interpret)
    mixed, *kept = mixer_forward(
        heads, parts, place_row, proj, taps, coefficients, interpret
    )
    mixed, *cot_pieces = tie((mixed, *gather_seq(own_cot)))
    w_out_own = jnp.swapaxes(
        exchange(out_part.reshape(parts, values, quarter)), 0, 1
    ).reshape(values, model)
    gated, out_gate, *mixed_pieces = gate_rows(
        heads, parts, mixed, normed_one, w_gate_in, gain, w_out_own, interpret
    )
    rows = own_tokens.astype(wide)
    inverse_one = row_norm(rows, first_gain)[1]
    after_mix = rows + scatter_seq(mixed_pieces)[0]
    normed_two, inverse_two = row_norm(after_mix, second_gain)
    normed_two, both_own, down_own = tie((lower(normed_two), both_own, down_own))
    across = flip(normed_two, 2)
    beside = flip(normed_two, 1)
    half = parts // 2
    normed_near, cot_near, hidden_near, grad_near, *back_near = ffn_rows(
        [normed_two, beside], cot_pieces[:half], both_own, down_own, interpret
    )
    normed_far, cot_far, hidden_far, grad_far, *back_far = ffn_rows(
        [across, flip(across, 1)], cot_pieces[half:], both_own, down_own, interpret
    )
    grad_both = over_rows(normed_near, grad_near) + over_rows(normed_far, grad_far)
    grad_down = over_rows(hidden_near, cot_near) + over_rows(hidden_far, cot_far)
    grad_down = from_lanes(
        to_lanes(lower(grad_down).reshape(shards, padded, model)), own
    ).reshape(model, -1)
    grad_ffn = jnp.concatenate([lower(grad_both), grad_down], axis=1)
    grad_normed_two, grad_ffn = scatter_seq(back_near + back_far, grad_ffn)
    grad_ffn = sum_dp(grad_ffn)
    back_two, grad_norm_ffn = norm_back(after_mix, inverse_two, second_gain, grad_normed_two)
    grad_after = own_cot.astype(wide) + back_two
    branch_pieces = gather_seq(lower(grad_after))
    down_near = lower(by_weight(hidden_near, down_own))
    down_far = lower(by_weight(hidden_far, down_own))
    down_near, down_far, *branch_pieces = tie((down_near, down_far, *branch_pieces))
    grad_branch, grad_gated = branch_rows(branch_pieces, w_out_own, interpret)
    grad_out = jnp.swapaxes(
        lower(over_rows(gated, grad_branch)).reshape(values, parts, quarter), 0, 1
    )
    grad_out = jnp.swapaxes(
        exchange(grad_out).reshape(shards, out_ratio, own, quarter), 1, 2
    ).reshape(model, -1)
    count = own_tokens.shape[0]
    result = after_mix + scatter_seq(
        [down_near[:count], down_near[count:], down_far[:count], down_far[count:]]
    )[0]
    grad_in, grad_taps, grad_gain, grad_small = mixer_backward(
        heads, parts, place_row, proj, out_gate, taps, coefficients, gain, [mixed, *kept],
        grad_gated, interpret
    )
    grad_w_in = jnp.concatenate([lower(over_rows(normed_one, grad_in)), grad_out], axis=1)
    grad_in, grad_w_in = tie((grad_in, grad_w_in))
    grad_w_in = sum_dp(grad_w_in)
    grad_first = grad_in[:, : width + LANES]
    grad_gate = grad_in[:, width + LANES :]
    one_far, one_near = (
        by_transpose(grad_first[span], w_in) + by_transpose(grad_gate[span], w_gate_in)
        for span in (slice(2 * count, None), slice(0, 2 * count))
    )
    back_one, grad_norm_attn = norm_back(
        rows,
        inverse_one,
        first_gain,
        scatter_direct([one_near[:count], one_near[count:], one_far[:count], one_far[count:]]),
    )
    grad_rows = lower(grad_after + back_one)[:, None, :]

    taps_full = lax.dynamic_update_slice_in_dim(
        jnp.zeros((CONV, head_count * ROW), wide), grad_taps[:CONV], place * width, 1
    )

    def to_heads(lane_row):
        return lax.dynamic_update_slice_in_dim(
            jnp.zeros((head_count,), wide), lane_row[1 : 2 * heads : 2], place * heads, 0
        )

    common = jnp.concatenate([grad_gain[0], to_heads(grad_small[1]), to_heads(grad_small[0])])
    packed = jnp.concatenate(
        [grad_norm_attn, grad_norm_ffn, taps_full.reshape(-1), common]
    )
    packed_count = packed.shape[0]
    packed = jnp.pad(packed, (0, -packed_count % (HALO * LANES)))
    def pieces_of(array):
        near = gather_seq(array)
        low_bit = jnp.bitwise_and(place, 1) != 0
        high_bit = jnp.bitwise_and(place, 2) != 0
        return [
            jnp.where(
                high_bit,
                jnp.where(low_bit, near[at ^ 3], near[at ^ 2]),
                jnp.where(low_bit, near[at ^ 1], near[at]),
            )
            for at in range(parts)
        ]

    def side_by_side(pieces):
        return jnp.concatenate(pieces, axis=1).astype(wide)

    def ffn_full(pieces):
        split = jnp.stack(
            [item.reshape(own, shards, padded)[..., :piece] for item in pieces], axis=2
        )
        return split.reshape(own, -1).astype(wide)

    ffn_pieces = pieces_of(grad_ffn)
    grad_w_gate = ffn_full([item[:, :ffn_own] for item in ffn_pieces])
    grad_w_up = ffn_full([item[:, ffn_own : 2 * ffn_own] for item in ffn_pieces])
    grad_w_down = jnp.concatenate(
        [
            from_lanes(to_lanes(item[None, :, 2 * ffn_own :]), padded)[0][:piece]
            for item in ffn_pieces
        ],
        axis=0,
    ).astype(wide)
    early = (
        lower(result)[:, None, :],
        grad_rows,
        grad_w_gate,
        grad_w_up,
        grad_w_down,
        packed,
    )
    grad_w_in, early = tie((grad_w_in, early))
    block_out, grad_rows, grad_w_gate, grad_w_up, grad_w_down, packed = early
    packed = sum_all(packed.reshape(-1, LANES)).reshape(-1)
    taps_at = 2 * model
    gain_at = taps_at + CONV * head_count * ROW
    heads_at = gain_at + DV
    shard = lax.axis_index("dp")
    norm_attn_total = lax.dynamic_slice_in_dim(packed[:model], shard * own, own, 0)
    norm_ffn_total = lax.dynamic_slice_in_dim(packed[model:taps_at], shard * own, own, 0)
    own_taps = conv_w.shape[1]
    taps_total = lax.dynamic_slice_in_dim(
        packed[taps_at:gain_at].reshape(CONV, -1), shard * own_taps, own_taps, 1
    )

    in_pieces = pieces_of(grad_w_in)
    total = width + LANES + values
    return (
        block_out,
        grad_rows,
        norm_attn_total,
        side_by_side([item[:, :width] for item in in_pieces]),
        side_by_side([item[:, width : width + 2 * heads] for item in in_pieces]),
        taps_total,
        packed[heads_at : heads_at + head_count],
        packed[heads_at + head_count : heads_at + 2 * head_count],
        side_by_side([item[:, width + LANES : total] for item in in_pieces]),
        packed[gain_at:heads_at],
        side_by_side(
            [
                jnp.swapaxes(item[:, total:].reshape(own, out_ratio, quarter), 0, 1).reshape(
                    out_rows, quarter
                )
                for item in in_pieces
            ]
        ),
        norm_ffn_total,
        grad_w_gate,
        grad_w_up,
        grad_w_down,
    )


def solution(mesh):
    return jax.shard_map(
        per_device,
        mesh=mesh,
        in_specs=(
            P("seq", "dp", None),
            P("seq", "dp", None),
            P("dp"),
            P("dp", None),
            P("dp", None),
            P(None, "dp"),
            P(),
            P(),
            P("dp", None),
            P(),
            P("dp", None),
            P("dp"),
            P("dp", None),
            P("dp", None),
            P("dp", None),
        ),
        out_specs=(
            P("seq", "dp", None),
            P("seq", "dp", None),
            P("dp"),
            P("dp", None),
            P("dp", None),
            P(None, "dp"),
            P(),
            P(),
            P("dp", None),
            P(),
            P("dp", None),
            P("dp"),
            P("dp", None),
            P("dp", None),
            P("dp", None),
        ),
        check_vma=False,
    )
```

```python
import jax
import jax.numpy as jnp
from jax import lax
from jax.experimental import pallas as pl
from jax.experimental.pallas import tpu as pltpu
from jax.sharding import PartitionSpec as P

DK = 128
DV = 256
CONV = 4
ROW = 2 * DK + DV
LANES = 128
CHUNK = 256
HALO = 8

epsilon = 1e-06
narrow = jnp.bfloat16
wide = jnp.float32


def by_weight(left, right):
    return jnp.dot(left, right, preferred_element_type=wide)


def by_transpose(left, right):
    return lax.dot_general(
        left, right, (((1,), (1,)), ((), ())), preferred_element_type=wide
    )


def over_rows(left, right):
    return lax.dot_general(
        left, right, (((0,), (0,)), ((), ())), preferred_element_type=wide
    )


def row_norm(values, gain):
    inverse = lax.rsqrt(jnp.mean(values * values, axis=-1, keepdims=True) + epsilon)
    return (values * inverse * gain, inverse)


def norm_back(values, inverse, gain, grad_out):
    scaled = grad_out * gain
    grad_in = inverse * scaled - values * inverse * inverse * inverse * jnp.mean(
        scaled * values, axis=-1, keepdims=True
    )
    grad_gain = jnp.sum(grad_out * values * inverse, axis=tuple(range(values.ndim - 1)))
    return (grad_in, grad_gain)


def lower(array):
    return array.astype(narrow)


def row_sum(array):
    return jnp.sum(array, axis=1, keepdims=True)


def grid_indices():
    rows = lax.broadcasted_iota(jnp.int32, (CHUNK, CHUNK), 0)
    columns = lax.broadcasted_iota(jnp.int32, (CHUNK, CHUNK), 1)
    return rows, columns


def exact_dot(left, right):
    return jnp.dot(
        left, right, precision=lax.Precision.HIGHEST, preferred_element_type=wide
    )


def shifted_rows(rows, before):
    return jnp.concatenate([before, rows], axis=0)


def convolved(extended, taps, count):
    start = HALO - CONV + 1
    summed = extended[start : start + count] * taps[0:1]
    for offset in range(1, CONV):
        summed = summed + extended[start + offset : start + offset + count] * taps[
            offset : offset + 1
        ]
    return summed


def gates(rates, coefficients):
    strength = jax.nn.sigmoid(rates)
    shifted = rates + coefficients[0:1]
    decay = coefficients[1:2] * jax.nn.softplus(shifted)
    return strength, shifted, decay


def unit(values):
    return lax.rsqrt(row_sum(values * values) + epsilon)


def in_turn(parts):
    waiting = list(parts)
    while waiting:
        still = []
        for part in waiting:
            try:
                next(part)
                still.append(part)
            except StopIteration:
                pass
        waiting = still


def invert(lower_part, rows, columns, store):
    apart = jnp.bitwise_xor(rows, columns)
    inverse = jnp.where(rows == columns, 1.0, 0.0) - jnp.where(apart == 1, lower_part, 0.0)
    level = 1
    while (1 << level) < CHUNK:
        corner = lower(
            jnp.where(lax.shift_right_logical(apart, level) == 1, lower_part, 0.0)
        )
        held = lower(inverse)
        yield
        side = lower(by_weight(corner, held))
        yield
        inverse = inverse - by_weight(held, side)
        level += 1
    store.append(lower(inverse))


def forward_kernel(
    heads,
    place_ref,
    proj_ref,
    rates_ref,
    taps_ref,
    coef_ref,
    mixed_ref,
    inverse_ref,
    state_ref,
    corrected_ref,
    update_ref,
    weight_ref,
    active_ref,
    slope_ref,
    inner_ref,
    pair_ref,
    before,
    state,
):
    @pl.when(pl.program_id(0) == 0)
    def _():
        before[...] = jnp.zeros_like(before)
        state[...] = jnp.zeros_like(state)

    count = proj_ref.shape[0]
    rows, columns = grid_indices()
    raw = proj_ref[...].astype(wide)
    summed = convolved(shifted_rows(raw, before[...]), taps_ref[...], count)
    before[...] = raw[count - HALO :]
    sig = jax.nn.sigmoid(summed)
    active = summed * sig
    active_ref[...] = lower(active)
    slope_ref[...] = lower(sig * (1.0 + summed * (1.0 - sig)))
    strength_rows, unused, decay_rows = gates(rates_ref[...].astype(wide), coef_ref[...])
    through = jnp.where(rows >= columns, 1.0, 0.0)
    states = {(0, head): state[head] for head in range(heads)}
    blocks = count // CHUNK
    cumulative_rows = [
        exact_dot(through, decay_rows[block * CHUNK : (block + 1) * CHUNK])
        for block in range(blocks)
    ]
    turned_rows = [item.T for item in cumulative_rows]

    def one(block, head):
        base = head * ROW
        here = slice(block * CHUNK, (block + 1) * CHUNK)
        query = active[here, base : base + DK]
        key = active[here, base + DK : base + 2 * DK]
        value = active[here, base + 2 * DK : base + ROW]
        query = query * (unit(query) * DK ** (-0.5))
        key = key * unit(key)
        strength = strength_rows[here, 2 * head : 2 * head + 1]
        cumulative = cumulative_rows[block][:, 2 * head + 1 : 2 * head + 2]
        across = turned_rows[block][2 * head + 1 : 2 * head + 2]
        final = cumulative[CHUNK - 1 :]
        fade = jnp.where(
            rows >= columns, jnp.exp(jnp.minimum(cumulative - across, 0.0)), 0.0
        )
        grown = jnp.exp(cumulative)
        key_low = lower(key)
        query_low = lower(query)
        dots = by_transpose(key_low, key_low)
        yield
        pair = jnp.where(rows > columns, fade * dots, 0.0)
        pair_ref[block, head] = lower(pair)
        lower_part = strength * pair
        store = []
        yield from invert(lower_part, rows, columns, store)
        inverse = store[0]
        yield
        update = by_weight(inverse, lower(strength * value))
        weight = lower(by_weight(inverse, lower(strength * grown * key)))
        inner = lower(by_transpose(query_low, key_low) * fade)
        inner_ref[block, head] = inner
        faded = lower(key * jnp.exp(final - cumulative))
        inverse_ref[block, head] = inverse
        span = slice(head * DV, head * DV + DV)
        update_ref[here, span] = lower(update)
        weight_ref[here, head * DK : head * DK + DK] = weight
        yield
        while (block, head) not in states:
            yield
        held = states[block, head]
        held_low = lower(held)
        state_ref[block, head] = held_low
        corrected = lower(update - by_transpose(weight, held_low))
        yield
        states[block + 1, head] = held * jnp.exp(final) + over_rows(corrected, faded)
        corrected_ref[here, span] = corrected
        result = grown * by_transpose(query_low, held_low) + by_weight(inner, corrected)
        yield
        mixed_ref[here, span] = lower(result)

    in_turn(one(block, head) for block in range(blocks) for head in range(heads))
    for head in range(heads):
        state[head] = states[blocks, head]


def on_piece(pieces, body):
    for at, piece in enumerate(pieces):

        @pl.when(pl.program_id(0) == at)
        def _(at=at, piece=piece):
            body(at, piece)


def entry_kernel(count, *refs):
    weight_ref, rates_ref, gain_ref, normed_ref, proj_ref = refs[count:]
    width = weight_ref.shape[1]

    def body(at, piece):
        normed = lower(row_norm(piece[...].astype(wide), gain_ref[0:1])[0])
        normed_ref[...] = normed
        proj_ref[:, :width] = lower(by_weight(normed, weight_ref[...]))
        proj_ref[:, width:] = lower(by_weight(normed, rates_ref[...]))

    on_piece(refs[:count], body)


def gate_kernel(
    heads, mixed_ref, normed_ref, weight_ref, gain_ref, out_ref, gated_ref, gate_ref, *partials
):
    gate = by_weight(normed_ref[...], weight_ref[...])
    gate_ref[...] = gate
    gain = gain_ref[0:1]
    for head in range(heads):
        span = slice(head * DV, head * DV + DV)
        normed = row_norm(mixed_ref[:, span].astype(wide), gain)[0]
        here = gate[:, span]
        gated_ref[:, span] = lower(normed * (here * jax.nn.sigmoid(here)))
    partial = lower(by_weight(gated_ref[...], out_ref[...]))

    def body(at, piece):
        piece[...] = partial

    on_piece(partials, body)


def ffn_kernel(count, *refs):
    normed_pieces, cot_pieces = refs[:count], refs[count : 2 * count]
    both_ref, down_ref, normed_ref, cot_ref, hidden_ref, grad_ref = refs[
        2 * count : 2 * count + 6
    ]
    backs = refs[2 * count + 6 :]
    units = down_ref.shape[0]

    def body(at, piece):
        normed = piece[...]
        cot = cot_pieces[at][...]
        normed_ref[...] = normed
        cot_ref[...] = cot
        gate_pre = by_weight(normed, both_ref[:, :units])
        up_pre = by_weight(normed, both_ref[:, units:])
        sig = jax.nn.sigmoid(gate_pre)
        silu = gate_pre * sig
        hidden_ref[...] = lower(silu * up_pre)
        grad_hidden = by_transpose(cot, down_ref[...])
        grad_ref[:, :units] = lower(
            grad_hidden * up_pre * sig * (1.0 + gate_pre * (1.0 - sig))
        )
        grad_ref[:, units:] = lower(grad_hidden * silu)
        backs[at][...] = lower(by_transpose(grad_ref[...], both_ref[...]))

    on_piece(normed_pieces, body)


def branch_kernel(count, *refs):
    gated_ref, weight_ref, grad_ref, out_ref, total = refs[count:]
    quarter = out_ref.shape[2]

    def body(at, piece):
        branch = piece[...]
        grad_ref[...] = by_transpose(branch, weight_ref[...])
        product = over_rows(gated_ref[...], branch)
        total[...] = product if at == 0 else total[...] + product

    on_piece(refs[:count], body)

    @pl.when(pl.program_id(0) == count - 1)
    def _():
        for at in range(out_ref.shape[0]):
            out_ref[at] = lower(total[:, at * quarter : (at + 1) * quarter])


def backward_kernel(
    heads,
    place_ref,
    proj_ref,
    edge_ref,
    rates_ref,
    gate_ref,
    taps_ref,
    coef_ref,
    gain_ref,
    mixed_ref,
    inverse_ref,
    state_ref,
    corrected_ref,
    update_ref,
    weight_ref,
    active_ref,
    slope_ref,
    inner_ref,
    pair_ref,
    grad_ref,
    out_ref,
    taps_grad_ref,
    gain_grad_ref,
    small_grad_ref,
    after,
    state_grad,
):
    step = pl.program_id(0)

    @pl.when(step == 0)
    def _():
        after[...] = jnp.zeros_like(after)
        state_grad[...] = jnp.zeros_like(state_grad)
        taps_grad_ref[...] = jnp.zeros_like(taps_grad_ref)
        gain_grad_ref[...] = jnp.zeros_like(gain_grad_ref)
        small_grad_ref[...] = jnp.zeros_like(small_grad_ref)

    count = proj_ref.shape[0]
    blocks = count // CHUNK
    rows, columns = grid_indices()
    lanes = lax.broadcasted_iota(jnp.int32, (CHUNK, LANES), 1)
    raw = proj_ref[...].astype(wide)
    edge = edge_ref[edge_ref.shape[0] - HALO :].astype(wide)
    edge = jnp.where(step == pl.num_programs(0) - 1, 0.0, edge)
    taps = taps_ref[...]
    extended = shifted_rows(raw, edge)
    active = active_ref[...].astype(wide)
    coefficients = coef_ref[...]
    strength_rows, shifted_rates, decay_rows = gates(
        rates_ref[...].astype(wide), coefficients
    )
    through = jnp.where(rows >= columns, 1.0, 0.0)
    onward = jnp.where(columns >= rows, 1.0, 0.0)
    gain = gain_ref[0:1]
    proj_width = heads * ROW
    total = out_ref.shape[1]
    cumulative_rows = [
        exact_dot(through, decay_rows[block * CHUNK : (block + 1) * CHUNK])
        for block in range(blocks)
    ]
    turned_rows = [item.T for item in cumulative_rows]
    laters = {(blocks - 1, head): state_grad[head] for head in range(heads)}
    active_grads = {}
    column_grads = {}
    gain_grads = []

    def one(block, head):
        here = slice(block * CHUNK, (block + 1) * CHUNK)
        span = slice(head * DV, head * DV + DV)
        grad_gated = grad_ref[here, span].astype(wide)
        mixed = mixed_ref[here, span].astype(wide)
        normed, head_inverse = row_norm(mixed, gain)
        gate = gate_ref[here, span]
        sig_gate = jax.nn.sigmoid(gate)
        gate_start = proj_width + head * DV
        out_ref[here, gate_start : gate_start + DV] = lower(
            grad_gated * normed * sig_gate * (1.0 + gate * (1.0 - sig_gate))
        )
        normed_grad = grad_gated * (gate * sig_gate)
        scaled = normed_grad * gain
        grad_mixed = lower(
            head_inverse * scaled
            - mixed
            * (head_inverse * head_inverse * head_inverse)
            * jnp.mean(scaled * mixed, axis=-1, keepdims=True)
        )
        gain_grads.append(
            jnp.sum(normed_grad * mixed * head_inverse, axis=0, keepdims=True)
        )
        base = head * ROW
        query_raw = active[here, base : base + DK]
        key_raw = active[here, base + DK : base + 2 * DK]
        value = active[here, base + 2 * DK : base + ROW]
        query_unit = unit(query_raw)
        key_unit = unit(key_raw)
        query = query_raw * (query_unit * DK ** (-0.5))
        key = key_raw * key_unit
        strength = strength_rows[here, 2 * head : 2 * head + 1]
        cumulative = cumulative_rows[block][:, 2 * head + 1 : 2 * head + 2]
        across = turned_rows[block][2 * head + 1 : 2 * head + 2]
        final = cumulative[CHUNK - 1 :]
        fade = jnp.where(
            rows >= columns, jnp.exp(jnp.minimum(cumulative - across, 0.0)), 0.0
        )
        strict_fade = jnp.where(rows > columns, fade, 0.0)
        grown = jnp.exp(cumulative)
        remaining = jnp.exp(final - cumulative)
        kept = jnp.exp(final)
        key_low = lower(key)
        query_low = lower(query)
        yield
        held = state_ref[block, head]
        corrected = corrected_ref[here, span]
        weight = weight_ref[here, head * DK : head * DK + DK]
        faded = key * remaining
        faded_low = lower(faded)
        grown_query = query * grown
        yield
        inner = inner_ref[block, head]
        inner_side = over_rows(inner, grad_mixed)
        state_side = over_rows(grad_mixed, lower(grown_query))
        dot_raw = by_transpose(grad_mixed, corrected)
        dot_grad_low = lower(dot_raw * fade)
        grown_grad = by_weight(grad_mixed, held)
        yield
        while (block, head) not in laters:
            yield
        later = laters[block, head]
        later_low = lower(later)
        corrected_grad_low = lower(inner_side + by_transpose(faded_low, later_low))
        yield
        laters[block - 1, head] = (
            later * kept + state_side - over_rows(corrected_grad_low, weight)
        )
        faded_grad = by_weight(corrected, later_low)
        weight_grad = lower(-by_weight(corrected_grad_low, held))
        inverse = inverse_ref[block, head]
        yield
        value_side = over_rows(inverse, corrected_grad_low)
        key_side = over_rows(inverse, weight_grad)
        yield
        lower_raw = -(
            by_transpose(lower(value_side), update_ref[here, span])
            + by_transpose(lower(key_side), weight)
        )
        inner_query = by_weight(dot_grad_low, key_low)
        inner_key = over_rows(dot_grad_low, query_low)
        yield
        lower_grad_low = lower(lower_raw * strict_fade)
        first_key = by_weight(lower_grad_low, key_low)
        second_key = over_rows(lower_grad_low, lower(strength * key))
        pairs = lower_raw * pair_ref[block, head].astype(wide)
        both = pairs * strength + dot_raw * inner.astype(wide)
        faded_sum = row_sum(faded_grad * faded)
        key_sum = row_sum(key_side * key)
        yield
        query_grad = grown * grown_grad + inner_query
        key_grad = (
            (strength * grown) * key_side
            + strength * first_key
            + second_key
            + inner_key
            + remaining * faded_grad
        )
        head_strength_grad = row_sum(value_side * value) + grown * key_sum + row_sum(pairs)
        head_spread = (
            (strength * grown) * key_sum
            + row_sum(both)
            + row_sum(grown_grad * grown_query)
            - faded_sum
        )
        column_total = jnp.sum(both, axis=0, keepdims=True)
        late_total = row_sum(jnp.where(columns >= rows, column_total, 0.0))
        final_grad = kept * jnp.sum(held.astype(wide) * later, keepdims=True) + jnp.sum(
            faded_sum, axis=0, keepdims=True
        )
        column_grads[block, head] = (
            head_strength_grad,
            head_spread,
            final_grad - late_total,
        )
        active_grads[block, head] = (
            DK ** (-0.5)
            * query_unit
            * (
                query_grad
                - query_raw * (query_unit * query_unit) * row_sum(query_grad * query_raw)
            ),
            key_unit
            * (key_grad - key_raw * (key_unit * key_unit) * row_sum(key_grad * key_raw)),
            strength * value_side,
        )

    in_turn(
        one(block, head) for block in reversed(range(blocks)) for head in range(heads)
    )
    for head in range(heads):
        state_grad[head] = laters[-1, head]
    for block in range(blocks):
        here = slice(block * CHUNK, (block + 1) * CHUNK)
        strength_grad = jnp.zeros((CHUNK, LANES), wide)
        spread_grad = jnp.zeros((CHUNK, LANES), wide)
        extra_grad = jnp.zeros((CHUNK, LANES), wide)
        for head in range(heads):
            first, second, third = column_grads[block, head]
            strength_grad = jnp.where(lanes == 2 * head, first, strength_grad)
            spread_grad = jnp.where(lanes == 2 * head + 1, second, spread_grad)
            extra_grad = jnp.where(lanes == 2 * head + 1, third, extra_grad)
        decay_grad = exact_dot(onward, spread_grad) + extra_grad
        shift_grad = decay_grad * coefficients[1:2] * jax.nn.sigmoid(shifted_rates[here])
        strength_here = strength_rows[here]
        rates_grad = strength_grad * strength_here * (1.0 - strength_here) + shift_grad
        out_ref[here, total - LANES :] = lower(rates_grad)
        small_grad_ref[0:1] += jnp.sum(shift_grad, axis=0, keepdims=True)
        small_grad_ref[1:2] += jnp.sum(decay_grad * decay_rows[here], axis=0, keepdims=True)
    gain_grad_ref[0:1] += sum(gain_grads)
    joined = jnp.concatenate(
        [
            jnp.concatenate(
                [part for head in range(heads) for part in active_grads[block, head]], axis=1
            )
            for block in range(blocks)
        ],
        axis=0,
    )
    summed_grad = joined * slope_ref[...].astype(wide)
    following = jnp.concatenate([summed_grad, after[...]], axis=0)
    after[...] = summed_grad[:HALO]
    proj_grad = following[CONV - 1 : CONV - 1 + count] * taps[0:1]
    start = HALO - CONV + 1
    for offset in range(CONV):
        if offset:
            shift = CONV - 1 - offset
            proj_grad = proj_grad + following[shift : shift + count] * taps[offset : offset + 1]
        taps_grad_ref[offset : offset + 1] += jnp.sum(
            summed_grad * extended[start + offset : start + offset + count],
            axis=0,
            keepdims=True,
        )
    out_ref[:, :proj_width] = lower(proj_grad)


def params():
    return pltpu.CompilerParams(
        dimension_semantics=("arbitrary",), vmem_limit_bytes=52 * 1024 * 1024
    )


def effort(length, heads, each=10000000):
    return pl.CostEstimate(
        flops=length * heads * each,
        bytes_accessed=length * heads * 1024,
        transcendentals=length * heads,
    )


def mixer_forward(heads, parts, place, proj, taps, coefficients, interpret=False):
    length = proj.shape[0]
    count = length // parts
    blocks = count // CHUNK
    width = heads * ROW
    values = heads * DV

    def tall(columns, at=0):
        return pl.BlockSpec((count, columns), lambda i, me: (jnp.bitwise_xor(i, me[0]), at))

    def whole(array):
        return pl.BlockSpec(array.shape, lambda i, me: (0,) * array.ndim)

    def stacked(first, second):
        return pl.BlockSpec((blocks, heads, first, second), lambda i, me: (i, 0, 0, 0))

    chunks = parts * blocks
    return pl.pallas_call(
        lambda *refs: forward_kernel(heads, *refs),
        grid_spec=pltpu.PrefetchScalarGridSpec(
            num_scalar_prefetch=1,
            grid=(parts,),
            in_specs=[
                tall(width),
                tall(LANES, width // LANES),
                whole(taps),
                whole(coefficients),
            ],
            out_specs=[
                tall(values),
                stacked(CHUNK, CHUNK),
                stacked(DV, DK),
                tall(values),
                tall(values),
                tall(heads * DK),
                tall(width),
                tall(width),
                stacked(CHUNK, CHUNK),
                stacked(CHUNK, CHUNK),
            ],
            scratch_shapes=[
                pltpu.VMEM((HALO, width), wide),
                pltpu.VMEM((heads, DV, DK), wide),
            ],
        ),
        out_shape=[
            jax.ShapeDtypeStruct((length, values), narrow),
            jax.ShapeDtypeStruct((chunks, heads, CHUNK, CHUNK), narrow),
            jax.ShapeDtypeStruct((chunks, heads, DV, DK), narrow),
            jax.ShapeDtypeStruct((length, values), narrow),
            jax.ShapeDtypeStruct((length, values), narrow),
            jax.ShapeDtypeStruct((length, heads * DK), narrow),
            jax.ShapeDtypeStruct((length, width), narrow),
            jax.ShapeDtypeStruct((length, width), narrow),
            jax.ShapeDtypeStruct((chunks, heads, CHUNK, CHUNK), narrow),
            jax.ShapeDtypeStruct((chunks, heads, CHUNK, CHUNK), narrow),
        ],
        compiler_params=params(),
        cost_estimate=effort(length, heads, 100000),
        interpret=interpret,
    )(place, proj, proj, taps, coefficients)


def fixed(shape):
    return pl.BlockSpec(shape, lambda i: (0,) * len(shape))


def rows_of(rows, columns):
    return pl.BlockSpec((rows, columns), lambda i: (i, 0))


def shape_of(rows, columns, kind=narrow):
    return jax.ShapeDtypeStruct((rows, columns), kind)


def row_call(kernel, steps, in_specs, out_specs, out_shape, flops, interpret):
    return pl.pallas_call(
        kernel,
        grid=(steps,),
        in_specs=in_specs,
        out_specs=out_specs,
        out_shape=out_shape,
        compiler_params=params(),
        cost_estimate=pl.CostEstimate(
            flops=flops, bytes_accessed=flops // 1024, transcendentals=0
        ),
        interpret=interpret,
    )


def columns_at(rows, columns, start):
    return pl.BlockSpec((rows, columns), lambda i: (0, start // columns))


def enter(pieces, weights, width, rates_at, gain, interpret):
    steps = len(pieces)
    rows, model = pieces[0].shape
    total = width + LANES
    return row_call(
        lambda *refs: entry_kernel(steps, *refs),
        steps,
        [fixed(item.shape) for item in pieces]
        + [
            columns_at(model, width, 0),
            columns_at(model, LANES, rates_at),
            fixed(gain.shape),
        ],
        [rows_of(rows, model), rows_of(rows, total)],
        [shape_of(steps * rows, model), shape_of(steps * rows, total)],
        steps * rows * total,
        interpret,
    )(*pieces, weights, weights, gain)


def gate_rows(heads, steps, mixed, normed, weights, start, gain, w_out, interpret):
    length, values = mixed.shape
    model = normed.shape[1]
    rows = length // steps
    return row_call(
        lambda *refs: gate_kernel(heads, *refs),
        steps,
        [
            rows_of(rows, values),
            rows_of(rows, model),
            columns_at(model, values, start),
            fixed(gain.shape),
            fixed(w_out.shape),
        ],
        [rows_of(rows, values), rows_of(rows, values)] + [fixed((rows, model))] * steps,
        [shape_of(length, values), shape_of(length, values, wide)]
        + [shape_of(rows, model)] * steps,
        length * values,
        interpret,
    )(mixed, normed, weights, gain, w_out)


def ffn_rows(normed_pieces, cot_pieces, both, down, interpret):
    steps = len(normed_pieces)
    rows, model = normed_pieces[0].shape
    units = down.shape[0]
    length = steps * rows
    return row_call(
        lambda *refs: ffn_kernel(steps, *refs),
        steps,
        [fixed(item.shape) for item in (*normed_pieces, *cot_pieces)]
        + [columns_at(model, 2 * units, 0), fixed(down.shape)],
        [
            rows_of(rows, model),
            rows_of(rows, model),
            rows_of(rows, units),
            rows_of(rows, 2 * units),
        ]
        + [fixed((rows, model))] * steps,
        [
            shape_of(length, model),
            shape_of(length, model),
            shape_of(length, units),
            shape_of(length, 2 * units),
        ]
        + [shape_of(rows, model)] * steps,
        10 * length * model * units,
        interpret,
    )(*normed_pieces, *cot_pieces, both, down)


def branch_rows(pieces, gated, weight, interpret):
    steps = len(pieces)
    rows, model = pieces[0].shape
    values = weight.shape[0]
    split = (steps, values, model // steps)
    return pl.pallas_call(
        lambda *refs: branch_kernel(steps, *refs),
        grid=(steps,),
        in_specs=[fixed(item.shape) for item in pieces]
        + [rows_of(rows, values), fixed(weight.shape)],
        out_specs=[rows_of(rows, values), fixed(split)],
        out_shape=[
            shape_of(steps * rows, values, wide),
            jax.ShapeDtypeStruct(split, narrow),
        ],
        scratch_shapes=[pltpu.VMEM((values, model), wide)],
        compiler_params=params(),
        cost_estimate=pl.CostEstimate(
            flops=4 * steps * rows * model * values, bytes_accessed=rows * model,
            transcendentals=0,
        ),
        interpret=interpret,
    )(*pieces, gated, weight)


def mixer_backward(
    heads, parts, place, proj, gate, taps, coefficients, gain, kept, grad_gated, interpret=False
):
    length = proj.shape[0]
    count = length // parts
    blocks = count // CHUNK
    width = heads * ROW
    values = heads * DV
    edge_rows = 2 * HALO
    ratio = count // edge_rows

    def tall(columns, at=0):
        return pl.BlockSpec(
            (count, columns), lambda i, me: (jnp.bitwise_xor(parts - 1 - i, me[0]), at)
        )

    def edge_at(i, me):
        previous = jnp.bitwise_xor(jnp.maximum(parts - 2 - i, 0), me[0])
        return (previous * ratio + ratio - 1, 0)

    def whole(shape):
        return pl.BlockSpec(shape, lambda i, me: (0,) * len(shape))

    def stacked(first, second):
        return pl.BlockSpec(
            (blocks, heads, first, second), lambda i, me: (parts - 1 - i, 0, 0, 0)
        )

    total = width + LANES + values
    return pl.pallas_call(
        lambda *refs: backward_kernel(heads, *refs),
        grid_spec=pltpu.PrefetchScalarGridSpec(
            num_scalar_prefetch=1,
            grid=(parts,),
            in_specs=[
                tall(width),
                pl.BlockSpec((edge_rows, width), edge_at),
                tall(LANES, width // LANES),
                tall(values),
                whole(taps.shape),
                whole(coefficients.shape),
                whole(gain.shape),
                tall(values),
                stacked(CHUNK, CHUNK),
                stacked(DV, DK),
                tall(values),
                tall(values),
                tall(heads * DK),
                tall(width),
                tall(width),
                stacked(CHUNK, CHUNK),
                stacked(CHUNK, CHUNK),
                tall(values),
            ],
            out_specs=[
                tall(total),
                whole((HALO, width)),
                whole((HALO, DV)),
                whole((HALO, LANES)),
            ],
            scratch_shapes=[
                pltpu.VMEM((HALO, width), wide),
                pltpu.VMEM((heads, DV, DK), wide),
            ],
        ),
        out_shape=[
            jax.ShapeDtypeStruct((length, total), narrow),
            jax.ShapeDtypeStruct((HALO, width), wide),
            jax.ShapeDtypeStruct((HALO, DV), wide),
            jax.ShapeDtypeStruct((HALO, LANES), wide),
        ],
        compiler_params=params(),
        cost_estimate=effort(length, heads, 100000),
        interpret=interpret,
    )(place, proj, proj, proj, gate, taps, coefficients, gain, *kept, grad_gated)


def to_lanes(array):
    groups, rows, columns = array.shape
    split = array.reshape(groups, rows, columns // LANES, LANES)
    return jnp.swapaxes(split, 1, 2).reshape(groups, -1, LANES)


def from_lanes(array, rows):
    groups = array.shape[0]
    split = array.reshape(groups, -1, rows, LANES)
    return jnp.swapaxes(split, 1, 2).reshape(groups, rows, -1)


def per_device(
    tokens,
    cotangent,
    norm_attn,
    w_qkv,
    w_ba,
    conv_w,
    a_log,
    dt_bias,
    w_outgate,
    head_gain,
    w_out,
    norm_ffn,
    w_gate,
    w_up,
    w_down,
    interpret=False,
):
    parts = lax.axis_size("seq")
    shards = lax.axis_size("dp")
    place = lax.axis_index("seq")
    head_count = a_log.shape[0]
    heads = head_count // parts
    width = heads * ROW
    values = heads * DV
    model = tokens.shape[2]
    own = norm_attn.shape[0]
    out_rows = w_out.shape[0]
    quarter = model // parts

    def mine(array, size, axis):
        return lax.dynamic_slice_in_dim(array, place * size, size, axis)

    tie = lax.optimization_barrier

    def flip(array, bit):
        return lax.ppermute(array, "seq", [(i, i ^ bit) for i in range(parts)])

    def over_dp(array):
        return lax.all_gather(array, "dp", axis=0, tiled=True)

    def sum_dp(array):
        return lax.psum_scatter(array, "dp", scatter_dimension=0, tiled=True)

    def gather_seq(array):
        across = flip(array, 2)
        return [array, flip(array, 1), across, flip(across, 1)]

    def scatter_seq(pieces, beside=None):
        own_piece, sibling, across, corner = pieces
        across = across.astype(wide) + flip(lower(corner), 1).astype(wide)
        across = flip(lower(across), 2)
        sibling = flip(lower(sibling), 1)
        if beside is not None:
            across, beside = tie((across, beside))
        total = own_piece.astype(wide) + sibling.astype(wide) + across.astype(wide)
        return (total, beside)

    def sum_bits(array, low, high):
        return sum(
            [
                lax.ppermute(array, "dp", [(i, i ^ (at << low)) for i in range(shards)])
                for at in range(1, 1 << (high - low))
            ],
            array,
        )

    def absolute(stack):
        return jnp.concatenate(
            [
                lax.dynamic_index_in_dim(stack, jnp.bitwise_xor(place, at), 0)
                for at in range(parts)
            ],
            axis=0,
        )

    def exchange(stack):
        pieces = [
            lax.dynamic_index_in_dim(stack, jnp.bitwise_xor(place, at), 0)
            for at in range(parts)
        ]
        return absolute(
            jnp.concatenate(
                [pieces[0]] + [flip(pieces[at], at) for at in range(1, parts)], axis=0
            )
        )

    ffn = w_gate.shape[1]
    piece = ffn // (shards * parts)
    ffn_own = -(-(piece * shards) // LANES) * LANES
    padded = ffn_own // shards

    def ffn_columns(array):
        split = array.reshape(own, shards, parts, piece)
        split = lax.dynamic_index_in_dim(split, place, 2, keepdims=False)
        split = jnp.pad(split, ((0, 0), (0, 0), (0, padded - piece)))
        return split.reshape(own, ffn_own)

    own_tokens = tokens[:, 0, :]
    own_cot = cotangent[:, 0, :]
    small_flat = jnp.concatenate([norm_attn, norm_ffn, conv_w.reshape(-1)])
    small_count = small_flat.shape[0]
    half_lanes = LANES // 2
    small_flat = jnp.pad(small_flat, (0, own * half_lanes - small_count))
    out_ratio = out_rows // own
    w_all = over_dp(
        jnp.concatenate(
            [
                mine(w_qkv, width, 1),
                mine(w_outgate, values, 1),
                jnp.swapaxes(
                    mine(w_out, quarter, 1).reshape(out_ratio, own, quarter), 0, 1
                ).reshape(own, -1),
                jnp.pad(mine(w_ba, 2 * heads, 1), ((0, 0), (0, half_lanes - 2 * heads))),
                small_flat.reshape(own, half_lanes),
            ],
            axis=1,
        )
    )
    token_pieces = gather_seq(own_tokens)
    rates_at = w_all.shape[1] - LANES
    small_all = w_all[:, -half_lanes:].reshape(shards, -1)[:, :small_count]
    first_gain = small_all[:, :own].reshape(-1).astype(wide)
    second_gain = small_all[:, own : 2 * own].reshape(-1).astype(wide)
    taps_all = jnp.swapaxes(small_all[:, 2 * own :].reshape(shards, CONV, -1), 0, 1)
    taps = mine(taps_all.reshape(CONV, -1), width, 1).astype(wide)
    taps = jnp.pad(taps, ((0, HALO - CONV), (0, 0)))
    both_part = jnp.concatenate([ffn_columns(w_gate), ffn_columns(w_up)], axis=1)
    down_part = jnp.pad(mine(w_down, piece, 0), ((0, padded - piece), (0, 0)))
    ffn_part = jnp.concatenate(
        [both_part, from_lanes(to_lanes(down_part[None]), own)[0]], axis=1
    )
    ffn_part, w_all = tie((ffn_part, w_all))
    ffn_all = over_dp(ffn_part)

    decay_part = mine(a_log, heads, 0)
    bias_part = mine(dt_bias, heads, 0)

    def odd_lanes(vector):
        spaced = jnp.stack([jnp.zeros_like(vector), vector], axis=1).reshape(-1)
        return jnp.pad(spaced, (0, LANES - 2 * heads))[None, :]

    coefficients = jnp.pad(
        jnp.concatenate([odd_lanes(bias_part), odd_lanes(-jnp.exp(decay_part))], axis=0),
        ((0, HALO - 2), (0, 0)),
    )
    gain = jnp.broadcast_to(head_gain.astype(wide)[None, :], (HALO, DV))
    place_row = place.astype(jnp.int32)[None]

    first_rows = jnp.broadcast_to(first_gain[None, :], (HALO, model))
    normed_one, proj = enter(token_pieces, w_all, width, rates_at, first_rows, interpret)
    proj, out_part = tie((proj, w_all[:, width + values : rates_at]))
    mixed, *kept = mixer_forward(
        heads, parts, place_row, proj, taps, coefficients, interpret
    )
    mixed, *cot_pieces = tie((mixed, *gather_seq(own_cot)))
    out_part = jnp.swapaxes(out_part.reshape(shards, own, out_ratio, quarter), 1, 2)
    w_out_own = jnp.swapaxes(
        exchange(out_part.reshape(parts, values, quarter)), 0, 1
    ).reshape(values, model)
    gated, out_gate, *mixed_pieces = gate_rows(
        heads, parts, mixed, normed_one, w_all, width, gain, w_out_own, interpret
    )
    rows = own_tokens.astype(wide)
    inverse_one = row_norm(rows, first_gain)[1]
    after_mix = rows + scatter_seq(mixed_pieces)[0]
    normed_two, inverse_two = row_norm(after_mix, second_gain)
    normed_two, ffn_all = tie((lower(normed_two), ffn_all))
    down_own = from_lanes(
        to_lanes(ffn_all[:, 2 * ffn_own :].reshape(shards, own, -1)), padded
    ).reshape(ffn_own, model)
    across = flip(normed_two, 2)
    beside = flip(normed_two, 1)
    half = parts // 2
    normed_near, cot_near, hidden_near, grad_near, *back_near = ffn_rows(
        [normed_two, beside], cot_pieces[:half], ffn_all, down_own, interpret
    )
    across, *back_near = tie((across, *back_near))
    normed_far, cot_far, hidden_far, grad_far, *back_far = ffn_rows(
        [across, flip(across, 1)], cot_pieces[half:], ffn_all, down_own, interpret
    )
    grad_both = over_rows(normed_near, grad_near) + over_rows(normed_far, grad_far)
    grad_down = over_rows(hidden_near, cot_near) + over_rows(hidden_far, cot_far)
    grad_down = from_lanes(
        to_lanes(lower(grad_down).reshape(shards, padded, model)), own
    ).reshape(model, -1)
    grad_ffn = jnp.concatenate([lower(grad_both), grad_down], axis=1)
    grad_normed_two, grad_ffn = scatter_seq(back_near + back_far, grad_ffn)
    grad_ffn = sum_dp(grad_ffn)
    back_two, unused = norm_back(after_mix, inverse_two, second_gain, grad_normed_two)
    grad_after = own_cot.astype(wide) + back_two
    grad_low = lower(grad_after)
    across = flip(grad_low, 2)
    beside = flip(grad_low, 1)
    down_near = lower(by_weight(hidden_near, down_own))
    down_far = lower(by_weight(hidden_far, down_own))
    across, down_near, down_far = tie((across, down_near, down_far))
    grad_gated, grad_out = branch_rows(
        [grad_low, beside, across, flip(across, 1)], gated, w_out_own, interpret
    )
    grad_out = exchange(grad_out)
    grad_out = jnp.swapaxes(grad_out.reshape(shards, out_ratio, own, quarter), 1, 2).reshape(
        model, -1
    )
    count = own_tokens.shape[0]
    result = after_mix + scatter_seq(
        [down_near[:count], down_near[count:], down_far[:count], down_far[count:]]
    )[0]
    grad_in, grad_taps, grad_gain, grad_small = mixer_backward(
        heads, parts, place_row, proj, out_gate, taps, coefficients, gain, [mixed, *kept],
        grad_gated, interpret
    )
    grad_w_in = jnp.concatenate([lower(over_rows(normed_one, grad_in)), grad_out], axis=1)
    grad_in, grad_w_in = tie((grad_in, grad_w_in))
    grad_w_in = sum_dp(grad_w_in)
    split = width + values
    one_far, one_near = (
        by_transpose(grad_in[span, :split], w_all[:, :split])
        + by_transpose(grad_in[span, split:], w_all[:, rates_at:])
        for span in (slice(2 * count, None), slice(0, 2 * count))
    )
    first_pieces = [
        one_near[:count],
        flip(lower(one_near[count:]), 1),
        flip(lower(one_far[:count]), 2),
        flip(lower(one_far[count:]), 3),
    ]

    taps_full = lax.dynamic_update_slice_in_dim(
        jnp.zeros((CONV, head_count * ROW), wide), grad_taps[:CONV], place * width, 1
    )

    def to_heads(lane_row):
        return lax.dynamic_update_slice_in_dim(
            jnp.zeros((head_count,), wide), lane_row[1 : 2 * heads : 2], place * heads, 0
        )

    packed = jnp.concatenate(
        [
            taps_full.reshape(-1, LANES),
            grad_gain[0].reshape(-1, LANES),
            jnp.pad(
                jnp.stack([to_heads(grad_small[1]), to_heads(grad_small[0])]),
                ((0, 0), (0, LANES - head_count)),
            ),
        ],
        axis=0,
    )
    packed = jnp.pad(packed, ((0, -packed.shape[0] % HALO), (0, 0)))
    packed = sum([flip(packed, at) for at in range(1, parts)], packed)
    bits = shards.bit_length() - 1
    packed = sum_bits(packed, bits // 2, bits)

    def in_order(near):
        low_bit = jnp.bitwise_and(place, 1) != 0
        high_bit = jnp.bitwise_and(place, 2) != 0
        return [
            jnp.where(
                high_bit,
                jnp.where(low_bit, near[at ^ 3], near[at ^ 2]),
                jnp.where(low_bit, near[at ^ 1], near[at]),
            )
            for at in range(parts)
        ]

    def side_by_side(pieces):
        return jnp.concatenate(pieces, axis=1).astype(wide)

    def ffn_full(pieces):
        split = jnp.stack(
            [item.reshape(own, shards, padded)[..., :piece] for item in pieces], axis=2
        )
        return split.reshape(own, -1).astype(wide)

    grad_w_in, packed, ffn_pieces, first_pieces = tie(
        (grad_w_in, packed, gather_seq(grad_ffn), first_pieces)
    )
    in_pieces = in_order(gather_seq(grad_w_in))
    packed = sum_bits(packed, 0, bits // 2)
    back_one, unused = norm_back(
        rows,
        inverse_one,
        first_gain,
        sum([item.astype(wide) for item in first_pieces[1:]], first_pieces[0]),
    )
    grad_rows = lower(grad_after + back_one)[:, None, :]
    ffn_pieces = in_order(ffn_pieces)
    grad_w_gate = ffn_full([item[:, :ffn_own] for item in ffn_pieces])
    grad_w_up = ffn_full([item[:, ffn_own : 2 * ffn_own] for item in ffn_pieces])
    grad_w_down = jnp.concatenate(
        [
            from_lanes(to_lanes(item[None, :, 2 * ffn_own :]), padded)[0][:piece]
            for item in ffn_pieces
        ],
        axis=0,
    ).astype(wide)
    def along(weights, grads):
        return sum(
            jnp.sum(weight.astype(wide) * grad, axis=1)
            for weight, grad in zip(weights, grads)
        )

    grad_norm_ffn = along((w_gate, w_up), (grad_w_gate, grad_w_up)) / norm_ffn.astype(wide)
    taps_rows = CONV * head_count * ROW // LANES
    gain_rows = taps_rows + DV // LANES
    own_taps = conv_w.shape[1]
    taps_total = lax.dynamic_slice_in_dim(
        packed[:taps_rows].reshape(CONV, -1), lax.axis_index("dp") * own_taps, own_taps, 1
    )
    total = split + LANES
    grad_w_qkv = side_by_side([item[:, :width] for item in in_pieces])
    grad_w_ba = side_by_side([item[:, split : split + 2 * heads] for item in in_pieces])
    grad_w_outgate = side_by_side([item[:, width:split] for item in in_pieces])
    grad_w_out = side_by_side(
        [
            jnp.swapaxes(item[:, total:].reshape(own, out_ratio, quarter), 0, 1).reshape(
                out_rows, quarter
            )
            for item in in_pieces
        ]
    )
    grad_norm_attn = along(
        (w_qkv, w_ba, w_outgate), (grad_w_qkv, grad_w_ba, grad_w_outgate)
    ) / norm_attn.astype(wide)
    return (
        lower(result)[:, None, :],
        grad_rows,
        grad_norm_attn,
        grad_w_qkv,
        grad_w_ba,
        taps_total,
        packed[gain_rows, :head_count],
        packed[gain_rows + 1, :head_count],
        grad_w_outgate,
        packed[taps_rows:gain_rows].reshape(-1),
        grad_w_out,
        grad_norm_ffn,
        grad_w_gate,
        grad_w_up,
        grad_w_down,
    )


def solution(mesh):
    return jax.shard_map(
        per_device,
        mesh=mesh,
        in_specs=(
            P("seq", "dp", None),
            P("seq", "dp", None),
            P("dp"),
            P("dp", None),
            P("dp", None),
            P(None, "dp"),
            P(),
            P(),
            P("dp", None),
            P(),
            P("dp", None),
            P("dp"),
            P("dp", None),
            P("dp", None),
            P("dp", None),
        ),
        out_specs=(
            P("seq", "dp", None),
            P("seq", "dp", None),
            P("dp"),
            P("dp", None),
            P("dp", None),
            P(None, "dp"),
            P(),
            P(),
            P("dp", None),
            P(),
            P("dp", None),
            P("dp"),
            P("dp", None),
            P("dp", None),
            P("dp", None),
        ),
        check_vma=False,
    )
```

```python
import jax
import jax.numpy as jnp
from jax import lax
from jax.experimental import pallas as pl
from jax.experimental.pallas import tpu as pltpu
from jax.sharding import PartitionSpec as P

DK = 128
DV = 256
CONV = 4
ROW = 2 * DK + DV
LANES = 128
CHUNK = 256
HALO = 8

epsilon = 1e-06
narrow = jnp.bfloat16
wide = jnp.float32


def by_weight(left, right):
    return jnp.dot(left, right, preferred_element_type=wide)


def by_transpose(left, right):
    return lax.dot_general(
        left, right, (((1,), (1,)), ((), ())), preferred_element_type=wide
    )


def over_rows(left, right):
    return lax.dot_general(
        left, right, (((0,), (0,)), ((), ())), preferred_element_type=wide
    )


def row_norm(values, gain):
    inverse = lax.rsqrt(jnp.mean(values * values, axis=-1, keepdims=True) + epsilon)
    return (values * inverse * gain, inverse)


def norm_back(values, inverse, gain, grad_out):
    scaled = grad_out * gain
    grad_in = inverse * scaled - values * inverse * inverse * inverse * jnp.mean(
        scaled * values, axis=-1, keepdims=True
    )
    grad_gain = jnp.sum(grad_out * values * inverse, axis=tuple(range(values.ndim - 1)))
    return (grad_in, grad_gain)


def lower(array):
    return array.astype(narrow)


def row_sum(array):
    return jnp.sum(array, axis=1, keepdims=True)


def grid_indices():
    rows = lax.broadcasted_iota(jnp.int32, (CHUNK, CHUNK), 0)
    columns = lax.broadcasted_iota(jnp.int32, (CHUNK, CHUNK), 1)
    return rows, columns


def exact_dot(left, right):
    return jnp.dot(
        left, right, precision=lax.Precision.HIGHEST, preferred_element_type=wide
    )


def shifted_rows(rows, before):
    return jnp.concatenate([before, rows], axis=0)


def convolved(extended, taps, count):
    start = HALO - CONV + 1
    summed = extended[start : start + count] * taps[0:1]
    for offset in range(1, CONV):
        summed = summed + extended[start + offset : start + offset + count] * taps[
            offset : offset + 1
        ]
    return summed


def gates(rates, coefficients):
    strength = jax.nn.sigmoid(rates)
    shifted = rates + coefficients[0:1]
    decay = coefficients[1:2] * jax.nn.softplus(shifted)
    return strength, shifted, decay


def unit(values):
    return lax.rsqrt(row_sum(values * values) + epsilon)


def in_turn(parts):
    waiting = list(parts)
    while waiting:
        still = []
        for part in waiting:
            try:
                next(part)
                still.append(part)
            except StopIteration:
                pass
        waiting = still


def invert(lower_part, rows, columns, store):
    apart = jnp.bitwise_xor(rows, columns)
    inverse = jnp.where(rows == columns, 1.0, 0.0) - jnp.where(apart == 1, lower_part, 0.0)
    level = 1
    while (1 << level) < CHUNK:
        corner = lower(
            jnp.where(lax.shift_right_logical(apart, level) == 1, lower_part, 0.0)
        )
        held = lower(inverse)
        yield
        side = lower(by_weight(corner, held))
        yield
        inverse = inverse - by_weight(held, side)
        level += 1
    store.append(lower(inverse))


def forward_kernel(
    heads,
    place_ref,
    proj_ref,
    rates_ref,
    taps_ref,
    coef_ref,
    mixed_ref,
    inverse_ref,
    state_ref,
    corrected_ref,
    update_ref,
    weight_ref,
    active_ref,
    slope_ref,
    inner_ref,
    pair_ref,
    before,
    state,
):
    @pl.when(pl.program_id(0) == 0)
    def _():
        before[...] = jnp.zeros_like(before)
        state[...] = jnp.zeros_like(state)

    count = proj_ref.shape[0]
    rows, columns = grid_indices()
    raw = proj_ref[...].astype(wide)
    summed = convolved(shifted_rows(raw, before[...]), taps_ref[...], count)
    before[...] = raw[count - HALO :]
    sig = jax.nn.sigmoid(summed)
    active = summed * sig
    active_ref[...] = lower(active)
    slope_ref[...] = lower(sig * (1.0 + summed * (1.0 - sig)))
    strength_rows, unused, decay_rows = gates(rates_ref[...].astype(wide), coef_ref[...])
    through = jnp.where(rows >= columns, 1.0, 0.0)
    states = {(0, head): state[head] for head in range(heads)}
    blocks = count // CHUNK
    cumulative_rows = [
        exact_dot(through, decay_rows[block * CHUNK : (block + 1) * CHUNK])
        for block in range(blocks)
    ]
    turned_rows = [item.T for item in cumulative_rows]

    def one(block, head):
        base = head * ROW
        here = slice(block * CHUNK, (block + 1) * CHUNK)
        query = active[here, base : base + DK]
        key = active[here, base + DK : base + 2 * DK]
        value = active[here, base + 2 * DK : base + ROW]
        query = query * (unit(query) * DK ** (-0.5))
        key = key * unit(key)
        strength = strength_rows[here, 2 * head : 2 * head + 1]
        cumulative = cumulative_rows[block][:, 2 * head + 1 : 2 * head + 2]
        across = turned_rows[block][2 * head + 1 : 2 * head + 2]
        final = cumulative[CHUNK - 1 :]
        fade = jnp.where(
            rows >= columns, jnp.exp(jnp.minimum(cumulative - across, 0.0)), 0.0
        )
        grown = jnp.exp(cumulative)
        key_low = lower(key)
        query_low = lower(query)
        dots = by_transpose(key_low, key_low)
        yield
        pair = jnp.where(rows > columns, fade * dots, 0.0)
        pair_ref[block, head] = lower(pair)
        lower_part = strength * pair
        store = []
        yield from invert(lower_part, rows, columns, store)
        inverse = store[0]
        yield
        update = by_weight(inverse, lower(strength * value))
        weight = lower(by_weight(inverse, lower(strength * grown * key)))
        inner = lower(by_transpose(query_low, key_low) * fade)
        inner_ref[block, head] = inner
        faded = lower(key * jnp.exp(final - cumulative))
        inverse_ref[block, head] = inverse
        span = slice(head * DV, head * DV + DV)
        update_ref[here, span] = lower(update)
        weight_ref[here, head * DK : head * DK + DK] = weight
        yield
        while (block, head) not in states:
            yield
        held = states[block, head]
        held_low = lower(held)
        state_ref[block, head] = held_low
        corrected = lower(update - by_transpose(weight, held_low))
        yield
        states[block + 1, head] = held * jnp.exp(final) + over_rows(corrected, faded)
        corrected_ref[here, span] = corrected
        result = grown * by_transpose(query_low, held_low) + by_weight(inner, corrected)
        yield
        mixed_ref[here, span] = lower(result)

    in_turn(one(block, head) for block in range(blocks) for head in range(heads))
    for head in range(heads):
        state[head] = states[blocks, head]


def on_piece(pieces, body):
    for at, piece in enumerate(pieces):

        @pl.when(pl.program_id(0) == at)
        def _(at=at, piece=piece):
            body(at, piece)


def entry_kernel(count, *refs):
    weight_ref, rates_ref, gain_ref, normed_ref, proj_ref = refs[count:]
    width = weight_ref.shape[1]

    def body(at, piece):
        normed = lower(row_norm(piece[...].astype(wide), gain_ref[0:1])[0])
        normed_ref[...] = normed
        proj_ref[:, :width] = lower(by_weight(normed, weight_ref[...]))
        proj_ref[:, width:] = lower(by_weight(normed, rates_ref[...]))

    on_piece(refs[:count], body)


def gate_kernel(
    heads, mixed_ref, normed_ref, weight_ref, gain_ref, out_ref, gated_ref, gate_ref, *partials
):
    gate = by_weight(normed_ref[...], weight_ref[...])
    gate_ref[...] = gate
    gain = gain_ref[0:1]
    for head in range(heads):
        span = slice(head * DV, head * DV + DV)
        normed = row_norm(mixed_ref[:, span].astype(wide), gain)[0]
        here = gate[:, span]
        gated_ref[:, span] = lower(normed * (here * jax.nn.sigmoid(here)))
    partial = lower(by_weight(gated_ref[...], out_ref[...]))

    def body(at, piece):
        piece[...] = partial

    on_piece(partials, body)


def ffn_kernel(count, *refs):
    normed_pieces, cot_pieces = refs[:count], refs[count : 2 * count]
    both_ref, down_ref, normed_ref, cot_ref, hidden_ref, grad_ref = refs[
        2 * count : 2 * count + 6
    ]
    backs = refs[2 * count + 6 :]
    units = down_ref.shape[0]

    def body(at, piece):
        normed = piece[...]
        cot = cot_pieces[at][...]
        normed_ref[...] = normed
        cot_ref[...] = cot
        gate_pre = by_weight(normed, both_ref[:, :units])
        up_pre = by_weight(normed, both_ref[:, units:])
        sig = jax.nn.sigmoid(gate_pre)
        silu = gate_pre * sig
        hidden_ref[...] = lower(silu * up_pre)
        grad_hidden = by_transpose(cot, down_ref[...])
        grad_ref[:, :units] = lower(
            grad_hidden * up_pre * sig * (1.0 + gate_pre * (1.0 - sig))
        )
        grad_ref[:, units:] = lower(grad_hidden * silu)
        backs[at][...] = lower(by_transpose(grad_ref[...], both_ref[...]))

    on_piece(normed_pieces, body)


def branch_kernel(count, *refs):
    gated_ref, weight_ref, grad_ref, out_ref, total = refs[count:]
    quarter = out_ref.shape[2]

    def body(at, piece):
        branch = piece[...]
        grad_ref[...] = by_transpose(branch, weight_ref[...])
        product = over_rows(gated_ref[...], branch)
        total[...] = product if at == 0 else total[...] + product

    on_piece(refs[:count], body)

    @pl.when(pl.program_id(0) == count - 1)
    def _():
        for at in range(out_ref.shape[0]):
            out_ref[at] = lower(total[:, at * quarter : (at + 1) * quarter])


def backward_kernel(
    heads,
    place_ref,
    proj_ref,
    edge_ref,
    rates_ref,
    gate_ref,
    taps_ref,
    coef_ref,
    gain_ref,
    mixed_ref,
    inverse_ref,
    state_ref,
    corrected_ref,
    update_ref,
    weight_ref,
    active_ref,
    slope_ref,
    inner_ref,
    pair_ref,
    grad_ref,
    out_ref,
    taps_grad_ref,
    gain_grad_ref,
    small_grad_ref,
    after,
    state_grad,
):
    step = pl.program_id(0)

    @pl.when(step == 0)
    def _():
        after[...] = jnp.zeros_like(after)
        state_grad[...] = jnp.zeros_like(state_grad)
        taps_grad_ref[...] = jnp.zeros_like(taps_grad_ref)
        gain_grad_ref[...] = jnp.zeros_like(gain_grad_ref)
        small_grad_ref[...] = jnp.zeros_like(small_grad_ref)

    count = proj_ref.shape[0]
    blocks = count // CHUNK
    rows, columns = grid_indices()
    lanes = lax.broadcasted_iota(jnp.int32, (CHUNK, LANES), 1)
    raw = proj_ref[...].astype(wide)
    edge = edge_ref[edge_ref.shape[0] - HALO :].astype(wide)
    edge = jnp.where(step == pl.num_programs(0) - 1, 0.0, edge)
    taps = taps_ref[...]
    extended = shifted_rows(raw, edge)
    active = active_ref[...].astype(wide)
    coefficients = coef_ref[...]
    strength_rows, shifted_rates, decay_rows = gates(
        rates_ref[...].astype(wide), coefficients
    )
    through = jnp.where(rows >= columns, 1.0, 0.0)
    onward = jnp.where(columns >= rows, 1.0, 0.0)
    gain = gain_ref[0:1]
    proj_width = heads * ROW
    total = out_ref.shape[1]
    cumulative_rows = [
        exact_dot(through, decay_rows[block * CHUNK : (block + 1) * CHUNK])
        for block in range(blocks)
    ]
    turned_rows = [item.T for item in cumulative_rows]
    laters = {(blocks - 1, head): state_grad[head] for head in range(heads)}
    active_grads = {}
    column_grads = {}
    gain_grads = []

    def one(block, head):
        here = slice(block * CHUNK, (block + 1) * CHUNK)
        span = slice(head * DV, head * DV + DV)
        grad_gated = grad_ref[here, span].astype(wide)
        mixed = mixed_ref[here, span].astype(wide)
        normed, head_inverse = row_norm(mixed, gain)
        gate = gate_ref[here, span]
        sig_gate = jax.nn.sigmoid(gate)
        gate_start = proj_width + head * DV
        out_ref[here, gate_start : gate_start + DV] = lower(
            grad_gated * normed * sig_gate * (1.0 + gate * (1.0 - sig_gate))
        )
        normed_grad = grad_gated * (gate * sig_gate)
        scaled = normed_grad * gain
        grad_mixed = lower(
            head_inverse * scaled
            - mixed
            * (head_inverse * head_inverse * head_inverse)
            * jnp.mean(scaled * mixed, axis=-1, keepdims=True)
        )
        gain_grads.append(
            jnp.sum(normed_grad * mixed * head_inverse, axis=0, keepdims=True)
        )
        base = head * ROW
        query_raw = active[here, base : base + DK]
        key_raw = active[here, base + DK : base + 2 * DK]
        value = active[here, base + 2 * DK : base + ROW]
        query_unit = unit(query_raw)
        key_unit = unit(key_raw)
        query = query_raw * (query_unit * DK ** (-0.5))
        key = key_raw * key_unit
        strength = strength_rows[here, 2 * head : 2 * head + 1]
        cumulative = cumulative_rows[block][:, 2 * head + 1 : 2 * head + 2]
        across = turned_rows[block][2 * head + 1 : 2 * head + 2]
        final = cumulative[CHUNK - 1 :]
        fade = jnp.where(
            rows >= columns, jnp.exp(jnp.minimum(cumulative - across, 0.0)), 0.0
        )
        strict_fade = jnp.where(rows > columns, fade, 0.0)
        grown = jnp.exp(cumulative)
        remaining = jnp.exp(final - cumulative)
        kept = jnp.exp(final)
        key_low = lower(key)
        query_low = lower(query)
        yield
        held = state_ref[block, head]
        corrected = corrected_ref[here, span]
        weight = weight_ref[here, head * DK : head * DK + DK]
        faded = key * remaining
        faded_low = lower(faded)
        grown_query = query * grown
        yield
        inner = inner_ref[block, head]
        inner_side = over_rows(inner, grad_mixed)
        state_side = over_rows(grad_mixed, lower(grown_query))
        dot_raw = by_transpose(grad_mixed, corrected)
        dot_grad_low = lower(dot_raw * fade)
        grown_grad = by_weight(grad_mixed, held)
        yield
        while (block, head) not in laters:
            yield
        later = laters[block, head]
        later_low = lower(later)
        corrected_grad_low = lower(inner_side + by_transpose(faded_low, later_low))
        yield
        laters[block - 1, head] = (
            later * kept + state_side - over_rows(corrected_grad_low, weight)
        )
        faded_grad = by_weight(corrected, later_low)
        weight_grad = lower(-by_weight(corrected_grad_low, held))
        inverse = inverse_ref[block, head]
        yield
        value_side = over_rows(inverse, corrected_grad_low)
        key_side = over_rows(inverse, weight_grad)
        yield
        lower_raw = -(
            by_transpose(lower(value_side), update_ref[here, span])
            + by_transpose(lower(key_side), weight)
        )
        inner_query = by_weight(dot_grad_low, key_low)
        inner_key = over_rows(dot_grad_low, query_low)
        yield
        lower_grad_low = lower(lower_raw * strict_fade)
        first_key = by_weight(lower_grad_low, key_low)
        second_key = over_rows(lower_grad_low, lower(strength * key))
        pairs = lower_raw * pair_ref[block, head].astype(wide)
        both = pairs * strength + dot_raw * inner.astype(wide)
        faded_sum = row_sum(faded_grad * faded)
        key_sum = row_sum(key_side * key)
        yield
        query_grad = grown * grown_grad + inner_query
        key_grad = (
            (strength * grown) * key_side
            + strength * first_key
            + second_key
            + inner_key
            + remaining * faded_grad
        )
        head_strength_grad = row_sum(value_side * value) + grown * key_sum + row_sum(pairs)
        head_spread = (
            (strength * grown) * key_sum
            + row_sum(both)
            + row_sum(grown_grad * grown_query)
            - faded_sum
        )
        column_total = jnp.sum(both, axis=0, keepdims=True)
        late_total = row_sum(jnp.where(columns >= rows, column_total, 0.0))
        final_grad = kept * jnp.sum(held.astype(wide) * later, keepdims=True) + jnp.sum(
            faded_sum, axis=0, keepdims=True
        )
        column_grads[block, head] = (
            head_strength_grad,
            head_spread,
            final_grad - late_total,
        )
        active_grads[block, head] = (
            DK ** (-0.5)
            * query_unit
            * (
                query_grad
                - query_raw * (query_unit * query_unit) * row_sum(query_grad * query_raw)
            ),
            key_unit
            * (key_grad - key_raw * (key_unit * key_unit) * row_sum(key_grad * key_raw)),
            strength * value_side,
        )

    in_turn(
        one(block, head) for block in reversed(range(blocks)) for head in range(heads)
    )
    for head in range(heads):
        state_grad[head] = laters[-1, head]
    for block in range(blocks):
        here = slice(block * CHUNK, (block + 1) * CHUNK)
        strength_grad = jnp.zeros((CHUNK, LANES), wide)
        spread_grad = jnp.zeros((CHUNK, LANES), wide)
        extra_grad = jnp.zeros((CHUNK, LANES), wide)
        for head in range(heads):
            first, second, third = column_grads[block, head]
            strength_grad = jnp.where(lanes == 2 * head, first, strength_grad)
            spread_grad = jnp.where(lanes == 2 * head + 1, second, spread_grad)
            extra_grad = jnp.where(lanes == 2 * head + 1, third, extra_grad)
        decay_grad = exact_dot(onward, spread_grad) + extra_grad
        shift_grad = decay_grad * coefficients[1:2] * jax.nn.sigmoid(shifted_rates[here])
        strength_here = strength_rows[here]
        rates_grad = strength_grad * strength_here * (1.0 - strength_here) + shift_grad
        out_ref[here, total - LANES :] = lower(rates_grad)
        small_grad_ref[0:1] += jnp.sum(shift_grad, axis=0, keepdims=True)
        small_grad_ref[1:2] += jnp.sum(decay_grad * decay_rows[here], axis=0, keepdims=True)
    gain_grad_ref[0:1] += sum(gain_grads)
    joined = jnp.concatenate(
        [
            jnp.concatenate(
                [part for head in range(heads) for part in active_grads[block, head]], axis=1
            )
            for block in range(blocks)
        ],
        axis=0,
    )
    summed_grad = joined * slope_ref[...].astype(wide)
    following = jnp.concatenate([summed_grad, after[...]], axis=0)
    after[...] = summed_grad[:HALO]
    proj_grad = following[CONV - 1 : CONV - 1 + count] * taps[0:1]
    start = HALO - CONV + 1
    for offset in range(CONV):
        if offset:
            shift = CONV - 1 - offset
            proj_grad = proj_grad + following[shift : shift + count] * taps[offset : offset + 1]
        taps_grad_ref[offset : offset + 1] += jnp.sum(
            summed_grad * extended[start + offset : start + offset + count],
            axis=0,
            keepdims=True,
        )
    out_ref[:, :proj_width] = lower(proj_grad)


def params():
    return pltpu.CompilerParams(
        dimension_semantics=("arbitrary",), vmem_limit_bytes=52 * 1024 * 1024
    )


def effort(length, heads, each=10000000):
    return pl.CostEstimate(
        flops=length * heads * each,
        bytes_accessed=length * heads * 1024,
        transcendentals=length * heads,
    )


def mixer_forward(heads, parts, place, proj, taps, coefficients, interpret=False):
    length = proj.shape[0]
    count = length // parts
    blocks = count // CHUNK
    width = heads * ROW
    values = heads * DV

    def tall(columns, at=0):
        return pl.BlockSpec((count, columns), lambda i, me: (jnp.bitwise_xor(i, me[0]), at))

    def whole(array):
        return pl.BlockSpec(array.shape, lambda i, me: (0,) * array.ndim)

    def stacked(first, second):
        return pl.BlockSpec((blocks, heads, first, second), lambda i, me: (i, 0, 0, 0))

    chunks = parts * blocks
    return pl.pallas_call(
        lambda *refs: forward_kernel(heads, *refs),
        grid_spec=pltpu.PrefetchScalarGridSpec(
            num_scalar_prefetch=1,
            grid=(parts,),
            in_specs=[
                tall(width),
                tall(LANES, width // LANES),
                whole(taps),
                whole(coefficients),
            ],
            out_specs=[
                tall(values),
                stacked(CHUNK, CHUNK),
                stacked(DV, DK),
                tall(values),
                tall(values),
                tall(heads * DK),
                tall(width),
                tall(width),
                stacked(CHUNK, CHUNK),
                stacked(CHUNK, CHUNK),
            ],
            scratch_shapes=[
                pltpu.VMEM((HALO, width), wide),
                pltpu.VMEM((heads, DV, DK), wide),
            ],
        ),
        out_shape=[
            jax.ShapeDtypeStruct((length, values), narrow),
            jax.ShapeDtypeStruct((chunks, heads, CHUNK, CHUNK), narrow),
            jax.ShapeDtypeStruct((chunks, heads, DV, DK), narrow),
            jax.ShapeDtypeStruct((length, values), narrow),
            jax.ShapeDtypeStruct((length, values), narrow),
            jax.ShapeDtypeStruct((length, heads * DK), narrow),
            jax.ShapeDtypeStruct((length, width), narrow),
            jax.ShapeDtypeStruct((length, width), narrow),
            jax.ShapeDtypeStruct((chunks, heads, CHUNK, CHUNK), narrow),
            jax.ShapeDtypeStruct((chunks, heads, CHUNK, CHUNK), narrow),
        ],
        compiler_params=params(),
        cost_estimate=effort(length, heads, 100000),
        interpret=interpret,
    )(place, proj, proj, taps, coefficients)


def fixed(shape):
    return pl.BlockSpec(shape, lambda i: (0,) * len(shape))


def rows_of(rows, columns):
    return pl.BlockSpec((rows, columns), lambda i: (i, 0))


def shape_of(rows, columns, kind=narrow):
    return jax.ShapeDtypeStruct((rows, columns), kind)


def row_call(kernel, steps, in_specs, out_specs, out_shape, flops, interpret):
    return pl.pallas_call(
        kernel,
        grid=(steps,),
        in_specs=in_specs,
        out_specs=out_specs,
        out_shape=out_shape,
        compiler_params=params(),
        cost_estimate=pl.CostEstimate(
            flops=flops, bytes_accessed=flops // 1024, transcendentals=0
        ),
        interpret=interpret,
    )


def columns_at(rows, columns, start):
    return pl.BlockSpec((rows, columns), lambda i: (0, start // columns))


def enter(pieces, weights, width, rates_at, gain, interpret):
    steps = len(pieces)
    rows, model = pieces[0].shape
    total = width + LANES
    return row_call(
        lambda *refs: entry_kernel(steps, *refs),
        steps,
        [fixed(item.shape) for item in pieces]
        + [
            columns_at(model, width, 0),
            columns_at(model, LANES, rates_at),
            fixed(gain.shape),
        ],
        [rows_of(rows, model), rows_of(rows, total)],
        [shape_of(steps * rows, model), shape_of(steps * rows, total)],
        steps * rows * total,
        interpret,
    )(*pieces, weights, weights, gain)


def gate_rows(heads, steps, mixed, normed, weights, start, gain, w_out, interpret):
    length, values = mixed.shape
    model = normed.shape[1]
    rows = length // steps
    return row_call(
        lambda *refs: gate_kernel(heads, *refs),
        steps,
        [
            rows_of(rows, values),
            rows_of(rows, model),
            columns_at(model, values, start),
            fixed(gain.shape),
            fixed(w_out.shape),
        ],
        [rows_of(rows, values), rows_of(rows, values)] + [fixed((rows, model))] * steps,
        [shape_of(length, values), shape_of(length, values, wide)]
        + [shape_of(rows, model)] * steps,
        length * values,
        interpret,
    )(mixed, normed, weights, gain, w_out)


def ffn_rows(normed_pieces, cot_pieces, both, down, interpret):
    steps = len(normed_pieces)
    rows, model = normed_pieces[0].shape
    units = down.shape[0]
    length = steps * rows
    return row_call(
        lambda *refs: ffn_kernel(steps, *refs),
        steps,
        [fixed(item.shape) for item in (*normed_pieces, *cot_pieces)]
        + [columns_at(model, 2 * units, 0), fixed(down.shape)],
        [
            rows_of(rows, model),
            rows_of(rows, model),
            rows_of(rows, units),
            rows_of(rows, 2 * units),
        ]
        + [fixed((rows, model))] * steps,
        [
            shape_of(length, model),
            shape_of(length, model),
            shape_of(length, units),
            shape_of(length, 2 * units),
        ]
        + [shape_of(rows, model)] * steps,
        10 * length * model * units,
        interpret,
    )(*normed_pieces, *cot_pieces, both, down)


def branch_rows(pieces, gated, weight, interpret):
    steps = len(pieces)
    rows, model = pieces[0].shape
    values = weight.shape[0]
    split = (steps, values, model // steps)
    return pl.pallas_call(
        lambda *refs: branch_kernel(steps, *refs),
        grid=(steps,),
        in_specs=[fixed(item.shape) for item in pieces]
        + [rows_of(rows, values), fixed(weight.shape)],
        out_specs=[rows_of(rows, values), fixed(split)],
        out_shape=[
            shape_of(steps * rows, values, wide),
            jax.ShapeDtypeStruct(split, narrow),
        ],
        scratch_shapes=[pltpu.VMEM((values, model), wide)],
        compiler_params=params(),
        cost_estimate=pl.CostEstimate(
            flops=4 * steps * rows * model * values, bytes_accessed=rows * model,
            transcendentals=0,
        ),
        interpret=interpret,
    )(*pieces, gated, weight)


def mixer_backward(
    heads, parts, place, proj, gate, taps, coefficients, gain, kept, grad_gated, interpret=False
):
    length = proj.shape[0]
    count = length // parts
    blocks = count // CHUNK
    width = heads * ROW
    values = heads * DV
    edge_rows = 2 * HALO
    ratio = count // edge_rows

    def tall(columns, at=0):
        return pl.BlockSpec(
            (count, columns), lambda i, me: (jnp.bitwise_xor(parts - 1 - i, me[0]), at)
        )

    def edge_at(i, me):
        previous = jnp.bitwise_xor(jnp.maximum(parts - 2 - i, 0), me[0])
        return (previous * ratio + ratio - 1, 0)

    def whole(shape):
        return pl.BlockSpec(shape, lambda i, me: (0,) * len(shape))

    def stacked(first, second):
        return pl.BlockSpec(
            (blocks, heads, first, second), lambda i, me: (parts - 1 - i, 0, 0, 0)
        )

    total = width + LANES + values
    return pl.pallas_call(
        lambda *refs: backward_kernel(heads, *refs),
        grid_spec=pltpu.PrefetchScalarGridSpec(
            num_scalar_prefetch=1,
            grid=(parts,),
            in_specs=[
                tall(width),
                pl.BlockSpec((edge_rows, width), edge_at),
                tall(LANES, width // LANES),
                tall(values),
                whole(taps.shape),
                whole(coefficients.shape),
                whole(gain.shape),
                tall(values),
                stacked(CHUNK, CHUNK),
                stacked(DV, DK),
                tall(values),
                tall(values),
                tall(heads * DK),
                tall(width),
                tall(width),
                stacked(CHUNK, CHUNK),
                stacked(CHUNK, CHUNK),
                tall(values),
            ],
            out_specs=[
                tall(total),
                whole((HALO, width)),
                whole((HALO, DV)),
                whole((HALO, LANES)),
            ],
            scratch_shapes=[
                pltpu.VMEM((HALO, width), wide),
                pltpu.VMEM((heads, DV, DK), wide),
            ],
        ),
        out_shape=[
            jax.ShapeDtypeStruct((length, total), narrow),
            jax.ShapeDtypeStruct((HALO, width), wide),
            jax.ShapeDtypeStruct((HALO, DV), wide),
            jax.ShapeDtypeStruct((HALO, LANES), wide),
        ],
        compiler_params=params(),
        cost_estimate=effort(length, heads, 100000),
        interpret=interpret,
    )(place, proj, proj, proj, gate, taps, coefficients, gain, *kept, grad_gated)


def unpack_kernel(source_ref, target_ref):
    rows = target_ref.shape[0]
    source = source_ref[...]
    stacked = jnp.concatenate(
        [source[:, at : at + LANES] for at in range(0, source.shape[1], LANES)], axis=0
    )
    for at in range(target_ref.shape[1] // LANES):
        target_ref[:, at * LANES : (at + 1) * LANES] = stacked[at * rows : (at + 1) * rows]


def unpack(array, start, shards, rows, model, interpret):
    own = array.shape[0] // shards
    columns = array.shape[1] - start
    return pl.pallas_call(
        unpack_kernel,
        grid=(shards,),
        in_specs=[pl.BlockSpec((own, columns), lambda i: (i, start // columns))],
        out_specs=pl.BlockSpec((rows, model), lambda i: (i, 0)),
        out_shape=shape_of(shards * rows, model),
        compiler_params=params(),
        interpret=interpret,
    )(array)


def assemble_kernel(shards, piece, padded, *refs):
    *pieces, gate_ref, up_ref, down_ref = refs
    units = shards * padded
    pieces = [item[...].astype(wide) for item in pieces]
    for at, target_ref in enumerate((gate_ref, up_ref)):
        target_ref[...] = jnp.concatenate(
            [
                item[:, at * units + block * padded : at * units + block * padded + piece]
                for block in range(shards)
                for item in pieces
            ],
            axis=1,
        )
    for at, item in enumerate(pieces):
        stacked = jnp.concatenate(
            [item[:, start : start + LANES] for start in range(2 * units, item.shape[1], LANES)],
            axis=0,
        )
        for block in range(down_ref.shape[1] // LANES):
            down_ref[
                at * piece : (at + 1) * piece, block * LANES : (block + 1) * LANES
            ] = stacked[block * padded : block * padded + piece]


def assemble(pieces, shards, piece, padded, model, interpret):
    own = pieces[0].shape[0]
    parts = len(pieces)
    full = (own, shards * parts * piece)
    return row_call(
        lambda *refs: assemble_kernel(shards, piece, padded, *refs),
        1,
        [fixed(item.shape) for item in pieces],
        [fixed(full), fixed(full), fixed((parts * piece, model))],
        [shape_of(*full, wide), shape_of(*full, wide), shape_of(parts * piece, model, wide)],
        1024,
        interpret,
    )(*pieces)


def to_lanes(array):
    groups, rows, columns = array.shape
    split = array.reshape(groups, rows, columns // LANES, LANES)
    return jnp.swapaxes(split, 1, 2).reshape(groups, -1, LANES)


def from_lanes(array, rows):
    groups = array.shape[0]
    split = array.reshape(groups, -1, rows, LANES)
    return jnp.swapaxes(split, 1, 2).reshape(groups, rows, -1)


def per_device(
    tokens,
    cotangent,
    norm_attn,
    w_qkv,
    w_ba,
    conv_w,
    a_log,
    dt_bias,
    w_outgate,
    head_gain,
    w_out,
    norm_ffn,
    w_gate,
    w_up,
    w_down,
    interpret=False,
):
    parts = lax.axis_size("seq")
    shards = lax.axis_size("dp")
    place = lax.axis_index("seq")
    head_count = a_log.shape[0]
    heads = head_count // parts
    width = heads * ROW
    values = heads * DV
    model = tokens.shape[2]
    own = norm_attn.shape[0]
    out_rows = w_out.shape[0]
    quarter = model // parts

    def mine(array, size, axis):
        return lax.dynamic_slice_in_dim(array, place * size, size, axis)

    tie = lax.optimization_barrier

    def flip(array, bit):
        return lax.ppermute(array, "seq", [(i, i ^ bit) for i in range(parts)])

    def over_dp(array):
        return lax.all_gather(array, "dp", axis=0, tiled=True)

    def sum_dp(array):
        return lax.psum_scatter(array, "dp", scatter_dimension=0, tiled=True)

    def gather_seq(array):
        across = flip(array, 2)
        return [array, flip(array, 1), across, flip(across, 1)]

    def scatter_seq(pieces, beside=None):
        own_piece, sibling, across, corner = pieces
        across = across.astype(wide) + flip(lower(corner), 1).astype(wide)
        across = flip(lower(across), 2)
        sibling = flip(lower(sibling), 1)
        if beside is not None:
            across, beside = tie((across, beside))
        total = own_piece.astype(wide) + sibling.astype(wide) + across.astype(wide)
        return (total, beside)

    def sum_bits(array, low, high):
        return sum(
            [
                lax.ppermute(array, "dp", [(i, i ^ (at << low)) for i in range(shards)])
                for at in range(1, 1 << (high - low))
            ],
            array,
        )

    def absolute(stack):
        return jnp.concatenate(
            [
                lax.dynamic_index_in_dim(stack, jnp.bitwise_xor(place, at), 0)
                for at in range(parts)
            ],
            axis=0,
        )

    def exchange(stack):
        pieces = [
            lax.dynamic_index_in_dim(stack, jnp.bitwise_xor(place, at), 0)
            for at in range(parts)
        ]
        return absolute(
            jnp.concatenate(
                [pieces[0]] + [flip(pieces[at], at) for at in range(1, parts)], axis=0
            )
        )

    ffn = w_gate.shape[1]
    piece = ffn // (shards * parts)
    ffn_own = -(-(piece * shards) // LANES) * LANES
    padded = ffn_own // shards

    def ffn_columns(array):
        split = array.reshape(own, shards, parts, piece)
        split = lax.dynamic_index_in_dim(split, place, 2, keepdims=False)
        split = jnp.pad(split, ((0, 0), (0, 0), (0, padded - piece)))
        return split.reshape(own, ffn_own)

    own_tokens = tokens[:, 0, :]
    own_cot = cotangent[:, 0, :]
    small_flat = jnp.concatenate([norm_attn, norm_ffn, conv_w.reshape(-1)])
    small_count = small_flat.shape[0]
    half_lanes = LANES // 2
    small_flat = jnp.pad(small_flat, (0, own * half_lanes - small_count))
    out_ratio = out_rows // own
    w_all = over_dp(
        jnp.concatenate(
            [
                mine(w_qkv, width, 1),
                mine(w_outgate, values, 1),
                jnp.swapaxes(
                    mine(w_out, quarter, 1).reshape(out_ratio, own, quarter), 0, 1
                ).reshape(own, -1),
                jnp.pad(mine(w_ba, 2 * heads, 1), ((0, 0), (0, half_lanes - 2 * heads))),
                small_flat.reshape(own, half_lanes),
            ],
            axis=1,
        )
    )
    token_pieces = gather_seq(own_tokens)
    rates_at = w_all.shape[1] - LANES
    small_all = w_all[:, -half_lanes:].reshape(shards, -1)[:, :small_count]
    first_gain = small_all[:, :own].reshape(-1).astype(wide)
    second_gain = small_all[:, own : 2 * own].reshape(-1).astype(wide)
    taps_all = jnp.swapaxes(small_all[:, 2 * own :].reshape(shards, CONV, -1), 0, 1)
    taps = mine(taps_all.reshape(CONV, -1), width, 1).astype(wide)
    taps = jnp.pad(taps, ((0, HALO - CONV), (0, 0)))
    both_part = jnp.concatenate([ffn_columns(w_gate), ffn_columns(w_up)], axis=1)
    down_part = jnp.pad(mine(w_down, piece, 0), ((0, padded - piece), (0, 0)))
    ffn_part = jnp.concatenate(
        [both_part, from_lanes(to_lanes(down_part[None]), own)[0]], axis=1
    )
    ffn_part, w_all, token_pieces, cot_pieces = tie(
        (ffn_part, w_all, token_pieces, gather_seq(own_cot))
    )
    ffn_all = over_dp(ffn_part)

    decay_part = mine(a_log, heads, 0)
    bias_part = mine(dt_bias, heads, 0)

    def odd_lanes(vector):
        spaced = jnp.stack([jnp.zeros_like(vector), vector], axis=1).reshape(-1)
        return jnp.pad(spaced, (0, LANES - 2 * heads))[None, :]

    coefficients = jnp.pad(
        jnp.concatenate([odd_lanes(bias_part), odd_lanes(-jnp.exp(decay_part))], axis=0),
        ((0, HALO - 2), (0, 0)),
    )
    gain = jnp.broadcast_to(head_gain.astype(wide)[None, :], (HALO, DV))
    place_row = place.astype(jnp.int32)[None]

    first_rows = jnp.broadcast_to(first_gain[None, :], (HALO, model))
    normed_one, proj = enter(token_pieces, w_all, width, rates_at, first_rows, interpret)
    proj, out_part = tie((proj, w_all[:, width + values : rates_at]))
    mixed, *kept = mixer_forward(
        heads, parts, place_row, proj, taps, coefficients, interpret
    )
    out_part = jnp.swapaxes(out_part.reshape(shards, own, out_ratio, quarter), 1, 2)
    w_out_own = jnp.swapaxes(
        exchange(out_part.reshape(parts, values, quarter)), 0, 1
    ).reshape(values, model)
    gated, out_gate, *mixed_pieces = gate_rows(
        heads, parts, mixed, normed_one, w_all, width, gain, w_out_own, interpret
    )
    rows = own_tokens.astype(wide)
    inverse_one = row_norm(rows, first_gain)[1]
    after_mix = rows + scatter_seq(mixed_pieces)[0]
    normed_two, inverse_two = row_norm(after_mix, second_gain)
    normed_two, ffn_all = tie((lower(normed_two), ffn_all))
    whole_tiles = padded % (2 * HALO) == 0 and piece % HALO == 0
    if whole_tiles:
        down_own = unpack(ffn_all, 2 * ffn_own, shards, padded, model, interpret)
    else:
        down_own = from_lanes(
            to_lanes(ffn_all[:, 2 * ffn_own :].reshape(shards, own, -1)), padded
        ).reshape(ffn_own, model)
    across = flip(normed_two, 2)
    beside = flip(normed_two, 1)
    half = parts // 2
    normed_near, cot_near, hidden_near, grad_near, *back_near = ffn_rows(
        [normed_two, beside], cot_pieces[:half], ffn_all, down_own, interpret
    )
    across, *back_near = tie((across, *back_near))
    normed_far, cot_far, hidden_far, grad_far, *back_far = ffn_rows(
        [across, flip(across, 1)], cot_pieces[half:], ffn_all, down_own, interpret
    )
    grad_both = over_rows(normed_near, grad_near) + over_rows(normed_far, grad_far)
    grad_down = over_rows(hidden_near, cot_near) + over_rows(hidden_far, cot_far)
    grad_down = from_lanes(
        to_lanes(lower(grad_down).reshape(shards, padded, model)), own
    ).reshape(model, -1)
    grad_ffn = jnp.concatenate([lower(grad_both), grad_down], axis=1)
    grad_normed_two, grad_ffn = scatter_seq(back_near + back_far, grad_ffn)
    grad_ffn = sum_dp(grad_ffn)
    back_two, unused = norm_back(after_mix, inverse_two, second_gain, grad_normed_two)
    grad_after = own_cot.astype(wide) + back_two
    grad_low = lower(grad_after)
    across = flip(grad_low, 2)
    beside = flip(grad_low, 1)
    down_near = lower(by_weight(hidden_near, down_own))
    down_far = lower(by_weight(hidden_far, down_own))
    across, down_near, down_far = tie((across, down_near, down_far))
    grad_gated, grad_out = branch_rows(
        [grad_low, beside, across, flip(across, 1)], gated, w_out_own, interpret
    )
    grad_out = exchange(grad_out)
    grad_out = jnp.swapaxes(grad_out.reshape(shards, out_ratio, own, quarter), 1, 2).reshape(
        model, -1
    )
    count = own_tokens.shape[0]
    result = after_mix + scatter_seq(
        [down_near[:count], down_near[count:], down_far[:count], down_far[count:]]
    )[0]
    grad_in, grad_taps, grad_gain, grad_small = mixer_backward(
        heads, parts, place_row, proj, out_gate, taps, coefficients, gain, [mixed, *kept],
        grad_gated, interpret
    )
    grad_w_in = jnp.concatenate([lower(over_rows(normed_one, grad_in)), grad_out], axis=1)
    grad_in, grad_w_in = tie((grad_in, grad_w_in))
    grad_w_in = sum_dp(grad_w_in)
    split = width + values
    one_far, one_near = (
        by_transpose(grad_in[span, :split], w_all[:, :split])
        + by_transpose(grad_in[span, split:], w_all[:, rates_at:])
        for span in (slice(2 * count, None), slice(0, 2 * count))
    )
    first_pieces = [
        one_near[:count],
        flip(lower(one_near[count:]), 1),
        flip(lower(one_far[:count]), 2),
        flip(lower(one_far[count:]), 3),
    ]

    taps_full = lax.dynamic_update_slice_in_dim(
        jnp.zeros((CONV, head_count * ROW), wide), grad_taps[:CONV], place * width, 1
    )

    def to_heads(lane_row):
        return lax.dynamic_update_slice_in_dim(
            jnp.zeros((head_count,), wide), lane_row[1 : 2 * heads : 2], place * heads, 0
        )

    packed = jnp.concatenate(
        [
            taps_full.reshape(-1, LANES),
            grad_gain[0].reshape(-1, LANES),
            jnp.pad(
                jnp.stack([to_heads(grad_small[1]), to_heads(grad_small[0])]),
                ((0, 0), (0, LANES - head_count)),
            ),
        ],
        axis=0,
    )
    packed = jnp.pad(packed, ((0, -packed.shape[0] % HALO), (0, 0)))
    packed = sum([flip(packed, at) for at in range(1, parts)], packed)
    bits = shards.bit_length() - 1
    packed = sum_bits(packed, bits // 2, bits)

    def in_order(near):
        low_bit = jnp.bitwise_and(place, 1) != 0
        high_bit = jnp.bitwise_and(place, 2) != 0
        return [
            jnp.where(
                high_bit,
                jnp.where(low_bit, near[at ^ 3], near[at ^ 2]),
                jnp.where(low_bit, near[at ^ 1], near[at]),
            )
            for at in range(parts)
        ]

    def side_by_side(pieces):
        return jnp.concatenate(pieces, axis=1).astype(wide)

    def ffn_full(pieces):
        split = jnp.stack(
            [item.reshape(own, shards, padded)[..., :piece] for item in pieces], axis=2
        )
        return split.reshape(own, -1).astype(wide)

    ffn_pieces = in_order(gather_seq(grad_ffn))
    if whole_tiles:
        ffn_grads = assemble(ffn_pieces, shards, piece, padded, model, interpret)
    else:
        ffn_grads = (
            ffn_full([item[:, :ffn_own] for item in ffn_pieces]),
            ffn_full([item[:, ffn_own : 2 * ffn_own] for item in ffn_pieces]),
            jnp.concatenate(
                [
                    from_lanes(to_lanes(item[None, :, 2 * ffn_own :]), padded)[0][:piece]
                    for item in ffn_pieces
                ],
                axis=0,
            ).astype(wide),
        )
    grad_w_in, packed, first_pieces, ffn_grads = tie(
        (grad_w_in, packed, first_pieces, ffn_grads)
    )
    grad_w_gate, grad_w_up, grad_w_down = ffn_grads
    in_pieces = in_order(gather_seq(grad_w_in))
    packed = sum_bits(packed, 0, bits // 2)
    back_one, unused = norm_back(
        rows,
        inverse_one,
        first_gain,
        sum([item.astype(wide) for item in first_pieces[1:]], first_pieces[0]),
    )
    grad_rows = lower(grad_after + back_one)[:, None, :]
    def along(weights, grads):
        return sum(
            jnp.sum(weight.astype(wide) * grad, axis=1)
            for weight, grad in zip(weights, grads)
        )

    grad_norm_ffn = along((w_gate, w_up), (grad_w_gate, grad_w_up)) / norm_ffn.astype(wide)
    taps_rows = CONV * head_count * ROW // LANES
    gain_rows = taps_rows + DV // LANES
    own_taps = conv_w.shape[1]
    taps_total = lax.dynamic_slice_in_dim(
        packed[:taps_rows].reshape(CONV, -1), lax.axis_index("dp") * own_taps, own_taps, 1
    )
    total = split + LANES
    grad_w_qkv = side_by_side([item[:, :width] for item in in_pieces])
    grad_w_ba = side_by_side([item[:, split : split + 2 * heads] for item in in_pieces])
    grad_w_outgate = side_by_side([item[:, width:split] for item in in_pieces])
    grad_w_out = side_by_side(
        [
            jnp.swapaxes(item[:, total:].reshape(own, out_ratio, quarter), 0, 1).reshape(
                out_rows, quarter
            )
            for item in in_pieces
        ]
    )
    grad_norm_attn = along(
        (w_qkv, w_ba, w_outgate), (grad_w_qkv, grad_w_ba, grad_w_outgate)
    ) / norm_attn.astype(wide)
    return (
        lower(result)[:, None, :],
        grad_rows,
        grad_norm_attn,
        grad_w_qkv,
        grad_w_ba,
        taps_total,
        packed[gain_rows, :head_count],
        packed[gain_rows + 1, :head_count],
        grad_w_outgate,
        packed[taps_rows:gain_rows].reshape(-1),
        grad_w_out,
        grad_norm_ffn,
        grad_w_gate,
        grad_w_up,
        grad_w_down,
    )


def solution(mesh):
    return jax.shard_map(
        per_device,
        mesh=mesh,
        in_specs=(
            P("seq", "dp", None),
            P("seq", "dp", None),
            P("dp"),
            P("dp", None),
            P("dp", None),
            P(None, "dp"),
            P(),
            P(),
            P("dp", None),
            P(),
            P("dp", None),
            P("dp"),
            P("dp", None),
            P("dp", None),
            P("dp", None),
        ),
        out_specs=(
            P("seq", "dp", None),
            P("seq", "dp", None),
            P("dp"),
            P("dp", None),
            P("dp", None),
            P(None, "dp"),
            P(),
            P(),
            P("dp", None),
            P(),
            P("dp", None),
            P("dp"),
            P("dp", None),
            P("dp", None),
            P("dp", None),
        ),
        check_vma=False,
    )
```

```python
import jax
import jax.numpy as jnp
from jax import lax
from jax.experimental import pallas as pl
from jax.experimental.pallas import tpu as pltpu
from jax.sharding import PartitionSpec as P

DK = 128
DV = 256
CONV = 4
ROW = 2 * DK + DV
LANES = 128
CHUNK = 256
HALO = 8

epsilon = 1e-06
narrow = jnp.bfloat16
wide = jnp.float32


def by_weight(left, right):
    return jnp.dot(left, right, preferred_element_type=wide)


def by_transpose(left, right):
    return lax.dot_general(
        left, right, (((1,), (1,)), ((), ())), preferred_element_type=wide
    )


def over_rows(left, right):
    return lax.dot_general(
        left, right, (((0,), (0,)), ((), ())), preferred_element_type=wide
    )


def row_norm(values, gain):
    inverse = lax.rsqrt(jnp.mean(values * values, axis=-1, keepdims=True) + epsilon)
    return (values * inverse * gain, inverse)


def norm_back(values, inverse, gain, grad_out):
    scaled = grad_out * gain
    grad_in = inverse * scaled - values * inverse * inverse * inverse * jnp.mean(
        scaled * values, axis=-1, keepdims=True
    )
    grad_gain = jnp.sum(grad_out * values * inverse, axis=tuple(range(values.ndim - 1)))
    return (grad_in, grad_gain)


def lower(array):
    return array.astype(narrow)


def row_sum(array):
    return jnp.sum(array, axis=1, keepdims=True)


def grid_indices():
    rows = lax.broadcasted_iota(jnp.int32, (CHUNK, CHUNK), 0)
    columns = lax.broadcasted_iota(jnp.int32, (CHUNK, CHUNK), 1)
    return rows, columns


def exact_dot(left, right):
    return jnp.dot(
        left, right, precision=lax.Precision.HIGHEST, preferred_element_type=wide
    )


def shifted_rows(rows, before):
    return jnp.concatenate([before, rows], axis=0)


def convolved(extended, taps, count):
    start = HALO - CONV + 1
    summed = extended[start : start + count] * taps[0:1]
    for offset in range(1, CONV):
        summed = summed + extended[start + offset : start + offset + count] * taps[
            offset : offset + 1
        ]
    return summed


def gates(rates, coefficients):
    strength = jax.nn.sigmoid(rates)
    shifted = rates + coefficients[0:1]
    decay = coefficients[1:2] * jax.nn.softplus(shifted)
    return strength, shifted, decay


def unit(values):
    return lax.rsqrt(row_sum(values * values) + epsilon)


def in_turn(parts):
    waiting = list(parts)
    while waiting:
        still = []
        for part in waiting:
            try:
                next(part)
                still.append(part)
            except StopIteration:
                pass
        waiting = still


def invert(lower_part, rows, columns, store):
    apart = jnp.bitwise_xor(rows, columns)
    inverse = jnp.where(rows == columns, 1.0, 0.0) - jnp.where(apart == 1, lower_part, 0.0)
    level = 1
    while (1 << level) < CHUNK:
        corner = lower(
            jnp.where(lax.shift_right_logical(apart, level) == 1, lower_part, 0.0)
        )
        held = lower(inverse)
        yield
        side = lower(by_weight(corner, held))
        yield
        inverse = inverse - by_weight(held, side)
        level += 1
    store.append(lower(inverse))


def forward_kernel(
    heads,
    place_ref,
    proj_ref,
    rates_ref,
    taps_ref,
    coef_ref,
    mixed_ref,
    inverse_ref,
    state_ref,
    corrected_ref,
    update_ref,
    weight_ref,
    active_ref,
    slope_ref,
    inner_ref,
    pair_ref,
    before,
    state,
):
    @pl.when(pl.program_id(0) == 0)
    def _():
        before[...] = jnp.zeros_like(before)
        state[...] = jnp.zeros_like(state)

    count = proj_ref.shape[0]
    rows, columns = grid_indices()
    raw = proj_ref[...].astype(wide)
    summed = convolved(shifted_rows(raw, before[...]), taps_ref[...], count)
    before[...] = raw[count - HALO :]
    sig = jax.nn.sigmoid(summed)
    active = summed * sig
    active_ref[...] = lower(active)
    slope_ref[...] = lower(sig * (1.0 + summed * (1.0 - sig)))
    strength_rows, unused, decay_rows = gates(rates_ref[...].astype(wide), coef_ref[...])
    through = jnp.where(rows >= columns, 1.0, 0.0)
    states = {(0, head): state[head] for head in range(heads)}
    blocks = count // CHUNK
    cumulative_rows = [
        exact_dot(through, decay_rows[block * CHUNK : (block + 1) * CHUNK])
        for block in range(blocks)
    ]
    turned_rows = [item.T for item in cumulative_rows]

    def one(block, head):
        base = head * ROW
        here = slice(block * CHUNK, (block + 1) * CHUNK)
        query = active[here, base : base + DK]
        key = active[here, base + DK : base + 2 * DK]
        value = active[here, base + 2 * DK : base + ROW]
        query = query * (unit(query) * DK ** (-0.5))
        key = key * unit(key)
        strength = strength_rows[here, 2 * head : 2 * head + 1]
        cumulative = cumulative_rows[block][:, 2 * head + 1 : 2 * head + 2]
        across = turned_rows[block][2 * head + 1 : 2 * head + 2]
        final = cumulative[CHUNK - 1 :]
        fade = jnp.where(
            rows >= columns, jnp.exp(jnp.minimum(cumulative - across, 0.0)), 0.0
        )
        grown = jnp.exp(cumulative)
        key_low = lower(key)
        query_low = lower(query)
        dots = by_transpose(key_low, key_low)
        yield
        pair = jnp.where(rows > columns, fade * dots, 0.0)
        pair_ref[block, head] = lower(pair)
        lower_part = strength * pair
        store = []
        yield from invert(lower_part, rows, columns, store)
        inverse = store[0]
        yield
        update = by_weight(inverse, lower(strength * value))
        weight = lower(by_weight(inverse, lower(strength * grown * key)))
        inner = lower(by_transpose(query_low, key_low) * fade)
        inner_ref[block, head] = inner
        faded = lower(key * jnp.exp(final - cumulative))
        inverse_ref[block, head] = inverse
        span = slice(head * DV, head * DV + DV)
        update_ref[here, span] = lower(update)
        weight_ref[here, head * DK : head * DK + DK] = weight
        yield
        while (block, head) not in states:
            yield
        held = states[block, head]
        held_low = lower(held)
        state_ref[block, head] = held_low
        corrected = lower(update - by_transpose(weight, held_low))
        yield
        states[block + 1, head] = held * jnp.exp(final) + over_rows(corrected, faded)
        corrected_ref[here, span] = corrected
        result = grown * by_transpose(query_low, held_low) + by_weight(inner, corrected)
        yield
        mixed_ref[here, span] = lower(result)

    in_turn(one(block, head) for block in range(blocks) for head in range(heads))
    for head in range(heads):
        state[head] = states[blocks, head]


def on_piece(pieces, body):
    for at, piece in enumerate(pieces):

        @pl.when(pl.program_id(0) == at)
        def _(at=at, piece=piece):
            body(at, piece)


def entry_kernel(count, *refs):
    weight_ref, rates_ref, gain_ref, normed_ref, proj_ref = refs[count:]
    width = weight_ref.shape[1]

    def body(at, piece):
        normed = lower(row_norm(piece[...].astype(wide), gain_ref[0:1])[0])
        normed_ref[...] = normed
        proj_ref[:, :width] = lower(by_weight(normed, weight_ref[...]))
        proj_ref[:, width:] = lower(by_weight(normed, rates_ref[...]))

    on_piece(refs[:count], body)


def gate_kernel(
    heads, earlier, mixed_ref, normed_ref, weight_ref, gain_ref, out_ref, *refs
):
    gated_ref, gate_ref, *partials = refs[earlier:]
    gate = by_weight(normed_ref[...], weight_ref[...])
    gate_ref[...] = gate
    gain = gain_ref[0:1]
    for head in range(heads):
        span = slice(head * DV, head * DV + DV)
        normed = row_norm(mixed_ref[:, span].astype(wide), gain)[0]
        here = gate[:, span]
        gated_ref[:, span] = lower(normed * (here * jax.nn.sigmoid(here)))
    partial = lower(by_weight(gated_ref[...], out_ref[...]))

    def body(at, piece):
        piece[...] = partial

    on_piece(partials, body)


def ffn_kernel(count, *refs):
    normed_pieces, cot_pieces = refs[:count], refs[count : 2 * count]
    both_ref, down_ref, normed_ref, cot_ref, hidden_ref, grad_ref = refs[
        2 * count : 2 * count + 6
    ]
    backs = refs[2 * count + 6 :]
    units = down_ref.shape[0]

    def body(at, piece):
        normed = piece[...]
        cot = cot_pieces[at][...]
        normed_ref[...] = normed
        cot_ref[...] = cot
        gate_pre = by_weight(normed, both_ref[:, :units])
        up_pre = by_weight(normed, both_ref[:, units:])
        sig = jax.nn.sigmoid(gate_pre)
        silu = gate_pre * sig
        hidden_ref[...] = lower(silu * up_pre)
        grad_hidden = by_transpose(cot, down_ref[...])
        grad_ref[:, :units] = lower(
            grad_hidden * up_pre * sig * (1.0 + gate_pre * (1.0 - sig))
        )
        grad_ref[:, units:] = lower(grad_hidden * silu)
        backs[at][...] = lower(by_transpose(grad_ref[...], both_ref[...]))

    on_piece(normed_pieces, body)


def branch_kernel(count, earlier, *refs):
    gated_ref, weight_ref = refs[count : count + 2]
    grad_ref, out_ref, *scratch = refs[count + 2 + earlier :]

    def body(at, piece):
        branch = piece[...]
        grad_ref[...] = by_transpose(branch, weight_ref[...])
        product = over_rows(gated_ref[...], branch)
        if not earlier:
            out_ref[...] = product if at == 0 else out_ref[...] + product
        elif at == 0:
            scratch[0][...] = refs[count + 2][...] + product
        else:
            scratch[0][...] += product

    on_piece(refs[:count], body)
    if earlier:
        quarter = out_ref.shape[2]

        @pl.when(pl.program_id(0) == count - 1)
        def _():
            for at in range(out_ref.shape[0]):
                out_ref[at] = lower(scratch[0][:, at * quarter : (at + 1) * quarter])


def backward_kernel(
    heads,
    place_ref,
    proj_ref,
    edge_ref,
    rates_ref,
    gate_ref,
    taps_ref,
    coef_ref,
    gain_ref,
    mixed_ref,
    inverse_ref,
    state_ref,
    corrected_ref,
    update_ref,
    weight_ref,
    active_ref,
    slope_ref,
    inner_ref,
    pair_ref,
    grad_ref,
    out_ref,
    taps_grad_ref,
    gain_grad_ref,
    small_grad_ref,
    after,
    state_grad,
):
    step = pl.program_id(0)

    @pl.when(step == 0)
    def _():
        after[...] = jnp.zeros_like(after)
        state_grad[...] = jnp.zeros_like(state_grad)
        taps_grad_ref[...] = jnp.zeros_like(taps_grad_ref)
        gain_grad_ref[...] = jnp.zeros_like(gain_grad_ref)
        small_grad_ref[...] = jnp.zeros_like(small_grad_ref)

    count = proj_ref.shape[0]
    blocks = count // CHUNK
    rows, columns = grid_indices()
    lanes = lax.broadcasted_iota(jnp.int32, (CHUNK, LANES), 1)
    raw = proj_ref[...].astype(wide)
    edge = edge_ref[edge_ref.shape[0] - HALO :].astype(wide)
    edge = jnp.where(step == pl.num_programs(0) - 1, 0.0, edge)
    taps = taps_ref[...]
    extended = shifted_rows(raw, edge)
    active = active_ref[...].astype(wide)
    coefficients = coef_ref[...]
    strength_rows, shifted_rates, decay_rows = gates(
        rates_ref[...].astype(wide), coefficients
    )
    through = jnp.where(rows >= columns, 1.0, 0.0)
    onward = jnp.where(columns >= rows, 1.0, 0.0)
    gain = gain_ref[0:1]
    proj_width = heads * ROW
    total = out_ref.shape[1]
    cumulative_rows = [
        exact_dot(through, decay_rows[block * CHUNK : (block + 1) * CHUNK])
        for block in range(blocks)
    ]
    turned_rows = [item.T for item in cumulative_rows]
    laters = {(blocks - 1, head): state_grad[head] for head in range(heads)}
    active_grads = {}
    column_grads = {}
    gain_grads = []

    def one(block, head):
        here = slice(block * CHUNK, (block + 1) * CHUNK)
        span = slice(head * DV, head * DV + DV)
        grad_gated = grad_ref[here, span].astype(wide)
        mixed = mixed_ref[here, span].astype(wide)
        normed, head_inverse = row_norm(mixed, gain)
        gate = gate_ref[here, span]
        sig_gate = jax.nn.sigmoid(gate)
        gate_start = proj_width + head * DV
        out_ref[here, gate_start : gate_start + DV] = lower(
            grad_gated * normed * sig_gate * (1.0 + gate * (1.0 - sig_gate))
        )
        normed_grad = grad_gated * (gate * sig_gate)
        scaled = normed_grad * gain
        grad_mixed = lower(
            head_inverse * scaled
            - mixed
            * (head_inverse * head_inverse * head_inverse)
            * jnp.mean(scaled * mixed, axis=-1, keepdims=True)
        )
        gain_grads.append(
            jnp.sum(normed_grad * mixed * head_inverse, axis=0, keepdims=True)
        )
        base = head * ROW
        query_raw = active[here, base : base + DK]
        key_raw = active[here, base + DK : base + 2 * DK]
        value = active[here, base + 2 * DK : base + ROW]
        query_unit = unit(query_raw)
        key_unit = unit(key_raw)
        query = query_raw * (query_unit * DK ** (-0.5))
        key = key_raw * key_unit
        strength = strength_rows[here, 2 * head : 2 * head + 1]
        cumulative = cumulative_rows[block][:, 2 * head + 1 : 2 * head + 2]
        across = turned_rows[block][2 * head + 1 : 2 * head + 2]
        final = cumulative[CHUNK - 1 :]
        fade = jnp.where(
            rows >= columns, jnp.exp(jnp.minimum(cumulative - across, 0.0)), 0.0
        )
        strict_fade = jnp.where(rows > columns, fade, 0.0)
        grown = jnp.exp(cumulative)
        remaining = jnp.exp(final - cumulative)
        kept = jnp.exp(final)
        key_low = lower(key)
        query_low = lower(query)
        yield
        held = state_ref[block, head]
        corrected = corrected_ref[here, span]
        weight = weight_ref[here, head * DK : head * DK + DK]
        faded = key * remaining
        faded_low = lower(faded)
        grown_query = query * grown
        yield
        inner = inner_ref[block, head]
        inner_side = over_rows(inner, grad_mixed)
        state_side = over_rows(grad_mixed, lower(grown_query))
        dot_raw = by_transpose(grad_mixed, corrected)
        dot_grad_low = lower(dot_raw * fade)
        grown_grad = by_weight(grad_mixed, held)
        yield
        while (block, head) not in laters:
            yield
        later = laters[block, head]
        later_low = lower(later)
        corrected_grad_low = lower(inner_side + by_transpose(faded_low, later_low))
        yield
        laters[block - 1, head] = (
            later * kept + state_side - over_rows(corrected_grad_low, weight)
        )
        faded_grad = by_weight(corrected, later_low)
        weight_grad = lower(-by_weight(corrected_grad_low, held))
        inverse = inverse_ref[block, head]
        yield
        value_side = over_rows(inverse, corrected_grad_low)
        key_side = over_rows(inverse, weight_grad)
        yield
        lower_raw = -(
            by_transpose(lower(value_side), update_ref[here, span])
            + by_transpose(lower(key_side), weight)
        )
        inner_query = by_weight(dot_grad_low, key_low)
        inner_key = over_rows(dot_grad_low, query_low)
        yield
        lower_grad_low = lower(lower_raw * strict_fade)
        first_key = by_weight(lower_grad_low, key_low)
        second_key = over_rows(lower_grad_low, lower(strength * key))
        pairs = lower_raw * pair_ref[block, head].astype(wide)
        both = pairs * strength + dot_raw * inner.astype(wide)
        faded_sum = row_sum(faded_grad * faded)
        key_sum = row_sum(key_side * key)
        yield
        query_grad = grown * grown_grad + inner_query
        key_grad = (
            (strength * grown) * key_side
            + strength * first_key
            + second_key
            + inner_key
            + remaining * faded_grad
        )
        head_strength_grad = row_sum(value_side * value) + grown * key_sum + row_sum(pairs)
        head_spread = (
            (strength * grown) * key_sum
            + row_sum(both)
            + row_sum(grown_grad * grown_query)
            - faded_sum
        )
        column_total = jnp.sum(both, axis=0, keepdims=True)
        late_total = row_sum(jnp.where(columns >= rows, column_total, 0.0))
        final_grad = kept * jnp.sum(held.astype(wide) * later, keepdims=True) + jnp.sum(
            faded_sum, axis=0, keepdims=True
        )
        column_grads[block, head] = (
            head_strength_grad,
            head_spread,
            final_grad - late_total,
        )
        active_grads[block, head] = (
            DK ** (-0.5)
            * query_unit
            * (
                query_grad
                - query_raw * (query_unit * query_unit) * row_sum(query_grad * query_raw)
            ),
            key_unit
            * (key_grad - key_raw * (key_unit * key_unit) * row_sum(key_grad * key_raw)),
            strength * value_side,
        )

    in_turn(
        one(block, head) for block in reversed(range(blocks)) for head in range(heads)
    )
    for head in range(heads):
        state_grad[head] = laters[-1, head]
    for block in range(blocks):
        here = slice(block * CHUNK, (block + 1) * CHUNK)
        strength_grad = jnp.zeros((CHUNK, LANES), wide)
        spread_grad = jnp.zeros((CHUNK, LANES), wide)
        extra_grad = jnp.zeros((CHUNK, LANES), wide)
        for head in range(heads):
            first, second, third = column_grads[block, head]
            strength_grad = jnp.where(lanes == 2 * head, first, strength_grad)
            spread_grad = jnp.where(lanes == 2 * head + 1, second, spread_grad)
            extra_grad = jnp.where(lanes == 2 * head + 1, third, extra_grad)
        decay_grad = exact_dot(onward, spread_grad) + extra_grad
        shift_grad = decay_grad * coefficients[1:2] * jax.nn.sigmoid(shifted_rates[here])
        strength_here = strength_rows[here]
        rates_grad = strength_grad * strength_here * (1.0 - strength_here) + shift_grad
        out_ref[here, total - LANES :] = lower(rates_grad)
        small_grad_ref[0:1] += jnp.sum(shift_grad, axis=0, keepdims=True)
        small_grad_ref[1:2] += jnp.sum(decay_grad * decay_rows[here], axis=0, keepdims=True)
    gain_grad_ref[0:1] += sum(gain_grads)
    joined = jnp.concatenate(
        [
            jnp.concatenate(
                [part for head in range(heads) for part in active_grads[block, head]], axis=1
            )
            for block in range(blocks)
        ],
        axis=0,
    )
    summed_grad = joined * slope_ref[...].astype(wide)
    following = jnp.concatenate([summed_grad, after[...]], axis=0)
    after[...] = summed_grad[:HALO]
    proj_grad = following[CONV - 1 : CONV - 1 + count] * taps[0:1]
    start = HALO - CONV + 1
    for offset in range(CONV):
        if offset:
            shift = CONV - 1 - offset
            proj_grad = proj_grad + following[shift : shift + count] * taps[offset : offset + 1]
        taps_grad_ref[offset : offset + 1] += jnp.sum(
            summed_grad * extended[start + offset : start + offset + count],
            axis=0,
            keepdims=True,
        )
    out_ref[:, :proj_width] = lower(proj_grad)


def params():
    return pltpu.CompilerParams(
        dimension_semantics=("arbitrary",), vmem_limit_bytes=52 * 1024 * 1024
    )


def effort(length, heads, each=10000000):
    return pl.CostEstimate(
        flops=length * heads * each,
        bytes_accessed=length * heads * 1024,
        transcendentals=length * heads,
    )


def mixer_forward(heads, parts, place, proj, taps, coefficients, interpret=False):
    length = proj.shape[0]
    count = length // parts
    blocks = count // CHUNK
    width = heads * ROW
    values = heads * DV

    def tall(columns, at=0):
        return pl.BlockSpec((count, columns), lambda i, me: (jnp.bitwise_xor(i, me[0]), at))

    def whole(array):
        return pl.BlockSpec(array.shape, lambda i, me: (0,) * array.ndim)

    def stacked(first, second):
        return pl.BlockSpec((blocks, heads, first, second), lambda i, me: (i, 0, 0, 0))

    chunks = parts * blocks
    return pl.pallas_call(
        lambda *refs: forward_kernel(heads, *refs),
        grid_spec=pltpu.PrefetchScalarGridSpec(
            num_scalar_prefetch=1,
            grid=(parts,),
            in_specs=[
                tall(width),
                tall(LANES, width // LANES),
                whole(taps),
                whole(coefficients),
            ],
            out_specs=[
                tall(values),
                stacked(CHUNK, CHUNK),
                stacked(DV, DK),
                tall(values),
                tall(values),
                tall(heads * DK),
                tall(width),
                tall(width),
                stacked(CHUNK, CHUNK),
                stacked(CHUNK, CHUNK),
            ],
            scratch_shapes=[
                pltpu.VMEM((HALO, width), wide),
                pltpu.VMEM((heads, DV, DK), wide),
            ],
        ),
        out_shape=[
            jax.ShapeDtypeStruct((length, values), narrow),
            jax.ShapeDtypeStruct((chunks, heads, CHUNK, CHUNK), narrow),
            jax.ShapeDtypeStruct((chunks, heads, DV, DK), narrow),
            jax.ShapeDtypeStruct((length, values), narrow),
            jax.ShapeDtypeStruct((length, values), narrow),
            jax.ShapeDtypeStruct((length, heads * DK), narrow),
            jax.ShapeDtypeStruct((length, width), narrow),
            jax.ShapeDtypeStruct((length, width), narrow),
            jax.ShapeDtypeStruct((chunks, heads, CHUNK, CHUNK), narrow),
            jax.ShapeDtypeStruct((chunks, heads, CHUNK, CHUNK), narrow),
        ],
        compiler_params=params(),
        cost_estimate=effort(length, heads, 100000),
        interpret=interpret,
    )(place, proj, proj, taps, coefficients)


def fixed(shape):
    return pl.BlockSpec(shape, lambda i: (0,) * len(shape))


def rows_of(rows, columns):
    return pl.BlockSpec((rows, columns), lambda i: (i, 0))


def shape_of(rows, columns, kind=narrow):
    return jax.ShapeDtypeStruct((rows, columns), kind)


def row_call(kernel, steps, in_specs, out_specs, out_shape, flops, interpret):
    return pl.pallas_call(
        kernel,
        grid=(steps,),
        in_specs=in_specs,
        out_specs=out_specs,
        out_shape=out_shape,
        compiler_params=params(),
        cost_estimate=pl.CostEstimate(
            flops=flops, bytes_accessed=flops // 1024, transcendentals=0
        ),
        interpret=interpret,
    )


def columns_at(rows, columns, start):
    return pl.BlockSpec((rows, columns), lambda i: (0, start // columns))


def enter(pieces, weights, width, rates_at, gain, interpret):
    steps = len(pieces)
    rows, model = pieces[0].shape
    total = width + LANES
    return row_call(
        lambda *refs: entry_kernel(steps, *refs),
        steps,
        [fixed(item.shape) for item in pieces]
        + [
            columns_at(model, width, 0),
            columns_at(model, LANES, rates_at),
            fixed(gain.shape),
        ],
        [rows_of(rows, model), rows_of(rows, total)],
        [shape_of(steps * rows, model), shape_of(steps * rows, total)],
        steps * rows * total,
        interpret,
    )(*pieces, weights, weights, gain)


def rows_from(rows, columns, first):
    return pl.BlockSpec((rows, columns), lambda i: (i + first, 0))


def gate_rows(
    heads, parts, first, steps, mixed, normed, weights, start, gain, w_out, earlier, interpret
):
    length, values = mixed.shape
    model = normed.shape[1]
    rows = length // parts
    return pl.pallas_call(
        lambda *refs: gate_kernel(heads, len(earlier), *refs),
        grid=(steps,),
        in_specs=[
            rows_from(rows, values, first),
            rows_from(rows, model, first),
            columns_at(model, values, start),
            fixed(gain.shape),
            fixed(w_out.shape),
        ]
        + [pl.BlockSpec(memory_space=pl.ANY)] * len(earlier),
        out_specs=[rows_from(rows, values, first)] * 2 + [fixed((rows, model))] * steps,
        out_shape=[shape_of(length, values), shape_of(length, values, wide)]
        + [shape_of(rows, model)] * steps,
        input_output_aliases={5 + at: at for at in range(len(earlier))},
        compiler_params=params(),
        cost_estimate=pl.CostEstimate(
            flops=length * values, bytes_accessed=length, transcendentals=0
        ),
        interpret=interpret,
    )(mixed, normed, weights, gain, w_out, *earlier)


def ffn_rows(normed_pieces, cot_pieces, both, down, interpret):
    steps = len(normed_pieces)
    rows, model = normed_pieces[0].shape
    units = down.shape[0]
    length = steps * rows
    return row_call(
        lambda *refs: ffn_kernel(steps, *refs),
        steps,
        [fixed(item.shape) for item in (*normed_pieces, *cot_pieces)]
        + [columns_at(model, 2 * units, 0), fixed(down.shape)],
        [
            rows_of(rows, model),
            rows_of(rows, model),
            rows_of(rows, units),
            rows_of(rows, 2 * units),
        ]
        + [fixed((rows, model))] * steps,
        [
            shape_of(length, model),
            shape_of(length, model),
            shape_of(length, units),
            shape_of(length, 2 * units),
        ]
        + [shape_of(rows, model)] * steps,
        10 * length * model * units,
        interpret,
    )(*normed_pieces, *cot_pieces, both, down)


def branch_rows(parts, first, pieces, gated, weight, earlier, interpret):
    steps = len(pieces)
    rows, model = pieces[0].shape
    values = weight.shape[0]
    split = (parts, values, model // parts)
    total = shape_of(values, model, wide)
    return pl.pallas_call(
        lambda *refs: branch_kernel(steps, len(earlier), *refs),
        grid=(steps,),
        in_specs=[fixed(item.shape) for item in pieces]
        + [rows_from(rows, values, first), fixed(weight.shape)]
        + ([fixed(total.shape), pl.BlockSpec(memory_space=pl.ANY)] if earlier else []),
        out_specs=[
            rows_from(rows, values, first),
            fixed(split) if earlier else fixed(total.shape),
        ],
        out_shape=[
            shape_of(parts * rows, values, wide),
            jax.ShapeDtypeStruct(split, narrow) if earlier else total,
        ],
        scratch_shapes=[pltpu.VMEM(total.shape, wide)] if earlier else [],
        input_output_aliases={steps + 3: 0} if earlier else {},
        compiler_params=params(),
        cost_estimate=pl.CostEstimate(
            flops=4 * steps * rows * model * values, bytes_accessed=rows * model,
            transcendentals=0,
        ),
        interpret=interpret,
    )(*pieces, gated, weight, *earlier)


def mixer_backward(
    heads, parts, place, proj, gate, taps, coefficients, gain, kept, grad_gated, interpret=False
):
    length = proj.shape[0]
    count = length // parts
    blocks = count // CHUNK
    width = heads * ROW
    values = heads * DV
    edge_rows = 2 * HALO
    ratio = count // edge_rows

    def tall(columns, at=0):
        return pl.BlockSpec(
            (count, columns), lambda i, me: (jnp.bitwise_xor(parts - 1 - i, me[0]), at)
        )

    def edge_at(i, me):
        previous = jnp.bitwise_xor(jnp.maximum(parts - 2 - i, 0), me[0])
        return (previous * ratio + ratio - 1, 0)

    def whole(shape):
        return pl.BlockSpec(shape, lambda i, me: (0,) * len(shape))

    def stacked(first, second):
        return pl.BlockSpec(
            (blocks, heads, first, second), lambda i, me: (parts - 1 - i, 0, 0, 0)
        )

    total = width + LANES + values
    return pl.pallas_call(
        lambda *refs: backward_kernel(heads, *refs),
        grid_spec=pltpu.PrefetchScalarGridSpec(
            num_scalar_prefetch=1,
            grid=(parts,),
            in_specs=[
                tall(width),
                pl.BlockSpec((edge_rows, width), edge_at),
                tall(LANES, width // LANES),
                tall(values),
                whole(taps.shape),
                whole(coefficients.shape),
                whole(gain.shape),
                tall(values),
                stacked(CHUNK, CHUNK),
                stacked(DV, DK),
                tall(values),
                tall(values),
                tall(heads * DK),
                tall(width),
                tall(width),
                stacked(CHUNK, CHUNK),
                stacked(CHUNK, CHUNK),
                tall(values),
            ],
            out_specs=[
                tall(total),
                whole((HALO, width)),
                whole((HALO, DV)),
                whole((HALO, LANES)),
            ],
            scratch_shapes=[
                pltpu.VMEM((HALO, width), wide),
                pltpu.VMEM((heads, DV, DK), wide),
            ],
        ),
        out_shape=[
            jax.ShapeDtypeStruct((length, total), narrow),
            jax.ShapeDtypeStruct((HALO, width), wide),
            jax.ShapeDtypeStruct((HALO, DV), wide),
            jax.ShapeDtypeStruct((HALO, LANES), wide),
        ],
        compiler_params=params(),
        cost_estimate=effort(length, heads, 100000),
        interpret=interpret,
    )(place, proj, proj, proj, gate, taps, coefficients, gain, *kept, grad_gated)


def unpack_kernel(source_ref, target_ref):
    rows = target_ref.shape[0]
    source = source_ref[...]
    stacked = jnp.concatenate(
        [source[:, at : at + LANES] for at in range(0, source.shape[1], LANES)], axis=0
    )
    for at in range(target_ref.shape[1] // LANES):
        target_ref[:, at * LANES : (at + 1) * LANES] = stacked[at * rows : (at + 1) * rows]


def unpack(array, start, shards, rows, model, interpret):
    own = array.shape[0] // shards
    columns = array.shape[1] - start
    return pl.pallas_call(
        unpack_kernel,
        grid=(shards,),
        in_specs=[pl.BlockSpec((own, columns), lambda i: (i, start // columns))],
        out_specs=pl.BlockSpec((rows, model), lambda i: (i, 0)),
        out_shape=shape_of(shards * rows, model),
        compiler_params=params(),
        interpret=interpret,
    )(array)


def assemble_kernel(shards, piece, padded, *refs):
    *pieces, gate_ref, up_ref, down_ref = refs
    units = shards * padded
    pieces = [item[...].astype(wide) for item in pieces]
    for at, target_ref in enumerate((gate_ref, up_ref)):
        target_ref[...] = jnp.concatenate(
            [
                item[:, at * units + block * padded : at * units + block * padded + piece]
                for block in range(shards)
                for item in pieces
            ],
            axis=1,
        )
    for at, item in enumerate(pieces):
        stacked = jnp.concatenate(
            [item[:, start : start + LANES] for start in range(2 * units, item.shape[1], LANES)],
            axis=0,
        )
        for block in range(down_ref.shape[1] // LANES):
            down_ref[
                at * piece : (at + 1) * piece, block * LANES : (block + 1) * LANES
            ] = stacked[block * padded : block * padded + piece]


def assemble(pieces, shards, piece, padded, model, interpret):
    own = pieces[0].shape[0]
    parts = len(pieces)
    full = (own, shards * parts * piece)
    return row_call(
        lambda *refs: assemble_kernel(shards, piece, padded, *refs),
        1,
        [fixed(item.shape) for item in pieces],
        [fixed(full), fixed(full), fixed((parts * piece, model))],
        [shape_of(*full, wide), shape_of(*full, wide), shape_of(parts * piece, model, wide)],
        1024,
        interpret,
    )(*pieces)


def finish_kernel(heads, gain_ref, weight_refs, pieces, grad_refs):
    qkv_ref, rates_ref, gate_ref, out_ref, norm_ref = grad_refs
    own = qkv_ref.shape[0]
    parts = len(pieces)
    width, values = qkv_ref.shape[1] // parts, gate_ref.shape[1] // parts
    split, total = width + values, width + values + LANES
    quarter = out_ref.shape[1] // parts
    norm = jnp.zeros((own, 1), wide)
    rates = []
    for at, piece in enumerate(pieces):
        item = piece[...].astype(wide)
        for target_ref, weight_ref, start, size in (
            (qkv_ref, weight_refs[0], 0, width),
            (gate_ref, weight_refs[2], width, values),
        ):
            span = slice(at * size, (at + 1) * size)
            grad = item[:, start : start + size]
            target_ref[:, span] = grad
            norm = norm + row_sum(grad * weight_ref[:, span].astype(wide))
        rates.append(item[:, split : split + 2 * heads])
        for row in range(out_ref.shape[0] // own):
            out_ref[row * own : (row + 1) * own, at * quarter : (at + 1) * quarter] = item[
                :, total + row * quarter : total + (row + 1) * quarter
            ]
    rates = jnp.concatenate(rates, axis=1)
    rates_ref[...] = rates
    norm = norm + row_sum(rates * weight_refs[1][...].astype(wide))
    norm_ref[...] = jnp.broadcast_to(norm / gain_ref[...], norm_ref.shape)


def finish(heads, gain, weights, pieces, out_shape, interpret):
    own = pieces[0].shape[0]
    shapes = [item.shape for item in weights] + [out_shape, (own, LANES)]
    return row_call(
        lambda *refs: finish_kernel(heads, refs[0], refs[1:4], refs[4:-5], refs[-5:]),
        1,
        [fixed(item.shape) for item in (gain, *weights, *pieces)],
        [fixed(item) for item in shapes],
        [shape_of(*item, wide) for item in shapes],
        1024,
        interpret,
    )(gain, *weights, *pieces)


def to_lanes(array):
    groups, rows, columns = array.shape
    split = array.reshape(groups, rows, columns // LANES, LANES)
    return jnp.swapaxes(split, 1, 2).reshape(groups, -1, LANES)


def from_lanes(array, rows):
    groups = array.shape[0]
    split = array.reshape(groups, -1, rows, LANES)
    return jnp.swapaxes(split, 1, 2).reshape(groups, rows, -1)


def per_device(
    tokens,
    cotangent,
    norm_attn,
    w_qkv,
    w_ba,
    conv_w,
    a_log,
    dt_bias,
    w_outgate,
    head_gain,
    w_out,
    norm_ffn,
    w_gate,
    w_up,
    w_down,
    interpret=False,
):
    parts = lax.axis_size("seq")
    shards = lax.axis_size("dp")
    place = lax.axis_index("seq")
    head_count = a_log.shape[0]
    heads = head_count // parts
    width = heads * ROW
    values = heads * DV
    model = tokens.shape[2]
    own = norm_attn.shape[0]
    out_rows = w_out.shape[0]
    quarter = model // parts

    def mine(array, size, axis):
        return lax.dynamic_slice_in_dim(array, place * size, size, axis)

    tie = lax.optimization_barrier

    def flip(array, bit):
        return lax.ppermute(array, "seq", [(i, i ^ bit) for i in range(parts)])

    def over_dp(array):
        return lax.all_gather(array, "dp", axis=0, tiled=True)

    def sum_dp(array):
        return lax.psum_scatter(array, "dp", scatter_dimension=0, tiled=True)

    def gather_seq(array):
        across = flip(array, 2)
        return [array, flip(array, 1), across, flip(across, 1)]

    def scatter_seq(pieces, beside=None):
        own_piece, sibling, across, corner = pieces
        across = across.astype(wide) + flip(lower(corner), 1).astype(wide)
        across = flip(lower(across), 2)
        sibling = flip(lower(sibling), 1)
        if beside is not None:
            across, beside = tie((across, beside))
        total = own_piece.astype(wide) + sibling.astype(wide) + across.astype(wide)
        return (total, beside)

    def sum_bits(array, low, high):
        return sum(
            [
                lax.ppermute(array, "dp", [(i, i ^ (at << low)) for i in range(shards)])
                for at in range(1, 1 << (high - low))
            ],
            array,
        )

    def absolute(stack):
        return jnp.concatenate(
            [
                lax.dynamic_index_in_dim(stack, jnp.bitwise_xor(place, at), 0)
                for at in range(parts)
            ],
            axis=0,
        )

    def exchange(stack):
        pieces = [
            lax.dynamic_index_in_dim(stack, jnp.bitwise_xor(place, at), 0)
            for at in range(parts)
        ]
        return absolute(
            jnp.concatenate(
                [pieces[0]] + [flip(pieces[at], at) for at in range(1, parts)], axis=0
            )
        )

    ffn = w_gate.shape[1]
    piece = ffn // (shards * parts)
    ffn_own = -(-(piece * shards) // LANES) * LANES
    padded = ffn_own // shards

    def ffn_columns(array):
        split = array.reshape(own, shards, parts, piece)
        split = lax.dynamic_index_in_dim(split, place, 2, keepdims=False)
        split = jnp.pad(split, ((0, 0), (0, 0), (0, padded - piece)))
        return split.reshape(own, ffn_own)

    own_tokens = tokens[:, 0, :]
    own_cot = cotangent[:, 0, :]
    small_flat = jnp.concatenate([norm_attn, norm_ffn, conv_w.reshape(-1)])
    small_count = small_flat.shape[0]
    half_lanes = LANES // 2
    small_flat = jnp.pad(small_flat, (0, own * half_lanes - small_count))
    out_ratio = out_rows // own
    w_all = over_dp(
        jnp.concatenate(
            [
                mine(w_qkv, width, 1),
                mine(w_outgate, values, 1),
                jnp.swapaxes(
                    mine(w_out, quarter, 1).reshape(out_ratio, own, quarter), 0, 1
                ).reshape(own, -1),
                jnp.pad(mine(w_ba, 2 * heads, 1), ((0, 0), (0, half_lanes - 2 * heads))),
                small_flat.reshape(own, half_lanes),
            ],
            axis=1,
        )
    )
    token_pieces = gather_seq(own_tokens)
    rates_at = w_all.shape[1] - LANES
    small_all = w_all[:, -half_lanes:].reshape(shards, -1)[:, :small_count]
    first_gain = small_all[:, :own].reshape(-1).astype(wide)
    second_gain = small_all[:, own : 2 * own].reshape(-1).astype(wide)
    taps_all = jnp.swapaxes(small_all[:, 2 * own :].reshape(shards, CONV, -1), 0, 1)
    taps = mine(taps_all.reshape(CONV, -1), width, 1).astype(wide)
    taps = jnp.pad(taps, ((0, HALO - CONV), (0, 0)))
    both_part = jnp.concatenate([ffn_columns(w_gate), ffn_columns(w_up)], axis=1)
    down_part = jnp.pad(mine(w_down, piece, 0), ((0, padded - piece), (0, 0)))
    ffn_part = jnp.concatenate(
        [both_part, from_lanes(to_lanes(down_part[None]), own)[0]], axis=1
    )
    ffn_part, w_all, token_pieces, cot_pieces = tie(
        (ffn_part, w_all, token_pieces, gather_seq(own_cot))
    )
    ffn_all = over_dp(ffn_part)

    decay_part = mine(a_log, heads, 0)
    bias_part = mine(dt_bias, heads, 0)

    def odd_lanes(vector):
        spaced = jnp.stack([jnp.zeros_like(vector), vector], axis=1).reshape(-1)
        return jnp.pad(spaced, (0, LANES - 2 * heads))[None, :]

    coefficients = jnp.pad(
        jnp.concatenate([odd_lanes(bias_part), odd_lanes(-jnp.exp(decay_part))], axis=0),
        ((0, HALO - 2), (0, 0)),
    )
    gain = jnp.broadcast_to(head_gain.astype(wide)[None, :], (HALO, DV))
    place_row = place.astype(jnp.int32)[None]

    first_rows = jnp.broadcast_to(first_gain[None, :], (HALO, model))
    normed_one, proj = enter(token_pieces, w_all, width, rates_at, first_rows, interpret)
    proj, out_part = tie((proj, w_all[:, width + values : rates_at]))
    mixed, *kept = mixer_forward(
        heads, parts, place_row, proj, taps, coefficients, interpret
    )
    out_part = jnp.swapaxes(out_part.reshape(shards, own, out_ratio, quarter), 1, 2)
    w_out_own = jnp.swapaxes(
        exchange(out_part.reshape(parts, values, quarter)), 0, 1
    ).reshape(values, model)
    half = parts // 2
    gate_args = (mixed, normed_one, w_all, width, gain, w_out_own)
    *both_halves, corner_across, corner = gate_rows(
        heads, parts, half, half, *gate_args, (), interpret
    )
    gated, out_gate, *mixed_near = gate_rows(
        heads, parts, 0, half, *gate_args, tuple(both_halves), interpret
    )
    mixed_pieces = [*mixed_near, corner_across, corner]
    rows = own_tokens.astype(wide)
    inverse_one = row_norm(rows, first_gain)[1]
    after_mix = rows + scatter_seq(mixed_pieces)[0]
    normed_two, inverse_two = row_norm(after_mix, second_gain)
    normed_two, ffn_all = tie((lower(normed_two), ffn_all))
    whole_tiles = padded % (2 * HALO) == 0 and piece % HALO == 0
    if whole_tiles:
        down_own = unpack(ffn_all, 2 * ffn_own, shards, padded, model, interpret)
    else:
        down_own = from_lanes(
            to_lanes(ffn_all[:, 2 * ffn_own :].reshape(shards, own, -1)), padded
        ).reshape(ffn_own, model)
    across = flip(normed_two, 2)
    beside = flip(normed_two, 1)
    normed_near, cot_near, hidden_near, grad_near, *back_near = ffn_rows(
        [normed_two, beside], cot_pieces[:half], ffn_all, down_own, interpret
    )
    across, *back_near = tie((across, *back_near))
    normed_far, cot_far, hidden_far, grad_far, *back_far = ffn_rows(
        [across, flip(across, 1)], cot_pieces[half:], ffn_all, down_own, interpret
    )
    grad_both = over_rows(normed_near, grad_near) + over_rows(normed_far, grad_far)
    grad_down = over_rows(hidden_near, cot_near) + over_rows(hidden_far, cot_far)
    grad_down = from_lanes(
        to_lanes(lower(grad_down).reshape(shards, padded, model)), own
    ).reshape(model, -1)
    grad_ffn = jnp.concatenate([lower(grad_both), grad_down], axis=1)
    grad_normed_two, grad_ffn = scatter_seq(back_near + back_far, grad_ffn)
    grad_ffn = sum_dp(grad_ffn)
    back_two, unused = norm_back(after_mix, inverse_two, second_gain, grad_normed_two)
    grad_after = own_cot.astype(wide) + back_two
    grad_low = lower(grad_after)
    across = flip(grad_low, 2)
    beside = flip(grad_low, 1)
    down_near = lower(by_weight(hidden_near, down_own))
    down_far = lower(by_weight(hidden_far, down_own))
    across, down_near, down_far = tie((across, down_near, down_far))
    grad_gated, out_total = branch_rows(
        parts, 0, [grad_low, beside], gated, w_out_own, (), interpret
    )
    across, out_total = tie((across, out_total))
    grad_gated, grad_out = branch_rows(
        parts,
        half,
        [across, flip(across, 1)],
        gated,
        w_out_own,
        (out_total, grad_gated),
        interpret,
    )
    grad_out = exchange(grad_out)
    grad_out = jnp.swapaxes(grad_out.reshape(shards, out_ratio, own, quarter), 1, 2).reshape(
        model, -1
    )
    count = own_tokens.shape[0]
    result = after_mix + scatter_seq(
        [down_near[:count], down_near[count:], down_far[:count], down_far[count:]]
    )[0]
    grad_in, grad_taps, grad_gain, grad_small = mixer_backward(
        heads, parts, place_row, proj, out_gate, taps, coefficients, gain, [mixed, *kept],
        grad_gated, interpret
    )
    grad_w_in = jnp.concatenate([lower(over_rows(normed_one, grad_in)), grad_out], axis=1)
    grad_in, grad_w_in = tie((grad_in, grad_w_in))
    grad_w_in = sum_dp(grad_w_in)
    split = width + values
    one_far, one_near = (
        by_transpose(grad_in[span, :split], w_all[:, :split])
        + by_transpose(grad_in[span, split:], w_all[:, rates_at:])
        for span in (slice(2 * count, None), slice(0, 2 * count))
    )
    first_pieces = [
        one_near[:count],
        flip(lower(one_near[count:]), 1),
        flip(lower(one_far[:count]), 2),
        flip(lower(one_far[count:]), 3),
    ]

    taps_full = lax.dynamic_update_slice_in_dim(
        jnp.zeros((CONV, head_count * ROW), wide), grad_taps[:CONV], place * width, 1
    )

    def to_heads(lane_row):
        return lax.dynamic_update_slice_in_dim(
            jnp.zeros((head_count,), wide), lane_row[1 : 2 * heads : 2], place * heads, 0
        )

    packed = jnp.concatenate(
        [
            taps_full.reshape(-1, LANES),
            grad_gain[0].reshape(-1, LANES),
            jnp.pad(
                jnp.stack([to_heads(grad_small[1]), to_heads(grad_small[0])]),
                ((0, 0), (0, LANES - head_count)),
            ),
        ],
        axis=0,
    )
    packed = jnp.pad(packed, ((0, -packed.shape[0] % HALO), (0, 0)))
    packed = sum([flip(packed, at) for at in range(1, parts)], packed)
    bits = shards.bit_length() - 1
    packed = sum_bits(packed, bits // 2, bits)

    def in_order(near):
        low_bit = jnp.bitwise_and(place, 1) != 0
        high_bit = jnp.bitwise_and(place, 2) != 0
        return [
            jnp.where(
                high_bit,
                jnp.where(low_bit, near[at ^ 3], near[at ^ 2]),
                jnp.where(low_bit, near[at ^ 1], near[at]),
            )
            for at in range(parts)
        ]

    def ffn_full(pieces):
        split = jnp.stack(
            [item.reshape(own, shards, padded)[..., :piece] for item in pieces], axis=2
        )
        return split.reshape(own, -1).astype(wide)

    ffn_pieces = in_order(gather_seq(grad_ffn))
    if whole_tiles:
        ffn_grads = assemble(ffn_pieces, shards, piece, padded, model, interpret)
    else:
        ffn_grads = (
            ffn_full([item[:, :ffn_own] for item in ffn_pieces]),
            ffn_full([item[:, ffn_own : 2 * ffn_own] for item in ffn_pieces]),
            jnp.concatenate(
                [
                    from_lanes(to_lanes(item[None, :, 2 * ffn_own :]), padded)[0][:piece]
                    for item in ffn_pieces
                ],
                axis=0,
            ).astype(wide),
        )
    grad_w_in, packed, first_pieces, ffn_grads = tie(
        (grad_w_in, packed, first_pieces, ffn_grads)
    )
    grad_w_gate, grad_w_up, grad_w_down = ffn_grads
    in_pieces = in_order(gather_seq(grad_w_in))
    packed = sum_bits(packed, 0, bits // 2)
    back_one, unused = norm_back(
        rows,
        inverse_one,
        first_gain,
        sum([item.astype(wide) for item in first_pieces[1:]], first_pieces[0]),
    )
    grad_rows = lower(grad_after + back_one)[:, None, :]
    def along(weights, grads):
        return sum(
            jnp.sum(weight.astype(wide) * grad, axis=1)
            for weight, grad in zip(weights, grads)
        )

    grad_norm_ffn = along((w_gate, w_up), (grad_w_gate, grad_w_up)) / norm_ffn.astype(wide)
    taps_rows = CONV * head_count * ROW // LANES
    gain_rows = taps_rows + DV // LANES
    own_taps = conv_w.shape[1]
    taps_total = lax.dynamic_slice_in_dim(
        packed[:taps_rows].reshape(CONV, -1), lax.axis_index("dp") * own_taps, own_taps, 1
    )
    grad_w_qkv, grad_w_ba, grad_w_outgate, grad_w_out, norm_lanes = finish(
        heads,
        norm_attn.astype(wide)[:, None],
        (w_qkv, w_ba, w_outgate),
        in_pieces,
        (out_rows, model),
        interpret,
    )
    grad_norm_attn = norm_lanes[:, 0]
    return (
        lower(result)[:, None, :],
        grad_rows,
        grad_norm_attn,
        grad_w_qkv,
        grad_w_ba,
        taps_total,
        packed[gain_rows, :head_count],
        packed[gain_rows + 1, :head_count],
        grad_w_outgate,
        packed[taps_rows:gain_rows].reshape(-1),
        grad_w_out,
        grad_norm_ffn,
        grad_w_gate,
        grad_w_up,
        grad_w_down,
    )


def solution(mesh):
    return jax.shard_map(
        per_device,
        mesh=mesh,
        in_specs=(
            P("seq", "dp", None),
            P("seq", "dp", None),
            P("dp"),
            P("dp", None),
            P("dp", None),
            P(None, "dp"),
            P(),
            P(),
            P("dp", None),
            P(),
            P("dp", None),
            P("dp"),
            P("dp", None),
            P("dp", None),
            P("dp", None),
        ),
        out_specs=(
            P("seq", "dp", None),
            P("seq", "dp", None),
            P("dp"),
            P("dp", None),
            P("dp", None),
            P(None, "dp"),
            P(),
            P(),
            P("dp", None),
            P(),
            P("dp", None),
            P("dp"),
            P("dp", None),
            P("dp", None),
            P("dp", None),
        ),
        check_vma=False,
    )
```

```python
import jax
import jax.numpy as jnp
from jax import lax
from jax.experimental import pallas as pl
from jax.experimental.pallas import tpu as pltpu
from jax.sharding import PartitionSpec as P

DK = 128
DV = 256
CONV = 4
ROW = 2 * DK + DV
LANES = 128
CHUNK = 256
HALO = 8

epsilon = 1e-06
narrow = jnp.bfloat16
wide = jnp.float32


def by_weight(left, right):
    return jnp.dot(left, right, preferred_element_type=wide)


def by_transpose(left, right):
    return lax.dot_general(
        left, right, (((1,), (1,)), ((), ())), preferred_element_type=wide
    )


def over_rows(left, right):
    return lax.dot_general(
        left, right, (((0,), (0,)), ((), ())), preferred_element_type=wide
    )


def row_norm(values, gain):
    inverse = lax.rsqrt(jnp.mean(values * values, axis=-1, keepdims=True) + epsilon)
    return (values * inverse * gain, inverse)


def norm_back(values, inverse, gain, grad_out):
    scaled = grad_out * gain
    grad_in = inverse * scaled - values * inverse * inverse * inverse * jnp.mean(
        scaled * values, axis=-1, keepdims=True
    )
    grad_gain = jnp.sum(grad_out * values * inverse, axis=tuple(range(values.ndim - 1)))
    return (grad_in, grad_gain)


def lower(array):
    return array.astype(narrow)


def row_sum(array):
    return jnp.sum(array, axis=1, keepdims=True)


def grid_indices():
    rows = lax.broadcasted_iota(jnp.int32, (CHUNK, CHUNK), 0)
    columns = lax.broadcasted_iota(jnp.int32, (CHUNK, CHUNK), 1)
    return rows, columns


def exact_dot(left, right):
    return jnp.dot(
        left, right, precision=lax.Precision.HIGHEST, preferred_element_type=wide
    )


def shifted_rows(rows, before):
    return jnp.concatenate([before, rows], axis=0)


def convolved(extended, taps, count):
    start = HALO - CONV + 1
    summed = extended[start : start + count] * taps[0:1]
    for offset in range(1, CONV):
        summed = summed + extended[start + offset : start + offset + count] * taps[
            offset : offset + 1
        ]
    return summed


def gates(rates, coefficients):
    strength = jax.nn.sigmoid(rates)
    shifted = rates + coefficients[0:1]
    decay = coefficients[1:2] * jax.nn.softplus(shifted)
    return strength, shifted, decay


def unit(values):
    return lax.rsqrt(row_sum(values * values) + epsilon)


def in_turn(parts):
    waiting = list(parts)
    while waiting:
        still = []
        for part in waiting:
            try:
                next(part)
                still.append(part)
            except StopIteration:
                pass
        waiting = still


def invert(lower_part, rows, columns, store):
    apart = jnp.bitwise_xor(rows, columns)
    inverse = jnp.where(rows == columns, 1.0, 0.0) - jnp.where(apart == 1, lower_part, 0.0)
    level = 1
    while (1 << level) < CHUNK:
        corner = lower(
            jnp.where(lax.shift_right_logical(apart, level) == 1, lower_part, 0.0)
        )
        held = lower(inverse)
        yield
        side = lower(by_weight(corner, held))
        yield
        inverse = inverse - by_weight(held, side)
        level += 1
    store.append(lower(inverse))


def forward_kernel(
    heads,
    place_ref,
    proj_ref,
    rates_ref,
    taps_ref,
    coef_ref,
    mixed_ref,
    inverse_ref,
    state_ref,
    corrected_ref,
    update_ref,
    weight_ref,
    active_ref,
    slope_ref,
    inner_ref,
    pair_ref,
    before,
    state,
):
    @pl.when(pl.program_id(0) == 0)
    def _():
        before[...] = jnp.zeros_like(before)
        state[...] = jnp.zeros_like(state)

    count = proj_ref.shape[0]
    rows, columns = grid_indices()
    raw = proj_ref[...].astype(wide)
    summed = convolved(shifted_rows(raw, before[...]), taps_ref[...], count)
    before[...] = raw[count - HALO :]
    sig = jax.nn.sigmoid(summed)
    active = summed * sig
    active_ref[...] = lower(active)
    slope_ref[...] = lower(sig * (1.0 + summed * (1.0 - sig)))
    strength_rows, unused, decay_rows = gates(rates_ref[...].astype(wide), coef_ref[...])
    through = jnp.where(rows >= columns, 1.0, 0.0)
    states = {(0, head): state[head] for head in range(heads)}
    blocks = count // CHUNK
    cumulative_rows = [
        exact_dot(through, decay_rows[block * CHUNK : (block + 1) * CHUNK])
        for block in range(blocks)
    ]
    turned_rows = [item.T for item in cumulative_rows]

    def one(block, head):
        base = head * ROW
        here = slice(block * CHUNK, (block + 1) * CHUNK)
        query = active[here, base : base + DK]
        key = active[here, base + DK : base + 2 * DK]
        value = active[here, base + 2 * DK : base + ROW]
        query = query * (unit(query) * DK ** (-0.5))
        key = key * unit(key)
        strength = strength_rows[here, 2 * head : 2 * head + 1]
        cumulative = cumulative_rows[block][:, 2 * head + 1 : 2 * head + 2]
        across = turned_rows[block][2 * head + 1 : 2 * head + 2]
        final = cumulative[CHUNK - 1 :]
        fade = jnp.where(
            rows >= columns, jnp.exp(jnp.minimum(cumulative - across, 0.0)), 0.0
        )
        grown = jnp.exp(cumulative)
        key_low = lower(key)
        query_low = lower(query)
        dots = by_transpose(key_low, key_low)
        yield
        pair = jnp.where(rows > columns, fade * dots, 0.0)
        pair_ref[block, head] = lower(pair)
        lower_part = strength * pair
        store = []
        yield from invert(lower_part, rows, columns, store)
        inverse = store[0]
        yield
        update = by_weight(inverse, lower(strength * value))
        weight = lower(by_weight(inverse, lower(strength * grown * key)))
        inner = lower(by_transpose(query_low, key_low) * fade)
        inner_ref[block, head] = inner
        faded = lower(key * jnp.exp(final - cumulative))
        inverse_ref[block, head] = inverse
        span = slice(head * DV, head * DV + DV)
        update_ref[here, span] = lower(update)
        weight_ref[here, head * DK : head * DK + DK] = weight
        yield
        while (block, head) not in states:
            yield
        held = states[block, head]
        held_low = lower(held)
        state_ref[block, head] = held_low
        corrected = lower(update - by_transpose(weight, held_low))
        yield
        states[block + 1, head] = held * jnp.exp(final) + over_rows(corrected, faded)
        corrected_ref[here, span] = corrected
        result = grown * by_transpose(query_low, held_low) + by_weight(inner, corrected)
        yield
        mixed_ref[here, span] = lower(result)

    in_turn(one(block, head) for block in range(blocks) for head in range(heads))
    for head in range(heads):
        state[head] = states[blocks, head]


def on_piece(pieces, body):
    for at, piece in enumerate(pieces):

        @pl.when(pl.program_id(0) == at)
        def _(at=at, piece=piece):
            body(at, piece)


def entry_kernel(count, *refs):
    weight_ref, rates_ref, gain_ref, normed_ref, proj_ref = refs[count:]
    width = weight_ref.shape[1]

    def body(at, piece):
        normed = lower(row_norm(piece[...].astype(wide), gain_ref[0:1])[0])
        normed_ref[...] = normed
        proj_ref[:, :width] = lower(by_weight(normed, weight_ref[...]))
        proj_ref[:, width:] = lower(by_weight(normed, rates_ref[...]))

    on_piece(refs[:count], body)


def gate_kernel(
    heads, earlier, mixed_ref, normed_ref, weight_ref, gain_ref, out_ref, *refs
):
    gated_ref, gate_ref, *partials = refs[earlier:]
    gate = by_weight(normed_ref[...], weight_ref[...])
    gate_ref[...] = gate
    gain = gain_ref[0:1]
    for head in range(heads):
        span = slice(head * DV, head * DV + DV)
        normed = row_norm(mixed_ref[:, span].astype(wide), gain)[0]
        here = gate[:, span]
        gated_ref[:, span] = lower(normed * (here * jax.nn.sigmoid(here)))
    partial = lower(by_weight(gated_ref[...], out_ref[...]))

    def body(at, piece):
        piece[...] = partial

    on_piece(partials, body)


def ffn_kernel(count, *refs):
    normed_pieces, cot_pieces = refs[:count], refs[count : 2 * count]
    both_ref, down_ref, normed_ref, cot_ref, hidden_ref, grad_ref = refs[
        2 * count : 2 * count + 6
    ]
    backs = refs[2 * count + 6 :]
    units = down_ref.shape[0]

    def body(at, piece):
        normed = piece[...]
        cot = cot_pieces[at][...]
        normed_ref[...] = normed
        cot_ref[...] = cot
        gate_pre = by_weight(normed, both_ref[:, :units])
        up_pre = by_weight(normed, both_ref[:, units:])
        sig = jax.nn.sigmoid(gate_pre)
        silu = gate_pre * sig
        hidden_ref[...] = lower(silu * up_pre)
        grad_hidden = by_transpose(cot, down_ref[...])
        grad_ref[:, :units] = lower(
            grad_hidden * up_pre * sig * (1.0 + gate_pre * (1.0 - sig))
        )
        grad_ref[:, units:] = lower(grad_hidden * silu)
        backs[at][...] = lower(by_transpose(grad_ref[...], both_ref[...]))

    on_piece(normed_pieces, body)


def branch_kernel(count, earlier, *refs):
    gated_ref, weight_ref = refs[count : count + 2]
    grad_ref, out_ref, *scratch = refs[count + 2 + earlier :]

    def body(at, piece):
        branch = piece[...]
        grad_ref[...] = by_transpose(branch, weight_ref[...])
        product = over_rows(gated_ref[...], branch)
        if not earlier:
            out_ref[...] = product if at == 0 else out_ref[...] + product
        elif at == 0:
            scratch[0][...] = refs[count + 2][...] + product
        else:
            scratch[0][...] += product

    on_piece(refs[:count], body)
    if earlier:
        quarter = out_ref.shape[2]

        @pl.when(pl.program_id(0) == count - 1)
        def _():
            for at in range(out_ref.shape[0]):
                out_ref[at] = lower(scratch[0][:, at * quarter : (at + 1) * quarter])


def backward_kernel(
    heads,
    place_ref,
    proj_ref,
    edge_ref,
    rates_ref,
    gate_ref,
    taps_ref,
    coef_ref,
    gain_ref,
    mixed_ref,
    inverse_ref,
    state_ref,
    corrected_ref,
    update_ref,
    weight_ref,
    active_ref,
    slope_ref,
    inner_ref,
    pair_ref,
    grad_ref,
    out_ref,
    taps_grad_ref,
    gain_grad_ref,
    small_grad_ref,
    after,
    state_grad,
):
    step = pl.program_id(0)

    @pl.when(step == 0)
    def _():
        after[...] = jnp.zeros_like(after)
        state_grad[...] = jnp.zeros_like(state_grad)
        taps_grad_ref[...] = jnp.zeros_like(taps_grad_ref)
        gain_grad_ref[...] = jnp.zeros_like(gain_grad_ref)
        small_grad_ref[...] = jnp.zeros_like(small_grad_ref)

    count = proj_ref.shape[0]
    blocks = count // CHUNK
    rows, columns = grid_indices()
    lanes = lax.broadcasted_iota(jnp.int32, (CHUNK, LANES), 1)
    raw = proj_ref[...].astype(wide)
    edge = edge_ref[edge_ref.shape[0] - HALO :].astype(wide)
    edge = jnp.where(step == pl.num_programs(0) - 1, 0.0, edge)
    taps = taps_ref[...]
    extended = shifted_rows(raw, edge)
    active = active_ref[...].astype(wide)
    coefficients = coef_ref[...]
    strength_rows, shifted_rates, decay_rows = gates(
        rates_ref[...].astype(wide), coefficients
    )
    through = jnp.where(rows >= columns, 1.0, 0.0)
    onward = jnp.where(columns >= rows, 1.0, 0.0)
    gain = gain_ref[0:1]
    proj_width = heads * ROW
    total = out_ref.shape[1]
    cumulative_rows = [
        exact_dot(through, decay_rows[block * CHUNK : (block + 1) * CHUNK])
        for block in range(blocks)
    ]
    turned_rows = [item.T for item in cumulative_rows]
    laters = {(blocks - 1, head): state_grad[head] for head in range(heads)}
    active_grads = {}
    column_grads = {}
    gain_grads = []

    def one(block, head):
        here = slice(block * CHUNK, (block + 1) * CHUNK)
        span = slice(head * DV, head * DV + DV)
        grad_gated = grad_ref[here, span].astype(wide)
        mixed = mixed_ref[here, span].astype(wide)
        normed, head_inverse = row_norm(mixed, gain)
        gate = gate_ref[here, span]
        sig_gate = jax.nn.sigmoid(gate)
        gate_start = proj_width + head * DV
        out_ref[here, gate_start : gate_start + DV] = lower(
            grad_gated * normed * sig_gate * (1.0 + gate * (1.0 - sig_gate))
        )
        normed_grad = grad_gated * (gate * sig_gate)
        scaled = normed_grad * gain
        grad_mixed = lower(
            head_inverse * scaled
            - mixed
            * (head_inverse * head_inverse * head_inverse)
            * jnp.mean(scaled * mixed, axis=-1, keepdims=True)
        )
        gain_grads.append(
            jnp.sum(normed_grad * mixed * head_inverse, axis=0, keepdims=True)
        )
        base = head * ROW
        query_raw = active[here, base : base + DK]
        key_raw = active[here, base + DK : base + 2 * DK]
        value = active[here, base + 2 * DK : base + ROW]
        query_unit = unit(query_raw)
        key_unit = unit(key_raw)
        query = query_raw * (query_unit * DK ** (-0.5))
        key = key_raw * key_unit
        strength = strength_rows[here, 2 * head : 2 * head + 1]
        cumulative = cumulative_rows[block][:, 2 * head + 1 : 2 * head + 2]
        across = turned_rows[block][2 * head + 1 : 2 * head + 2]
        final = cumulative[CHUNK - 1 :]
        fade = jnp.where(
            rows >= columns, jnp.exp(jnp.minimum(cumulative - across, 0.0)), 0.0
        )
        strict_fade = jnp.where(rows > columns, fade, 0.0)
        grown = jnp.exp(cumulative)
        remaining = jnp.exp(final - cumulative)
        kept = jnp.exp(final)
        key_low = lower(key)
        query_low = lower(query)
        yield
        held = state_ref[block, head]
        corrected = corrected_ref[here, span]
        weight = weight_ref[here, head * DK : head * DK + DK]
        faded = key * remaining
        faded_low = lower(faded)
        grown_query = query * grown
        yield
        inner = inner_ref[block, head]
        inner_side = over_rows(inner, grad_mixed)
        state_side = over_rows(grad_mixed, lower(grown_query))
        dot_raw = by_transpose(grad_mixed, corrected)
        dot_grad_low = lower(dot_raw * fade)
        grown_grad = by_weight(grad_mixed, held)
        yield
        while (block, head) not in laters:
            yield
        later = laters[block, head]
        later_low = lower(later)
        corrected_grad_low = lower(inner_side + by_transpose(faded_low, later_low))
        yield
        laters[block - 1, head] = (
            later * kept + state_side - over_rows(corrected_grad_low, weight)
        )
        faded_grad = by_weight(corrected, later_low)
        weight_grad = lower(-by_weight(corrected_grad_low, held))
        inverse = inverse_ref[block, head]
        yield
        value_side = over_rows(inverse, corrected_grad_low)
        key_side = over_rows(inverse, weight_grad)
        yield
        lower_raw = -(
            by_transpose(lower(value_side), update_ref[here, span])
            + by_transpose(lower(key_side), weight)
        )
        inner_query = by_weight(dot_grad_low, key_low)
        inner_key = over_rows(dot_grad_low, query_low)
        yield
        lower_grad_low = lower(lower_raw * strict_fade)
        first_key = by_weight(lower_grad_low, key_low)
        second_key = over_rows(lower_grad_low, lower(strength * key))
        pairs = lower_raw * pair_ref[block, head].astype(wide)
        both = pairs * strength + dot_raw * inner.astype(wide)
        faded_sum = row_sum(faded_grad * faded)
        key_sum = row_sum(key_side * key)
        yield
        query_grad = grown * grown_grad + inner_query
        key_grad = (
            (strength * grown) * key_side
            + strength * first_key
            + second_key
            + inner_key
            + remaining * faded_grad
        )
        head_strength_grad = row_sum(value_side * value) + grown * key_sum + row_sum(pairs)
        head_spread = (
            (strength * grown) * key_sum
            + row_sum(both)
            + row_sum(grown_grad * grown_query)
            - faded_sum
        )
        column_total = jnp.sum(both, axis=0, keepdims=True)
        late_total = row_sum(jnp.where(columns >= rows, column_total, 0.0))
        final_grad = kept * jnp.sum(held.astype(wide) * later, keepdims=True) + jnp.sum(
            faded_sum, axis=0, keepdims=True
        )
        column_grads[block, head] = (
            head_strength_grad,
            head_spread,
            final_grad - late_total,
        )
        active_grads[block, head] = (
            DK ** (-0.5)
            * query_unit
            * (
                query_grad
                - query_raw * (query_unit * query_unit) * row_sum(query_grad * query_raw)
            ),
            key_unit
            * (key_grad - key_raw * (key_unit * key_unit) * row_sum(key_grad * key_raw)),
            strength * value_side,
        )

    in_turn(
        one(block, head) for block in reversed(range(blocks)) for head in range(heads)
    )
    for head in range(heads):
        state_grad[head] = laters[-1, head]
    for block in range(blocks):
        here = slice(block * CHUNK, (block + 1) * CHUNK)
        strength_grad = jnp.zeros((CHUNK, LANES), wide)
        spread_grad = jnp.zeros((CHUNK, LANES), wide)
        extra_grad = jnp.zeros((CHUNK, LANES), wide)
        for head in range(heads):
            first, second, third = column_grads[block, head]
            strength_grad = jnp.where(lanes == 2 * head, first, strength_grad)
            spread_grad = jnp.where(lanes == 2 * head + 1, second, spread_grad)
            extra_grad = jnp.where(lanes == 2 * head + 1, third, extra_grad)
        decay_grad = exact_dot(onward, spread_grad) + extra_grad
        shift_grad = decay_grad * coefficients[1:2] * jax.nn.sigmoid(shifted_rates[here])
        strength_here = strength_rows[here]
        rates_grad = strength_grad * strength_here * (1.0 - strength_here) + shift_grad
        out_ref[here, total - LANES :] = lower(rates_grad)
        small_grad_ref[0:1] += jnp.sum(shift_grad, axis=0, keepdims=True)
        small_grad_ref[1:2] += jnp.sum(decay_grad * decay_rows[here], axis=0, keepdims=True)
    gain_grad_ref[0:1] += sum(gain_grads)
    joined = jnp.concatenate(
        [
            jnp.concatenate(
                [part for head in range(heads) for part in active_grads[block, head]], axis=1
            )
            for block in range(blocks)
        ],
        axis=0,
    )
    summed_grad = joined * slope_ref[...].astype(wide)
    following = jnp.concatenate([summed_grad, after[...]], axis=0)
    after[...] = summed_grad[:HALO]
    proj_grad = following[CONV - 1 : CONV - 1 + count] * taps[0:1]
    start = HALO - CONV + 1
    for offset in range(CONV):
        if offset:
            shift = CONV - 1 - offset
            proj_grad = proj_grad + following[shift : shift + count] * taps[offset : offset + 1]
        taps_grad_ref[offset : offset + 1] += jnp.sum(
            summed_grad * extended[start + offset : start + offset + count],
            axis=0,
            keepdims=True,
        )
    out_ref[:, :proj_width] = lower(proj_grad)


def params():
    return pltpu.CompilerParams(
        dimension_semantics=("arbitrary",), vmem_limit_bytes=52 * 1024 * 1024
    )


def effort(length, heads, each=10000000):
    return pl.CostEstimate(
        flops=length * heads * each,
        bytes_accessed=length * heads * 1024,
        transcendentals=length * heads,
    )


def mixer_forward(heads, parts, place, proj, taps, coefficients, interpret=False):
    length = proj.shape[0]
    count = length // parts
    blocks = count // CHUNK
    width = heads * ROW
    values = heads * DV

    def tall(columns, at=0):
        return pl.BlockSpec((count, columns), lambda i, me: (jnp.bitwise_xor(i, me[0]), at))

    def whole(array):
        return pl.BlockSpec(array.shape, lambda i, me: (0,) * array.ndim)

    def stacked(first, second):
        return pl.BlockSpec((blocks, heads, first, second), lambda i, me: (i, 0, 0, 0))

    chunks = parts * blocks
    return pl.pallas_call(
        lambda *refs: forward_kernel(heads, *refs),
        grid_spec=pltpu.PrefetchScalarGridSpec(
            num_scalar_prefetch=1,
            grid=(parts,),
            in_specs=[
                tall(width),
                tall(LANES, width // LANES),
                whole(taps),
                whole(coefficients),
            ],
            out_specs=[
                tall(values),
                stacked(CHUNK, CHUNK),
                stacked(DV, DK),
                tall(values),
                tall(values),
                tall(heads * DK),
                tall(width),
                tall(width),
                stacked(CHUNK, CHUNK),
                stacked(CHUNK, CHUNK),
            ],
            scratch_shapes=[
                pltpu.VMEM((HALO, width), wide),
                pltpu.VMEM((heads, DV, DK), wide),
            ],
        ),
        out_shape=[
            jax.ShapeDtypeStruct((length, values), narrow),
            jax.ShapeDtypeStruct((chunks, heads, CHUNK, CHUNK), narrow),
            jax.ShapeDtypeStruct((chunks, heads, DV, DK), narrow),
            jax.ShapeDtypeStruct((length, values), narrow),
            jax.ShapeDtypeStruct((length, values), narrow),
            jax.ShapeDtypeStruct((length, heads * DK), narrow),
            jax.ShapeDtypeStruct((length, width), narrow),
            jax.ShapeDtypeStruct((length, width), narrow),
            jax.ShapeDtypeStruct((chunks, heads, CHUNK, CHUNK), narrow),
            jax.ShapeDtypeStruct((chunks, heads, CHUNK, CHUNK), narrow),
        ],
        compiler_params=params(),
        cost_estimate=effort(length, heads, 100000),
        interpret=interpret,
    )(place, proj, proj, taps, coefficients)


def fixed(shape):
    return pl.BlockSpec(shape, lambda i: (0,) * len(shape))


def rows_of(rows, columns):
    return pl.BlockSpec((rows, columns), lambda i: (i, 0))


def shape_of(rows, columns, kind=narrow):
    return jax.ShapeDtypeStruct((rows, columns), kind)


def row_call(kernel, steps, in_specs, out_specs, out_shape, flops, interpret):
    return pl.pallas_call(
        kernel,
        grid=(steps,),
        in_specs=in_specs,
        out_specs=out_specs,
        out_shape=out_shape,
        compiler_params=params(),
        cost_estimate=pl.CostEstimate(
            flops=flops, bytes_accessed=flops // 1024, transcendentals=0
        ),
        interpret=interpret,
    )


def columns_at(rows, columns, start):
    return pl.BlockSpec((rows, columns), lambda i: (0, start // columns))


def enter(pieces, weights, width, rates_at, gain, interpret):
    steps = len(pieces)
    rows, model = pieces[0].shape
    total = width + LANES
    return row_call(
        lambda *refs: entry_kernel(steps, *refs),
        steps,
        [fixed(item.shape) for item in pieces]
        + [
            columns_at(model, width, 0),
            columns_at(model, LANES, rates_at),
            fixed(gain.shape),
        ],
        [rows_of(rows, model), rows_of(rows, total)],
        [shape_of(steps * rows, model), shape_of(steps * rows, total)],
        steps * rows * total,
        interpret,
    )(*pieces, weights, weights, gain)


def rows_from(rows, columns, first):
    return pl.BlockSpec((rows, columns), lambda i: (i + first, 0))


def gate_rows(
    heads, parts, first, steps, mixed, normed, weights, start, gain, w_out, earlier, interpret
):
    length, values = mixed.shape
    model = normed.shape[1]
    rows = length // parts
    return pl.pallas_call(
        lambda *refs: gate_kernel(heads, len(earlier), *refs),
        grid=(steps,),
        in_specs=[
            rows_from(rows, values, first),
            rows_from(rows, model, first),
            columns_at(model, values, start),
            fixed(gain.shape),
            fixed(w_out.shape),
        ]
        + [pl.BlockSpec(memory_space=pl.ANY)] * len(earlier),
        out_specs=[rows_from(rows, values, first)] * 2 + [fixed((rows, model))] * steps,
        out_shape=[shape_of(length, values), shape_of(length, values, wide)]
        + [shape_of(rows, model)] * steps,
        input_output_aliases={5 + at: at for at in range(len(earlier))},
        compiler_params=params(),
        cost_estimate=pl.CostEstimate(
            flops=length * values, bytes_accessed=length, transcendentals=0
        ),
        interpret=interpret,
    )(mixed, normed, weights, gain, w_out, *earlier)


def ffn_rows(normed_pieces, cot_pieces, both, down, interpret):
    steps = len(normed_pieces)
    rows, model = normed_pieces[0].shape
    units = down.shape[0]
    length = steps * rows
    return row_call(
        lambda *refs: ffn_kernel(steps, *refs),
        steps,
        [fixed(item.shape) for item in (*normed_pieces, *cot_pieces)]
        + [columns_at(model, 2 * units, 0), fixed(down.shape)],
        [
            rows_of(rows, model),
            rows_of(rows, model),
            rows_of(rows, units),
            rows_of(rows, 2 * units),
        ]
        + [fixed((rows, model))] * steps,
        [
            shape_of(length, model),
            shape_of(length, model),
            shape_of(length, units),
            shape_of(length, 2 * units),
        ]
        + [shape_of(rows, model)] * steps,
        10 * length * model * units,
        interpret,
    )(*normed_pieces, *cot_pieces, both, down)


def branch_rows(parts, first, pieces, gated, weight, earlier, interpret):
    steps = len(pieces)
    rows, model = pieces[0].shape
    values = weight.shape[0]
    split = (parts, values, model // parts)
    total = shape_of(values, model, wide)
    return pl.pallas_call(
        lambda *refs: branch_kernel(steps, len(earlier), *refs),
        grid=(steps,),
        in_specs=[fixed(item.shape) for item in pieces]
        + [rows_from(rows, values, first), fixed(weight.shape)]
        + ([fixed(total.shape), pl.BlockSpec(memory_space=pl.ANY)] if earlier else []),
        out_specs=[
            rows_from(rows, values, first),
            fixed(split) if earlier else fixed(total.shape),
        ],
        out_shape=[
            shape_of(parts * rows, values, wide),
            jax.ShapeDtypeStruct(split, narrow) if earlier else total,
        ],
        scratch_shapes=[pltpu.VMEM(total.shape, wide)] if earlier else [],
        input_output_aliases={steps + 3: 0} if earlier else {},
        compiler_params=params(),
        cost_estimate=pl.CostEstimate(
            flops=4 * steps * rows * model * values, bytes_accessed=rows * model,
            transcendentals=0,
        ),
        interpret=interpret,
    )(*pieces, gated, weight, *earlier)


def mixer_backward(
    heads, parts, place, proj, gate, taps, coefficients, gain, kept, grad_gated, interpret=False
):
    length = proj.shape[0]
    count = length // parts
    blocks = count // CHUNK
    width = heads * ROW
    values = heads * DV
    edge_rows = 2 * HALO
    ratio = count // edge_rows

    def tall(columns, at=0):
        return pl.BlockSpec(
            (count, columns), lambda i, me: (jnp.bitwise_xor(parts - 1 - i, me[0]), at)
        )

    def edge_at(i, me):
        previous = jnp.bitwise_xor(jnp.maximum(parts - 2 - i, 0), me[0])
        return (previous * ratio + ratio - 1, 0)

    def whole(shape):
        return pl.BlockSpec(shape, lambda i, me: (0,) * len(shape))

    def stacked(first, second):
        return pl.BlockSpec(
            (blocks, heads, first, second), lambda i, me: (parts - 1 - i, 0, 0, 0)
        )

    total = width + LANES + values
    return pl.pallas_call(
        lambda *refs: backward_kernel(heads, *refs),
        grid_spec=pltpu.PrefetchScalarGridSpec(
            num_scalar_prefetch=1,
            grid=(parts,),
            in_specs=[
                tall(width),
                pl.BlockSpec((edge_rows, width), edge_at),
                tall(LANES, width // LANES),
                tall(values),
                whole(taps.shape),
                whole(coefficients.shape),
                whole(gain.shape),
                tall(values),
                stacked(CHUNK, CHUNK),
                stacked(DV, DK),
                tall(values),
                tall(values),
                tall(heads * DK),
                tall(width),
                tall(width),
                stacked(CHUNK, CHUNK),
                stacked(CHUNK, CHUNK),
                tall(values),
            ],
            out_specs=[
                tall(total),
                whole((HALO, width)),
                whole((HALO, DV)),
                whole((HALO, LANES)),
            ],
            scratch_shapes=[
                pltpu.VMEM((HALO, width), wide),
                pltpu.VMEM((heads, DV, DK), wide),
            ],
        ),
        out_shape=[
            jax.ShapeDtypeStruct((length, total), narrow),
            jax.ShapeDtypeStruct((HALO, width), wide),
            jax.ShapeDtypeStruct((HALO, DV), wide),
            jax.ShapeDtypeStruct((HALO, LANES), wide),
        ],
        compiler_params=params(),
        cost_estimate=effort(length, heads, 100000),
        interpret=interpret,
    )(place, proj, proj, proj, gate, taps, coefficients, gain, *kept, grad_gated)


def unpack_kernel(source_ref, target_ref):
    rows = target_ref.shape[0]
    source = source_ref[...]
    stacked = jnp.concatenate(
        [source[:, at : at + LANES] for at in range(0, source.shape[1], LANES)], axis=0
    )
    for at in range(target_ref.shape[1] // LANES):
        target_ref[:, at * LANES : (at + 1) * LANES] = stacked[at * rows : (at + 1) * rows]


def unpack(array, start, shards, rows, model, interpret):
    own = array.shape[0] // shards
    columns = array.shape[1] - start
    return pl.pallas_call(
        unpack_kernel,
        grid=(shards,),
        in_specs=[pl.BlockSpec((own, columns), lambda i: (i, start // columns))],
        out_specs=pl.BlockSpec((rows, model), lambda i: (i, 0)),
        out_shape=shape_of(shards * rows, model),
        compiler_params=params(),
        interpret=interpret,
    )(array)


def assemble_kernel(shards, piece, padded, *refs):
    *pieces, gate_ref, up_ref, down_ref = refs
    units = shards * padded
    pieces = [item[...].astype(wide) for item in pieces]
    for at, target_ref in enumerate((gate_ref, up_ref)):
        target_ref[...] = jnp.concatenate(
            [
                item[:, at * units + block * padded : at * units + block * padded + piece]
                for block in range(shards)
                for item in pieces
            ],
            axis=1,
        )
    for at, item in enumerate(pieces):
        stacked = jnp.concatenate(
            [item[:, start : start + LANES] for start in range(2 * units, item.shape[1], LANES)],
            axis=0,
        )
        for block in range(down_ref.shape[1] // LANES):
            down_ref[
                at * piece : (at + 1) * piece, block * LANES : (block + 1) * LANES
            ] = stacked[block * padded : block * padded + piece]


def assemble(pieces, shards, piece, padded, model, interpret):
    own = pieces[0].shape[0]
    parts = len(pieces)
    full = (own, shards * parts * piece)
    return row_call(
        lambda *refs: assemble_kernel(shards, piece, padded, *refs),
        1,
        [fixed(item.shape) for item in pieces],
        [fixed(full), fixed(full), fixed((parts * piece, model))],
        [shape_of(*full, wide), shape_of(*full, wide), shape_of(parts * piece, model, wide)],
        1024,
        interpret,
    )(*pieces)


def finish_kernel(heads, gain_ref, weight_refs, pieces, grad_refs):
    qkv_ref, rates_ref, gate_ref, out_ref, norm_ref = grad_refs
    own = qkv_ref.shape[0]
    parts = len(pieces)
    width, values = qkv_ref.shape[1] // parts, gate_ref.shape[1] // parts
    split, total = width + values, width + values + LANES
    quarter = out_ref.shape[1] // parts
    norm = jnp.zeros((own, 1), wide)
    rates = []
    for at, piece in enumerate(pieces):
        item = piece[...].astype(wide)
        for target_ref, weight_ref, start, size in (
            (qkv_ref, weight_refs[0], 0, width),
            (gate_ref, weight_refs[2], width, values),
        ):
            span = slice(at * size, (at + 1) * size)
            grad = item[:, start : start + size]
            target_ref[:, span] = grad
            norm = norm + row_sum(grad * weight_ref[:, span].astype(wide))
        rates.append(item[:, split : split + 2 * heads])
        for row in range(out_ref.shape[0] // own):
            out_ref[row * own : (row + 1) * own, at * quarter : (at + 1) * quarter] = item[
                :, total + row * quarter : total + (row + 1) * quarter
            ]
    rates = jnp.concatenate(rates, axis=1)
    rates_ref[...] = rates
    norm = norm + row_sum(rates * weight_refs[1][...].astype(wide))
    norm_ref[...] = jnp.broadcast_to(norm / gain_ref[...], norm_ref.shape)


def finish(heads, gain, weights, pieces, out_shape, interpret):
    own = pieces[0].shape[0]
    shapes = [item.shape for item in weights] + [out_shape, (own, LANES)]
    return row_call(
        lambda *refs: finish_kernel(heads, refs[0], refs[1:4], refs[4:-5], refs[-5:]),
        1,
        [fixed(item.shape) for item in (gain, *weights, *pieces)],
        [fixed(item) for item in shapes],
        [shape_of(*item, wide) for item in shapes],
        1024,
        interpret,
    )(gain, *weights, *pieces)


def to_lanes(array):
    groups, rows, columns = array.shape
    split = array.reshape(groups, rows, columns // LANES, LANES)
    return jnp.swapaxes(split, 1, 2).reshape(groups, -1, LANES)


def from_lanes(array, rows):
    groups = array.shape[0]
    split = array.reshape(groups, -1, rows, LANES)
    return jnp.swapaxes(split, 1, 2).reshape(groups, rows, -1)


def per_device(
    tokens,
    cotangent,
    norm_attn,
    w_qkv,
    w_ba,
    conv_w,
    a_log,
    dt_bias,
    w_outgate,
    head_gain,
    w_out,
    norm_ffn,
    w_gate,
    w_up,
    w_down,
    interpret=False,
):
    parts = lax.axis_size("seq")
    shards = lax.axis_size("dp")
    place = lax.axis_index("seq")
    head_count = a_log.shape[0]
    heads = head_count // parts
    width = heads * ROW
    values = heads * DV
    model = tokens.shape[2]
    own = norm_attn.shape[0]
    out_rows = w_out.shape[0]
    quarter = model // parts

    def mine(array, size, axis):
        return lax.dynamic_slice_in_dim(array, place * size, size, axis)

    tie = lax.optimization_barrier

    def flip(array, bit):
        return lax.ppermute(array, "seq", [(i, i ^ bit) for i in range(parts)])

    def over_dp(array):
        return lax.all_gather(array, "dp", axis=0, tiled=True)

    def sum_dp(array):
        return lax.psum_scatter(array, "dp", scatter_dimension=0, tiled=True)

    def gather_seq(array):
        across = flip(array, 2)
        return [array, flip(array, 1), across, flip(across, 1)]

    def scatter_seq(pieces, beside=None):
        own_piece, sibling, across, corner = pieces
        across = across.astype(wide) + flip(lower(corner), 1).astype(wide)
        across = flip(lower(across), 2)
        sibling = flip(lower(sibling), 1)
        if beside is not None:
            across, beside = tie((across, beside))
        total = own_piece.astype(wide) + sibling.astype(wide) + across.astype(wide)
        return (total, beside)

    def sum_bits(array, low, high):
        return sum(
            [
                lax.ppermute(array, "dp", [(i, i ^ (at << low)) for i in range(shards)])
                for at in range(1, 1 << (high - low))
            ],
            array,
        )

    def absolute(stack):
        return jnp.concatenate(
            [
                lax.dynamic_index_in_dim(stack, jnp.bitwise_xor(place, at), 0)
                for at in range(parts)
            ],
            axis=0,
        )

    def exchange(stack):
        pieces = [
            lax.dynamic_index_in_dim(stack, jnp.bitwise_xor(place, at), 0)
            for at in range(parts)
        ]
        return absolute(
            jnp.concatenate(
                [pieces[0]] + [flip(pieces[at], at) for at in range(1, parts)], axis=0
            )
        )

    ffn = w_gate.shape[1]
    piece = ffn // (shards * parts)
    ffn_own = -(-(piece * shards) // LANES) * LANES
    padded = ffn_own // shards

    def ffn_columns(array):
        split = array.reshape(own, shards, parts, piece)
        split = lax.dynamic_index_in_dim(split, place, 2, keepdims=False)
        split = jnp.pad(split, ((0, 0), (0, 0), (0, padded - piece)))
        return split.reshape(own, ffn_own)

    own_tokens = tokens[:, 0, :]
    own_cot = cotangent[:, 0, :]
    small_flat = jnp.concatenate([norm_attn, norm_ffn, conv_w.reshape(-1)])
    small_count = small_flat.shape[0]
    half_lanes = LANES // 2
    small_flat = jnp.pad(small_flat, (0, own * half_lanes - small_count))
    out_ratio = out_rows // own
    w_all = over_dp(
        jnp.concatenate(
            [
                mine(w_qkv, width, 1),
                mine(w_outgate, values, 1),
                jnp.swapaxes(
                    mine(w_out, quarter, 1).reshape(out_ratio, own, quarter), 0, 1
                ).reshape(own, -1),
                jnp.pad(mine(w_ba, 2 * heads, 1), ((0, 0), (0, half_lanes - 2 * heads))),
                small_flat.reshape(own, half_lanes),
            ],
            axis=1,
        )
    )
    token_pieces = gather_seq(own_tokens)
    rates_at = w_all.shape[1] - LANES
    small_all = w_all[:, -half_lanes:].reshape(shards, -1)[:, :small_count]
    first_gain = small_all[:, :own].reshape(-1).astype(wide)
    second_gain = small_all[:, own : 2 * own].reshape(-1).astype(wide)
    taps_all = jnp.swapaxes(small_all[:, 2 * own :].reshape(shards, CONV, -1), 0, 1)
    taps = mine(taps_all.reshape(CONV, -1), width, 1).astype(wide)
    taps = jnp.pad(taps, ((0, HALO - CONV), (0, 0)))
    both_part = jnp.concatenate([ffn_columns(w_gate), ffn_columns(w_up)], axis=1)
    down_part = jnp.pad(mine(w_down, piece, 0), ((0, padded - piece), (0, 0)))
    ffn_part = jnp.concatenate(
        [both_part, from_lanes(to_lanes(down_part[None]), own)[0]], axis=1
    )
    ffn_part, w_all, token_pieces, cot_pieces = tie(
        (ffn_part, w_all, token_pieces, gather_seq(own_cot))
    )
    ffn_all = over_dp(ffn_part)

    decay_part = mine(a_log, heads, 0)
    bias_part = mine(dt_bias, heads, 0)

    def odd_lanes(vector):
        spaced = jnp.stack([jnp.zeros_like(vector), vector], axis=1).reshape(-1)
        return jnp.pad(spaced, (0, LANES - 2 * heads))[None, :]

    coefficients = jnp.pad(
        jnp.concatenate([odd_lanes(bias_part), odd_lanes(-jnp.exp(decay_part))], axis=0),
        ((0, HALO - 2), (0, 0)),
    )
    gain = jnp.broadcast_to(head_gain.astype(wide)[None, :], (HALO, DV))
    place_row = place.astype(jnp.int32)[None]

    first_rows = jnp.broadcast_to(first_gain[None, :], (HALO, model))
    normed_one, proj = enter(token_pieces, w_all, width, rates_at, first_rows, interpret)
    proj, out_part = tie((proj, w_all[:, width + values : rates_at]))
    mixed, *kept = mixer_forward(
        heads, parts, place_row, proj, taps, coefficients, interpret
    )
    out_part = jnp.swapaxes(out_part.reshape(shards, own, out_ratio, quarter), 1, 2)
    w_out_own = jnp.swapaxes(
        exchange(out_part.reshape(parts, values, quarter)), 0, 1
    ).reshape(values, model)
    half = parts // 2
    gate_args = (mixed, normed_one, w_all, width, gain, w_out_own)
    *both_halves, corner_across, corner = gate_rows(
        heads, parts, half, half, *gate_args, (), interpret
    )
    gated, out_gate, *mixed_near = gate_rows(
        heads, parts, 0, half, *gate_args, tuple(both_halves), interpret
    )
    mixed_pieces = [*mixed_near, corner_across, corner]
    rows = own_tokens.astype(wide)
    inverse_one = row_norm(rows, first_gain)[1]
    after_mix = rows + scatter_seq(mixed_pieces)[0]
    normed_two, inverse_two = row_norm(after_mix, second_gain)
    normed_two, ffn_all = tie((lower(normed_two), ffn_all))
    whole_tiles = padded % (2 * HALO) == 0 and piece % HALO == 0
    if whole_tiles:
        down_own = unpack(ffn_all, 2 * ffn_own, shards, padded, model, interpret)
    else:
        down_own = from_lanes(
            to_lanes(ffn_all[:, 2 * ffn_own :].reshape(shards, own, -1)), padded
        ).reshape(ffn_own, model)
    across = flip(normed_two, 2)
    beside = flip(normed_two, 1)
    normed_near, cot_near, hidden_near, grad_near, *back_near = ffn_rows(
        [normed_two, beside], cot_pieces[:half], ffn_all, down_own, interpret
    )
    across, *back_near = tie((across, *back_near))
    normed_far, cot_far, hidden_far, grad_far, *back_far = ffn_rows(
        [across, flip(across, 1)], cot_pieces[half:], ffn_all, down_own, interpret
    )
    grad_both = over_rows(normed_near, grad_near) + over_rows(normed_far, grad_far)
    grad_down = over_rows(hidden_near, cot_near) + over_rows(hidden_far, cot_far)
    grad_down = from_lanes(
        to_lanes(lower(grad_down).reshape(shards, padded, model)), own
    ).reshape(model, -1)
    grad_ffn = jnp.concatenate([lower(grad_both), grad_down], axis=1)
    grad_normed_two, grad_ffn = scatter_seq(back_near + back_far, grad_ffn)
    grad_ffn = sum_dp(grad_ffn)
    back_two, unused = norm_back(after_mix, inverse_two, second_gain, grad_normed_two)
    grad_after = own_cot.astype(wide) + back_two
    grad_low = lower(grad_after)
    across = flip(grad_low, 2)
    beside = flip(grad_low, 1)
    down_near = lower(by_weight(hidden_near, down_own))
    down_far = lower(by_weight(hidden_far, down_own))
    across, down_near, down_far = tie((across, down_near, down_far))
    grad_gated, out_total = branch_rows(
        parts, 0, [grad_low, beside], gated, w_out_own, (), interpret
    )
    across, out_total = tie((across, out_total))
    grad_gated, grad_out = branch_rows(
        parts,
        half,
        [across, flip(across, 1)],
        gated,
        w_out_own,
        (out_total, grad_gated),
        interpret,
    )
    grad_out = exchange(grad_out)
    grad_out = jnp.swapaxes(grad_out.reshape(shards, out_ratio, own, quarter), 1, 2).reshape(
        model, -1
    )
    count = own_tokens.shape[0]
    down_across = down_far[:count].astype(wide) + flip(down_far[count:], 1).astype(wide)
    down_across, grad_gated = tie((lower(down_across), grad_gated))
    down_across = flip(down_across, 2)
    down_beside = flip(down_near[count:], 1)
    grad_in, grad_taps, grad_gain, grad_small = mixer_backward(
        heads, parts, place_row, proj, out_gate, taps, coefficients, gain, [mixed, *kept],
        grad_gated, interpret
    )
    grad_taps, down_across, down_beside = tie((grad_taps, down_across, down_beside))
    result = (
        after_mix
        + down_near[:count].astype(wide)
        + down_beside.astype(wide)
        + down_across.astype(wide)
    )
    grad_w_in = jnp.concatenate([lower(over_rows(normed_one, grad_in)), grad_out], axis=1)
    grad_in, grad_w_in = tie((grad_in, grad_w_in))
    grad_w_in = sum_dp(grad_w_in)
    split = width + values
    w_cat = jnp.concatenate([w_all[:, :split], w_all[:, rates_at:]], axis=1)
    one_far = lower(by_transpose(grad_in[2 * count :], w_cat))
    one_near = lower(by_transpose(grad_in[: 2 * count], w_cat))
    first_pieces = [
        one_near[:count],
        flip(one_near[count:], 1),
        flip(one_far[:count], 2),
        flip(one_far[count:], 3),
    ]

    taps_full = lax.dynamic_update_slice_in_dim(
        jnp.zeros((CONV, head_count * ROW), wide), grad_taps[:CONV], place * width, 1
    )

    def to_heads(lane_row):
        return lax.dynamic_update_slice_in_dim(
            jnp.zeros((head_count,), wide), lane_row[1 : 2 * heads : 2], place * heads, 0
        )

    packed = jnp.concatenate(
        [
            taps_full.reshape(-1, LANES),
            grad_gain[0].reshape(-1, LANES),
            jnp.pad(
                jnp.stack([to_heads(grad_small[1]), to_heads(grad_small[0])]),
                ((0, 0), (0, LANES - head_count)),
            ),
        ],
        axis=0,
    )
    packed = jnp.pad(packed, ((0, -packed.shape[0] % HALO), (0, 0)))
    packed = sum([flip(packed, at) for at in range(1, parts)], packed)
    bits = shards.bit_length() - 1
    packed = sum_bits(packed, bits // 2, bits)

    def in_order(near):
        low_bit = jnp.bitwise_and(place, 1) != 0
        high_bit = jnp.bitwise_and(place, 2) != 0
        return [
            jnp.where(
                high_bit,
                jnp.where(low_bit, near[at ^ 3], near[at ^ 2]),
                jnp.where(low_bit, near[at ^ 1], near[at]),
            )
            for at in range(parts)
        ]

    def ffn_full(pieces):
        split = jnp.stack(
            [item.reshape(own, shards, padded)[..., :piece] for item in pieces], axis=2
        )
        return split.reshape(own, -1).astype(wide)

    ffn_pieces = in_order(gather_seq(grad_ffn))
    if whole_tiles:
        ffn_grads = assemble(ffn_pieces, shards, piece, padded, model, interpret)
    else:
        ffn_grads = (
            ffn_full([item[:, :ffn_own] for item in ffn_pieces]),
            ffn_full([item[:, ffn_own : 2 * ffn_own] for item in ffn_pieces]),
            jnp.concatenate(
                [
                    from_lanes(to_lanes(item[None, :, 2 * ffn_own :]), padded)[0][:piece]
                    for item in ffn_pieces
                ],
                axis=0,
            ).astype(wide),
        )
    grad_w_in, packed, first_pieces, ffn_grads = tie(
        (grad_w_in, packed, first_pieces, ffn_grads)
    )
    grad_w_gate, grad_w_up, grad_w_down = ffn_grads
    in_pieces = in_order(gather_seq(grad_w_in))
    packed = sum_bits(packed, 0, bits // 2)
    back_one, unused = norm_back(
        rows,
        inverse_one,
        first_gain,
        sum([item.astype(wide) for item in first_pieces]),
    )
    grad_rows = lower(grad_after + back_one)[:, None, :]
    def along(weights, grads):
        return sum(
            jnp.sum(weight.astype(wide) * grad, axis=1)
            for weight, grad in zip(weights, grads)
        )

    grad_norm_ffn = along((w_gate, w_up), (grad_w_gate, grad_w_up)) / norm_ffn.astype(wide)
    taps_rows = CONV * head_count * ROW // LANES
    gain_rows = taps_rows + DV // LANES
    own_taps = conv_w.shape[1]
    taps_total = lax.dynamic_slice_in_dim(
        packed[:taps_rows].reshape(CONV, -1), lax.axis_index("dp") * own_taps, own_taps, 1
    )
    grad_w_qkv, grad_w_ba, grad_w_outgate, grad_w_out, norm_lanes = finish(
        heads,
        norm_attn.astype(wide)[:, None],
        (w_qkv, w_ba, w_outgate),
        in_pieces,
        (out_rows, model),
        interpret,
    )
    grad_norm_attn = norm_lanes[:, 0]
    return (
        lower(result)[:, None, :],
        grad_rows,
        grad_norm_attn,
        grad_w_qkv,
        grad_w_ba,
        taps_total,
        packed[gain_rows, :head_count],
        packed[gain_rows + 1, :head_count],
        grad_w_outgate,
        packed[taps_rows:gain_rows].reshape(-1),
        grad_w_out,
        grad_norm_ffn,
        grad_w_gate,
        grad_w_up,
        grad_w_down,
    )


def solution(mesh):
    return jax.shard_map(
        per_device,
        mesh=mesh,
        in_specs=(
            P("seq", "dp", None),
            P("seq", "dp", None),
            P("dp"),
            P("dp", None),
            P("dp", None),
            P(None, "dp"),
            P(),
            P(),
            P("dp", None),
            P(),
            P("dp", None),
            P("dp"),
            P("dp", None),
            P("dp", None),
            P("dp", None),
        ),
        out_specs=(
            P("seq", "dp", None),
            P("seq", "dp", None),
            P("dp"),
            P("dp", None),
            P("dp", None),
            P(None, "dp"),
            P(),
            P(),
            P("dp", None),
            P(),
            P("dp", None),
            P("dp"),
            P("dp", None),
            P("dp", None),
            P("dp", None),
        ),
        check_vma=False,
    )
```
